32 devices in a mesh: dp: 8 (over z, x), tensor: 4 (over y, core).
Axes of the slice: x: 2, y: 2, z: 4, core: 2. Of those that a mesh axis runs over, the one named last changes fastest.
Arguments:
- tokens: bfloat16 [17344, 768], P(('dp', 'tensor')), may hold values from -16 to 16
- lengths: int32 [32, 6], P(('dp', 'tensor')), may hold values from 1 to 197, 542 in all within a row
- capacity: int32 [17344], P(('dp', 'tensor')), may hold values from 0 to 1, as said below
- norm1_gain: float32 [768], replicated, may hold values from 0.1 to 1.9
- router: float32 [768], replicated, may hold values from -0.21875 to 0.21875
- w_qkv: bfloat16 [768, 2304], replicated, may hold values from -0.21875 to 0.21875
- w_out: bfloat16 [768, 768], replicated, may hold values from -1.25 to 1.25
- norm2_gain: float32 [768], replicated, may hold values from 0.1 to 1.9
- w_up: bfloat16 [768, 3072], P(None, 'tensor'), may hold values from -0.21875 to 0.21875
- w_down: bfloat16 [3072, 768], P('tensor'), may hold values from -0.109375 to 0.109375
- cotangent: bfloat16 [17344, 768], P(('dp', 'tensor')), may hold values from -6 to 6
Outputs:
- mixed: bfloat16 [17344, 768], P(('dp', 'tensor'))
- grad_input: float32 [17344, 768], P(('dp', 'tensor'))
- grad_norm1_gain: float32 [768], replicated
- grad_router: float32 [768], replicated
- grad_qkv: float32 [768, 2304], P(('dp', 'tensor'))
- grad_out_proj: float32 [768, 768], P(('dp', 'tensor'))
- grad_norm2_gain: float32 [768], replicated
- grad_up: float32 [768, 3072], P(None, 'tensor')
- grad_down: float32 [3072, 768], P('tensor')
- norms: float32 [3], replicated
The draws below stay inside these ranges and needn't reach their ends.
Inputs may be any that keep to these rules, and one draw needn't show every extreme that they name: Each image's 6 crop lengths sum to 542, and its longest crop has 197 tokens. `capacity`: exactly 271 tokens of each image are 1.
All inputs are finite; a program needn't handle non-finite values.
Results may differ from the reference program's by a relative error of at most 0.013.
Values may be sent and summed in bfloat16 or wider, within the bound.
No kernel may reach another device: no remote copies, remote signals or barrier semaphores. Data moves between devices by JAX's collectives and lax.ppermute only.
A program may use at most 192 MiB of HBM per device.

```python
import math
import jax
import jax.numpy as jnp
import numpy as np
from jax import lax

HEADS = 12
HEAD_DIM = 64
D = 768
FF = 3072
CROPS = 6
ROWS_IMG = 542
CROP_MOST = 197
IMAGES = 32
TOKENS = 17344


def draw_tokens(key, part):
    key = jax.random.fold_in(key, 11)
    col_key, row_key = jax.random.split(key)
    columns = 10.0 ** jax.random.uniform(col_key, (D,), dtype=jnp.float32) / 4.6
    image_index = (jnp.arange(TOKENS) // ROWS_IMG).astype(jnp.float32)
    image_ramp = image_index / float(max(IMAGES - 1, 1))
    base_draw = jnp.clip(jax.random.normal(row_key, (TOKENS, D), dtype=jnp.float32), -4.0, 4.0)
    row_scale = jnp.sqrt(1.0 + 2.0 * image_ramp)
    return (base_draw * row_scale[:, None] * columns[None, :]).astype(jnp.bfloat16)


def draw_capacity(key, part):
    key = jax.random.fold_in(key, 23)
    scores = jax.random.randint(key, (IMAGES, ROWS_IMG), 0, 1 << 20) * ROWS_IMG + jnp.arange(ROWS_IMG)[None, :]
    sort_order = jnp.argsort(scores, axis=-1, stable=True)
    token_rank = jnp.argsort(sort_order, axis=-1, stable=True)
    return (token_rank < ROWS_IMG // 2).astype(jnp.int32).reshape(TOKENS)


def steps_of(own_key, dims, shards, low, high):
    gain, own = 1.0, jax.random.fold_in(own_key, 6)
    for axis_at, shards_of in shards:
        draws = jnp.exp(jax.random.uniform(jax.random.fold_in(own, axis_at), (shards_of,), jnp.float32, low / len(shards), high / len(shards)))
        gain = gain * jnp.repeat(draws, dims[axis_at] // shards_of).reshape([-1 if axis == axis_at else 1 for axis in range(len(dims))])
    return gain


def length_profile(number_of, total, most, skew):
    weights = [(1 << 20) // math.isqrt(standing ** skew) + 1 for standing in range(2, number_of + 1)]
    rest, counts = total - most - (number_of - 1), [1] * (number_of - 1)
    while rest > 0:
        free = [i for i in range(number_of - 1) if counts[i] < most]
        whole, remaining = sum([weights[i] for i in free]), rest
        for i in free:
            addition = min(most - counts[i], max(1, remaining * weights[i] // whole), rest)
            counts[i] = counts[i] + addition
            rest = rest - addition
    return np.array([most] + counts)


def uneven_parts(rng, amount, total, reach, skew):
    if amount == 2:
        one = jax.random.randint(rng, (), max(1, total - reach), min(reach, total - 1) + 1)
        return jnp.stack([one, total - one])
    sizes = jnp.asarray(length_profile(amount, total, reach, skew), jnp.int32)
    pairs = (amount - 1) // 2
    source_of, taker = sizes[1:1 + 2 * pairs:2], sizes[2:2 + 2 * pairs:2]
    slack = jnp.minimum(source_of - 1, reach - taker)
    shifted = jax.random.randint(jax.random.fold_in(rng, 1), (pairs,), 0, 1 << 20) % (slack + 1)
    sizes = sizes.at[1:1 + 2 * pairs:2].set(source_of - shifted).at[2:2 + 2 * pairs:2].set(taker + shifted)
    return sizes[jax.random.permutation(jax.random.fold_in(rng, 2), amount)]


def noise(stream_key, shape, width, reach, cuts=(), kind=jnp.bfloat16):
    array = jax.random.normal(stream_key, shape, jnp.float32) * width
    if len(cuts) > 0:
        array = steps_of(stream_key, shape, cuts, -0.22, 0.18) * array
    return jnp.clip(array, min=-reach, max=reach).astype(kind)


def setup_inputs(seed: int = 0) -> dict:
    keys = jax.random.split(jax.random.key(seed), 12)
    tokens = draw_tokens(jax.random.fold_in(keys[11], 71), 0)
    lengths = jax.vmap(lambda own: uneven_parts(own, CROPS, ROWS_IMG, CROP_MOST, 1))(jax.random.split(keys[1], IMAGES)).reshape((IMAGES, CROPS)).astype(jnp.int32)
    capacity = draw_capacity(jax.random.fold_in(keys[11], 71), 0)
    norm1_gain = jnp.clip(1.0 + 0.18 * jax.random.normal(keys[3], (D,), jnp.float32), 0.1, 1.9)
    router = noise(keys[4], (D,), D ** -0.5, 0.21875, (), jnp.float32)
    w_qkv = noise(keys[5], (D, 3 * D), D ** -0.5, 0.21875)
    w_out = noise(keys[6], (D, D), (D // 32) ** -0.5, 1.25)
    norm2_gain = jnp.clip(1.0 + 0.18 * jax.random.normal(keys[7], (D,), jnp.float32), 0.1, 1.9)
    w_up = noise(keys[8], (D, FF), D ** -0.5, 0.21875, ((1, 4),))
    w_down = noise(keys[9], (FF, D), FF ** -0.5, 0.109375, ((0, 4),))
    cotangent = noise(keys[10], (TOKENS, D), 1.0, 6.0, ((0, 32),))
    return dict(tokens=tokens, lengths=lengths, capacity=capacity, norm1_gain=norm1_gain, router=router, w_qkv=w_qkv, w_out=w_out, norm2_gain=norm2_gain, w_up=w_up, w_down=w_down, cotangent=cotangent)


EPSILON = 1e-06
NEGATIVE = -1000000000.0
HIGHEST = lax.Precision.HIGHEST

@jax.custom_vjp
def low(v):
    return lax.optimization_barrier(v.astype(jnp.bfloat16)).astype(jnp.float32)

@jax.custom_vjp
def low_back(v):
    return v

def low_keep(v):
    return (low(v), None)

def low_pass(kept, grad):
    return (grad,)

def back_keep(v):
    return (v, None)

def back_low(kept, grad):
    return (low(grad),)
low.defvjp(low_keep, low_pass)
low_back.defvjp(back_keep, back_low)

def layer_norm(inputs, gain_vec):
    center = inputs - lax.optimization_barrier(jnp.mean(inputs, axis=-1, keepdims=True))
    inverse = lax.rsqrt(lax.optimization_barrier(jnp.mean(center * center, axis=-1, keepdims=True)) + EPSILON)
    return center * inverse * gain_vec

def crop_ids(lengths, img_rows):
    crop_ends = jnp.cumsum(lengths, axis=-1)
    position = lax.broadcasted_iota(jnp.int32, (lengths.shape[0], img_rows, lengths.shape[1]), 1)
    return lax.optimization_barrier(jnp.sum((position >= crop_ends[:, None, :]).astype(jnp.int32), axis=-1))

def allowed_keys(crop_of, chosen):
    tok_count = crop_of.shape[0]
    same_crop = crop_of[:, None] == crop_of[None, :]
    itself = lax.broadcasted_iota(jnp.int32, (tok_count, tok_count), 0) == lax.broadcasted_iota(jnp.int32, (tok_count, tok_count), 1)
    return same_crop & ((chosen[None, :] == 1) | itself)

def layer_image(params, inputs, crop_of, chosen):
    gain_one, router_vec, qkv_mat, out_mat, gain_two, up_mat, down_mat = params
    tok_count = inputs.shape[0]
    normed1 = low(layer_norm(inputs, gain_one))
    router_gate = jax.nn.sigmoid(jnp.dot(normed1, router_vec, precision=HIGHEST))
    united_qkv = low(low_back(jnp.dot(normed1, qkv_mat, precision=HIGHEST)))
    queries = united_qkv[:, :D].reshape(tok_count, HEADS, HEAD_DIM)
    key_heads = united_qkv[:, D:2 * D].reshape(tok_count, HEADS, HEAD_DIM)
    values = united_qkv[:, 2 * D:].reshape(tok_count, HEADS, HEAD_DIM)
    score_scale = 1.0 / math.sqrt(HEAD_DIM)
    raw_scores = low_back(jnp.einsum('qhd,khd->hqk', queries, key_heads, precision=HIGHEST) * score_scale)
    allowed = allowed_keys(crop_of, chosen)
    attn_prob = low(jax.nn.softmax(jnp.where(allowed[None], raw_scores, NEGATIVE), axis=-1))
    mixed_heads = low(low_back(jnp.einsum('hqk,khd->qhd', attn_prob, values, precision=HIGHEST).reshape(tok_count, D)))
    attended = low_back(jnp.dot(mixed_heads, out_mat, precision=HIGHEST))
    selected = chosen.astype(jnp.float32)
    branch = selected[:, None] * router_gate[:, None] * attended
    resid = inputs + branch
    normed2 = low(layer_norm(resid, gain_two))
    pre_act = low_back(jnp.dot(normed2, up_mat, precision=HIGHEST))
    activation = low(jax.nn.gelu(pre_act, approximate=True))
    hidden_branch = jnp.dot(activation, down_mat, precision=HIGHEST)
    square_terms = jnp.stack([jnp.sum(resid * resid), jnp.sum(branch * branch), jnp.sum(hidden_branch * hidden_branch)])
    return (resid + hidden_branch, square_terms)

def reference(tokens, lengths, capacity, norm1_gain, router, w_qkv, w_out, norm2_gain, w_up, w_down, cotangent):
    params = (norm1_gain, router, w_qkv.astype(jnp.float32), w_out.astype(jnp.float32), norm2_gain, w_up.astype(jnp.float32), w_down.astype(jnp.float32))
    inputs_all = tokens.astype(jnp.float32).reshape(IMAGES, ROWS_IMG, D)
    crops_all = crop_ids(lengths, ROWS_IMG)
    chosen_all = capacity.reshape(IMAGES, ROWS_IMG)
    cot_all = cotangent.astype(jnp.float32).reshape(IMAGES, ROWS_IMG, D)
    zero_grads = jax.tree.map(jnp.zeros_like, params)

    def scan_step(carried, packed):
        grad_sums, square_sums = carried
        inputs, crop_of, chosen, cot_rows = packed
        layer_out, pullback, square_terms = jax.vjp(lambda p_all, r_all: layer_image(p_all, r_all, crop_of, chosen), params, inputs, has_aux=True)
        param_grads, row_grads = pullback(cot_rows)
        grad_sums = jax.tree.map(lambda left, right: left + right, grad_sums, param_grads)
        return ((grad_sums, square_sums + square_terms), (layer_out.astype(jnp.bfloat16), row_grads))
    (grad_sums, square_sums), (outputs, row_grads) = lax.scan(scan_step, (zero_grads, jnp.zeros((3,), jnp.float32)), (inputs_all, crops_all, chosen_all, cot_all))
    norms = jnp.sqrt(square_sums / (TOKENS * D))
    return (outputs.reshape(TOKENS, D), row_grads.reshape(TOKENS, D), grad_sums[0], grad_sums[1], grad_sums[2], grad_sums[3], grad_sums[4], grad_sums[5], grad_sums[6], norms)
```

```python
import math

import jax
import jax.numpy as jnp
from jax import lax
from jax.experimental import pallas as pl
from jax.experimental.pallas import tpu as pltpu
from jax.sharding import PartitionSpec as P

HEADS = 12
HEAD_DIM = 64
PAIR = 2 * HEAD_DIM
EPSILON = 1e-06
NEGATIVE = -1000000000.0
GELU_C = math.sqrt(2.0 / math.pi)
GELU_A = 0.044715
F32 = jnp.float32
BF16 = jnp.bfloat16
VMEM_LIMIT = 60 * 1024 * 1024
ALL = ("dp", "tensor")


def dot_nn(a, b):
    return lax.dot_general(a, b, (((1,), (0,)), ((), ())), preferred_element_type=F32)


def dot_nt(a, b):
    return lax.dot_general(a, b, (((1,), (1,)), ((), ())), preferred_element_type=F32)


def dot_tn(a, b):
    return lax.dot_general(a, b, (((0,), (0,)), ((), ())), preferred_element_type=F32)


def iota(shape, dim):
    return lax.broadcasted_iota(jnp.int32, shape, dim)


def norm_rows(rows, gain):
    center = rows - jnp.mean(rows, axis=-1, keepdims=True)
    inverse = lax.rsqrt(jnp.mean(center * center, axis=-1, keepdims=True) + EPSILON)
    unit = center * inverse
    return unit * gain, unit, inverse


def norm_back(grad_out, unit, inverse, gain):
    scaled = grad_out * gain
    mean_grad = jnp.mean(scaled, axis=-1, keepdims=True)
    mean_cross = jnp.mean(scaled * unit, axis=-1, keepdims=True)
    grad_in = inverse * (scaled - mean_grad - unit * mean_cross)
    return grad_in, jnp.sum(grad_out * unit, axis=0, keepdims=True)


def call(body, outs, name, flops=0, moved=0, scratch=(), n_in=None, smem=()):
    vmem = pl.BlockSpec(memory_space=pltpu.VMEM)
    scalar = pl.BlockSpec(memory_space=pltpu.SMEM)
    return pl.pallas_call(
        body,
        out_shape=tuple(jax.ShapeDtypeStruct(s, d) for s, d in outs),
        in_specs=[scalar if i in smem else vmem for i in range(n_in)],
        out_specs=tuple(vmem for _ in outs),
        scratch_shapes=list(scratch),
        compiler_params=pltpu.CompilerParams(vmem_limit_bytes=VMEM_LIMIT),
        cost_estimate=pl.CostEstimate(flops=flops, bytes_accessed=moved, transcendentals=0),
        name=name,
    )


def places(cap, rows, half, blk):
    k, j = iota((rows, rows), 0), iota((rows, rows), 1)
    cap_col = jnp.sum(jnp.where(k == j, cap, 0.0), axis=1, keepdims=True)
    rank_row = jnp.sum(jnp.where(k < j, cap_col, 0.0), axis=0, keepdims=True)
    rank_col = jnp.sum(jnp.where(j < k, cap, 0.0), axis=1, keepdims=True)
    at_row = iota((1, rows), 1).astype(F32)
    at_col = iota((rows, 1), 0).astype(F32)
    dest_row = jnp.where(cap > 0.5, rank_row, blk + at_row - rank_row)
    dest_col = jnp.where(cap_col > 0.5, rank_col, blk + at_col - rank_col)
    return dest_row.astype(jnp.int32), dest_col.astype(jnp.int32)


def pre_body(tok, cot, cap, lens, gain2, xc, xn, cc, cn, n2n, bias):
    rows = tok.shape[0]
    blk = xc.shape[0]
    dest_row, _ = places(cap[...].astype(F32), rows, rows // 2, blk)
    pick = (iota((2 * blk, rows), 0) == dest_row).astype(BF16)
    x = dot_nn(pick, tok[...])
    c = dot_nn(pick, cot[...])
    xc[...] = x[:blk].astype(BF16)
    xn[...] = x[blk:].astype(BF16)
    cc[...] = c[:blk].astype(BF16)
    cn[...] = c[blk:].astype(BF16)
    n2n[...] = norm_rows(x[blk:], gain2[...])[0].astype(BF16)
    position = iota((1, rows), 1)
    crop = jnp.ones((1, rows), F32)
    end = 0
    for s in range(lens.shape[1]):
        end = end + lens[0, s]
        crop = crop + (position >= end).astype(F32)
    crop_col = jnp.sum(jnp.where(iota((blk, rows), 0) == dest_row, crop, 0.0), axis=1, keepdims=True)
    crop_row = jnp.sum(
        jnp.where(iota((blk, blk), 0) == iota((blk, blk), 1), crop_col, 0.0), axis=0, keepdims=True
    )
    bias[...] = jnp.where(crop_col == crop_row, 0.0, NEGATIVE)


def half_mask(shape, e):
    return (iota(shape, 1) < HEAD_DIM) == (e == 0)


def fore_body(
    half,
    xc, bias, gain1, router, w_qkv, w_out, gain2,
    n1, qkv, probs, heads, attended, gate, n2c, stats,
):
    blk, width = xc.shape
    x = xc[...].astype(F32)
    low = norm_rows(x, gain1[...])[0].astype(BF16)
    n1[...] = low
    logit = jnp.sum(low.astype(F32) * router[...], axis=-1, keepdims=True)
    gated = jnp.where(iota((blk, 1), 0) < half, jax.nn.sigmoid(logit), 0.0)
    gate[...] = gated
    qkv[...] = dot_nn(low, w_qkv[...]).astype(BF16)
    scale = 1.0 / math.sqrt(HEAD_DIM)
    for pair in range(HEADS // 2):
        at = pair * PAIR
        q = qkv[:, at : at + PAIR]
        k = qkv[:, width + at : width + at + PAIR]
        v = qkv[:, 2 * width + at : 2 * width + at + PAIR]
        total = None
        for e in range(2):
            mask = half_mask((blk, PAIR), e)
            zero = jnp.zeros_like(q)
            scores = dot_nt(jnp.where(mask, q, zero), k) * scale + bias[...]
            exponent = jnp.exp(scores - jnp.max(scores, axis=-1, keepdims=True))
            prob = (exponent / jnp.sum(exponent, axis=-1, keepdims=True)).astype(BF16)
            probs[2 * pair + e] = prob
            part = dot_nn(prob, jnp.where(mask, v, zero))
            total = part if total is None else total + part
        heads[:, at : at + PAIR] = total.astype(BF16)
    att = dot_nn(heads[...], w_out[...])
    attended[...] = att
    branch = gated * att
    resid = x + branch
    n2c[...] = norm_rows(resid, gain2[...])[0].astype(BF16)
    stats[0:1, :] = jnp.sum(resid * resid, axis=0, keepdims=True)
    stats[1:2, :] = jnp.sum(branch * branch, axis=0, keepdims=True)


def mlp_body(sources, blk, *refs):
    n2s, cots = refs[:sources], refs[sources : 2 * sources]
    w_up, w_down = refs[2 * sources : 2 * sources + 2]
    outs = refs[2 * sources + 2 :]
    hidden, d_n2, g_up, g_down, n2, cot, act, dpre = outs
    for s in range(sources):
        n2[s * blk : (s + 1) * blk] = n2s[s][...]
        cot[s * blk : (s + 1) * blk] = cots[s][...]

    @pl.loop(0, sources)
    def _(s):
        rows = pl.ds(pl.multiple_of(s * blk, 16), blk)
        pre = dot_nn(n2[rows, :], w_up[...])
        d_act = dot_nt(cot[rows, :], w_down[...])
        square = pre * pre
        t = jnp.tanh(GELU_C * pre * (1.0 + GELU_A * square))
        half_up = 0.5 * (1.0 + t)
        slope = half_up + 0.5 * pre * (1.0 - t * t) * (GELU_C * (1.0 + 3.0 * GELU_A * square))
        a = (pre * half_up).astype(BF16)
        d = (d_act * slope).astype(BF16)
        act[rows, :] = a
        dpre[rows, :] = d
        hidden[rows, :] = dot_nn(a, w_down[...]).astype(BF16)
        d_n2[rows, :] = dot_nt(d, w_up[...]).astype(BF16)

    tile = 256

    @pl.loop(0, g_up.shape[1] // tile)
    def _(n):
        cols = pl.ds(pl.multiple_of(n * tile, tile), tile)
        g_up[:, cols] = dot_tn(n2[...], dpre[:, cols]).astype(BF16)
        g_down[cols, :] = dot_tn(act[:, cols], cot[...]).astype(BF16)


def back_body(
    half,
    d_n2, cc, xc, attended, gate, heads, qkv, probs, n1, w_qkv, w_out, gain1, gain2, router,
    grad_in, g_qkv, g_proj, gains, d_qkv,
):
    blk, width = xc.shape
    scale = 1.0 / math.sqrt(HEAD_DIM)
    x = xc[...].astype(F32)
    gated = gate[...]
    resid = x + gated * attended[...]
    _, unit2, inverse2 = norm_rows(resid, gain2[...])
    back2, g_gain2 = norm_back(d_n2[...].astype(F32), unit2, inverse2, gain2[...])
    d_resid = cc[...].astype(F32) + back2
    d_att = (d_resid * gated).astype(BF16)
    keep = (iota((blk, 1), 0) < half).astype(F32)
    d_gate = keep * jnp.sum(d_resid * attended[...], axis=-1, keepdims=True)
    d_logit = d_gate * gated * (1.0 - gated)
    g_proj[...] = dot_tn(heads[...], d_att).astype(BF16)
    d_heads = dot_nt(d_att, w_out[...]).astype(BF16)
    for pair in range(HEADS // 2):
        at = pair * PAIR
        q = qkv[:, at : at + PAIR]
        k = qkv[:, width + at : width + at + PAIR]
        v = qkv[:, 2 * width + at : 2 * width + at + PAIR]
        d_o = d_heads[:, at : at + PAIR]
        zero = jnp.zeros_like(q)
        d_q = d_k = d_v = 0.0
        for e in range(2):
            mask = half_mask((blk, PAIR), e)
            d_oe = jnp.where(mask, d_o, zero)
            prob = probs[2 * pair + e]
            prob_f = prob.astype(F32)
            d_prob = dot_nt(d_oe, v)
            d_score = (
                prob_f * (d_prob - jnp.sum(prob_f * d_prob, axis=-1, keepdims=True))
            ).astype(BF16)
            d_v = d_v + dot_tn(prob, d_oe)
            d_q = d_q + dot_nn(d_score, jnp.where(mask, k, zero))
            d_k = d_k + dot_tn(d_score, jnp.where(mask, q, zero))
        d_qkv[:, at : at + PAIR] = (d_q * scale).astype(BF16)
        d_qkv[:, width + at : width + at + PAIR] = (d_k * scale).astype(BF16)
        d_qkv[:, 2 * width + at : 2 * width + at + PAIR] = d_v.astype(BF16)
    low = n1[...]
    g_qkv[...] = dot_tn(low, d_qkv[...]).astype(BF16)
    d_n1 = dot_nt(d_qkv[...], w_qkv[...]) + d_logit * router[...]
    _, unit1, inverse1 = norm_rows(x, gain1[...])
    back1, g_gain1 = norm_back(d_n1, unit1, inverse1, gain1[...])
    grad_in[...] = d_resid + back1
    gains[0:1, :] = g_gain1
    gains[1:2, :] = jnp.sum(d_logit * low.astype(F32), axis=0, keepdims=True)
    gains[2:3, :] = g_gain2


def put_back(pick, rows):
    top = rows.astype(BF16)
    rest = (rows - top.astype(F32)).astype(BF16)
    return dot_nn(pick, top) + dot_nn(pick, rest)


def post_body(
    cap, hidden_c, hidden_n, d_n2n, xc, xn, cn, attended, gate, grad_in_c, gain2,
    mixed, grad_in, stats,
):
    rows = mixed.shape[0]
    blk = xc.shape[0]
    _, dest_col = places(cap[...].astype(F32), rows, rows // 2, blk)
    pick_c = (iota((rows, blk), 1) == dest_col).astype(BF16)
    pick_n = (iota((rows, blk), 1) + blk == dest_col).astype(BF16)
    h_c, h_n = hidden_c[...].astype(F32), hidden_n[...].astype(F32)
    x_n = xn[...].astype(F32)
    mix_c = (xc[...].astype(F32) + gate[...] * attended[...] + h_c).astype(BF16)
    mix_n = (x_n + h_n).astype(BF16)
    mixed[...] = (dot_nn(pick_c, mix_c) + dot_nn(pick_n, mix_n)).astype(BF16)
    _, unit, inverse = norm_rows(x_n, gain2[...])
    back, g_gain2 = norm_back(d_n2n[...].astype(F32), unit, inverse, gain2[...])
    d_resid = cn[...].astype(F32) + back
    grad_in[...] = put_back(pick_c, grad_in_c[...]) + put_back(pick_n, d_resid)
    stats[0:1, :] = g_gain2
    stats[1:2, :] = jnp.sum(x_n * x_n, axis=0, keepdims=True)
    stats[2:3, :] = jnp.sum(h_c * h_c, axis=0, keepdims=True) + jnp.sum(
        h_n * h_n, axis=0, keepdims=True
    )


CORES = 2


def tensor_shift(array, size, dy, dc):
    steps = [
        (y * CORES + c, ((y + dy) % (size // CORES)) * CORES + (c ^ dc))
        for y in range(size // CORES)
        for c in range(CORES)
    ]
    return lax.ppermute(array, "tensor", steps)


def gather_rows(array, size):
    held = [array] + [tensor_shift(array, size, dy, 0) for dy in range(1, size // CORES)]
    out = []
    for a in held:
        out += [a, tensor_shift(a, size, 0, 1)]
    return out


def scatter_rows(parts, size):
    total = None
    for dy in range(size // CORES):
        other = tensor_shift(parts[2 * dy + 1], size, 0, 1)
        joint = parts[2 * dy].astype(F32) + other.astype(F32)
        if dy:
            joint = tensor_shift(joint.astype(BF16), size, -dy, 0).astype(F32)
        total = joint if total is None else total + joint
    return total


def shards(
    tokens, lengths, capacity, norm1_gain, router, w_qkv, w_out, norm2_gain, w_up, w_down, cotangent
):
    rows, width = tokens.shape
    half = rows // 2
    blk = -(-half // 16) * 16
    hidden_units = w_up.shape[1]
    tsize = lax.axis_size("tensor")
    cap = capacity.reshape(1, rows)
    gain1, gain2, route = (a.reshape(1, width) for a in (norm1_gain, norm2_gain, router))
    small = (blk, width)

    xc, xn, cc, cn, n2n, bias = call(
        pre_body,
        [(small, BF16)] * 5 + [((blk, blk), F32)],
        "pre",
        flops=4 * 2 * blk * rows * width,
        moved=8 * rows * width,
        n_in=5,
        smem=(3,),
    )(tokens, cotangent, cap, lengths, gain2)

    cc_all = gather_rows(cc, tsize)
    cn_all = gather_rows(cn, tsize)
    n2n_all = gather_rows(n2n, tsize)

    n1, qkv, probs, heads, attended, gate, n2c, stats1 = call(
        lambda *refs: fore_body(half, *refs),
        [
            (small, BF16), ((blk, 3 * width), BF16), ((HEADS, blk, blk), BF16), (small, BF16),
            (small, F32), ((blk, 1), F32), (small, BF16), ((2, width), F32),
        ],
        "fore",
        flops=2 * blk * width * 4 * width + 4 * blk * blk * width * 4,
        moved=4 * width * width * 2 + 20 * blk * width,
        n_in=7,
    )(xc, bias, gain1, route, w_qkv, w_out, gain2)

    n2c_all = gather_rows(n2c, tsize)

    sources = 2 * tsize
    tall = (sources * blk, width)
    hidden_p, d_n2_p, g_up, g_down = call(
        lambda *refs: mlp_body(sources, blk, *refs),
        [(tall, BF16), (tall, BF16), ((width, hidden_units), BF16), ((hidden_units, width), BF16)],
        "mlp",
        flops=12 * sources * blk * width * hidden_units,
        moved=8 * sources * blk * width,
        scratch=[
            pltpu.VMEM(tall, BF16), pltpu.VMEM(tall, BF16),
            pltpu.VMEM((sources * blk, hidden_units), BF16), pltpu.VMEM((sources * blk, hidden_units), BF16),
        ],
        n_in=2 * sources + 2,
    )(*n2c_all, *n2n_all, *cc_all, *cn_all, w_up, w_down)

    def cut(array, s):
        return array[s * blk : (s + 1) * blk]

    d_n2c = scatter_rows([cut(d_n2_p, s) for s in range(tsize)], tsize)
    d_n2n = scatter_rows([cut(d_n2_p, tsize + s) for s in range(tsize)], tsize)
    hidden_c = scatter_rows([cut(hidden_p, s) for s in range(tsize)], tsize)
    hidden_n = scatter_rows([cut(hidden_p, tsize + s) for s in range(tsize)], tsize)

    g_up, g_down = lax.psum((g_up, g_down), "dp")

    grad_in_c, g_qkv, g_proj, gains = call(
        lambda *refs: back_body(half, *refs),
        [(small, F32), ((width, 3 * width), BF16), ((width, width), BF16), ((3, width), F32)],
        "back",
        flops=4 * blk * width * 4 * width + 8 * blk * blk * width * 4,
        moved=8 * width * width * 2 + 20 * blk * width,
        scratch=[pltpu.VMEM((blk, 3 * width), BF16)],
        n_in=14,
    )(d_n2c, cc, xc, attended, gate, heads, qkv, probs, n1, w_qkv, w_out, gain1, gain2, route)

    qkv_share, proj_share = (
        lax.psum_scatter(g, ALL, scatter_dimension=0, tiled=True).astype(F32)
        for g in (g_qkv, g_proj)
    )

    mixed, grad_input, stats2 = call(
        post_body,
        [((rows, width), BF16), ((rows, width), F32), ((3, width), F32)],
        "post",
        flops=6 * 2 * rows * blk * width,
        moved=20 * rows * width,
        n_in=11,
    )(cap, hidden_c, hidden_n, d_n2n, xc, xn, cn, attended, gate, grad_in_c, gain2)

    sums = jnp.stack(
        [
            gains[0],
            gains[1],
            gains[2] + stats2[0],
            stats1[0] + stats2[1],
            stats1[1],
            stats2[2],
        ]
    )
    sums = lax.psum(sums, ALL)
    count = rows * width * lax.axis_size("dp") * lax.axis_size("tensor")
    norms = jnp.sqrt(jnp.sum(sums[3:], axis=-1) / count)
    return (
        mixed,
        grad_input,
        sums[0],
        sums[1],
        qkv_share,
        proj_share,
        sums[2],
        g_up.astype(F32),
        g_down.astype(F32),
        norms,
    )


def solution(mesh):
    return jax.shard_map(
        shards,
        mesh=mesh,
        in_specs=(
            P(("dp", "tensor"), None),
            P(("dp", "tensor"), None),
            P(("dp", "tensor")),
            P(),
            P(),
            P(),
            P(),
            P(),
            P(None, "tensor"),
            P("tensor", None),
            P(("dp", "tensor"), None),
        ),
        out_specs=(
            P(("dp", "tensor"), None),
            P(("dp", "tensor"), None),
            P(),
            P(),
            P(("dp", "tensor"), None),
            P(("dp", "tensor"), None),
            P(),
            P(None, "tensor"),
            P("tensor", None),
            P(),
        ),
        check_vma=False,
    )
```

```python
import math

import jax
import jax.numpy as jnp
from jax import lax
from jax.experimental import pallas as pl
from jax.experimental.pallas import tpu as pltpu
from jax.sharding import PartitionSpec as P

HEADS = 12
HEAD_DIM = 64
PAIR = 2 * HEAD_DIM
EPSILON = 1e-06
NEGATIVE = -1000000000.0
GELU_C = math.sqrt(2.0 / math.pi)
GELU_A = 0.044715
F32 = jnp.float32
BF16 = jnp.bfloat16
VMEM_LIMIT = 24


def dot_nn(a, b):
    return lax.dot_general(a, b, (((1,), (0,)), ((), ())), preferred_element_type=F32)


def dot_nt(a, b):
    return lax.dot_general(a, b, (((1,), (1,)), ((), ())), preferred_element_type=F32)


def dot_tn(a, b):
    return lax.dot_general(a, b, (((0,), (0,)), ((), ())), preferred_element_type=F32)


def iota(shape, dim):
    return lax.broadcasted_iota(jnp.int32, shape, dim)


def row_of(ref):
    return ref[...].reshape(1, ref.shape[0])


def norm_rows(rows, gain):
    center = rows - jnp.mean(rows, axis=-1, keepdims=True)
    inverse = lax.rsqrt(jnp.mean(center * center, axis=-1, keepdims=True) + EPSILON)
    unit = center * inverse
    return unit * gain, unit, inverse


def norm_back(grad_out, unit, inverse, gain):
    scaled = grad_out * gain
    mean_grad = jnp.mean(scaled, axis=-1, keepdims=True)
    mean_cross = jnp.mean(scaled * unit, axis=-1, keepdims=True)
    grad_in = inverse * (scaled - mean_grad - unit * mean_cross)
    return grad_in, jnp.sum(grad_out * unit, axis=0, keepdims=True)


def call(body, outs, name, scratch=(), loose=(), after=(), weight=1.0, limit=VMEM_LIMIT):
    vmem = pl.BlockSpec(memory_space=pltpu.VMEM)
    anywhere = pl.BlockSpec(memory_space=pl.ANY)

    def run(*args):
        count = len(args)
        cuts = [a[1:] if isinstance(a, tuple) else None for a in args]
        args = [a[0] if isinstance(a, tuple) else a for a in args]
        given = list({id(a): a for a in args}.values())
        index = [[id(g) for g in given].index(id(a)) for a in args]

        def inner(*refs):
            held = [refs[i] for i in index]
            for i, cut in enumerate(cuts):
                if cut:
                    held[i] = held[i].at[pl.ds(cut[0] * cut[1], cut[1])]
            body(*held, *refs[len(given) + len(after) :])

        spaces = [anywhere if any(index[j] == i for j in loose) else vmem for i in range(len(given))]
        return pl.pallas_call(
            inner,
            out_shape=tuple(jax.ShapeDtypeStruct(s, d) for s, d in outs),
            in_specs=spaces + [anywhere] * len(after),
            out_specs=tuple(vmem for _ in outs),
            scratch_shapes=list(scratch),
            compiler_params=pltpu.CompilerParams(vmem_limit_bytes=limit * 2**20),
            cost_estimate=pl.CostEstimate(
                flops=1 + int(weight * 1e9), bytes_accessed=1, transcendentals=0
            ),
            name=name,
        )(*given, *after)

    return run


def places(cap, rows, half, blk):
    k, j = iota((rows, rows), 0), iota((rows, rows), 1)
    cap_col = jnp.sum(jnp.where(k == j, cap, 0.0), axis=1, keepdims=True)
    rank_row = jnp.sum(jnp.where(k < j, cap_col, 0.0), axis=0, keepdims=True)
    rank_col = jnp.sum(jnp.where(j < k, cap, 0.0), axis=1, keepdims=True)
    at_row = iota((1, rows), 1).astype(F32)
    at_col = iota((rows, 1), 0).astype(F32)
    dest_row = jnp.where(cap > 0.5, rank_row, blk + at_row - rank_row)
    dest_col = jnp.where(cap_col > 0.5, rank_col, blk + at_col - rank_col)
    return dest_row.astype(jnp.int32), dest_col.astype(jnp.int32)


def sorted_rows(cot, cap, blk):
    rows = cot.shape[0]
    dest_row, _ = places(row_of(cap).astype(F32), rows, rows // 2, blk)
    pick = (iota((2 * blk, rows), 0) == dest_row).astype(BF16)
    c = dot_nn(pick, cot[...]).astype(BF16)
    return c[blk:], c[:blk]


def pre_body(
    tok_far, cot_far, cap_far, lens_far, gain2_far, cot_core, cap_core,
    xc, xn, n2n, cotn, cotc, cotn_core, cotc_core, bias,
    tok, cot, cap, lens, gain2, sems,
):
    pairs = ((cap_far, cap), (tok_far, tok), (lens_far, lens), (gain2_far, gain2), (cot_far, cot))
    copies = [pltpu.make_async_copy(a, b, sems.at[i]) for i, (a, b) in enumerate(pairs)]
    for c in copies:
        c.start()
    cotn_core[...], cotc_core[...] = sorted_rows(cot_core, cap_core, xc.shape[0])
    for c in copies:
        c.wait()
    rows = tok.shape[0]
    blk = xc.shape[0]
    dest_row, _ = places(row_of(cap).astype(F32), rows, rows // 2, blk)
    pick = (iota((2 * blk, rows), 0) == dest_row).astype(BF16)
    x = dot_nn(pick, tok[...])
    xc[...] = x[:blk].astype(BF16)
    xn[...] = x[blk:].astype(BF16)
    n2n[...] = norm_rows(x[blk:], row_of(gain2))[0].astype(BF16)
    c = dot_nn(pick, cot[...]).astype(BF16)
    cotn[...] = c[blk:]
    cotc[...] = c[:blk]
    position = iota((1, rows), 1)
    crop = jnp.ones((1, rows), F32)
    end = 0
    for s in range(lens.shape[1]):
        end = end + lens[0, s]
        crop = crop + (position >= end).astype(F32)
    crop_col = jnp.sum(jnp.where(iota((blk, rows), 0) == dest_row, crop, 0.0), axis=1, keepdims=True)
    crop_row = jnp.sum(
        jnp.where(iota((blk, blk), 0) == iota((blk, blk), 1), crop_col, 0.0), axis=0, keepdims=True
    )
    bias[...] = jnp.where(crop_col == crop_row, 0.0, NEGATIVE)


def sort_body(count, *refs):
    for cot, cap, out_n, out_c in zip(*(refs[k * count : (k + 1) * count] for k in range(4))):
        out_n[...], out_c[...] = sorted_rows(cot, cap, out_n.shape[0])


def half_mask(shape, e):
    return (iota(shape, 1) < HEAD_DIM) == (e == 0)


def fore_body(
    half,
    xc, bias, gain1, router, w_qkv, w_out, gain2,
    n1, qkv, probs, heads, attended, gate, n2c, stats,
):
    blk, width = xc.shape
    x = xc[...].astype(F32)
    low = norm_rows(x, row_of(gain1))[0].astype(BF16)
    n1[...] = low
    logit = jnp.sum(low.astype(F32) * row_of(router), axis=-1, keepdims=True)
    gated = jnp.where(iota((blk, 1), 0) < half, jax.nn.sigmoid(logit), 0.0)
    gate[...] = gated
    qkv[...] = dot_nn(low, w_qkv[...]).astype(BF16)
    scale = 1.0 / math.sqrt(HEAD_DIM)
    for pair in range(HEADS // 2):
        at = pair * PAIR
        q = qkv[:, at : at + PAIR]
        k = qkv[:, width + at : width + at + PAIR]
        v = qkv[:, 2 * width + at : 2 * width + at + PAIR]
        total = None
        for e in range(2):
            mask = half_mask((blk, PAIR), e)
            zero = jnp.zeros_like(q)
            scores = dot_nt(jnp.where(mask, q, zero), k) * scale + bias[...]
            exponent = jnp.exp(scores - jnp.max(scores, axis=-1, keepdims=True))
            prob = (exponent / jnp.sum(exponent, axis=-1, keepdims=True)).astype(BF16)
            probs[2 * pair + e] = prob
            part = dot_nn(prob, jnp.where(mask, v, zero))
            total = part if total is None else total + part
        heads[:, at : at + PAIR] = total.astype(BF16)
    att = dot_nn(heads[...], w_out[...])
    attended[...] = att
    branch = gated * att
    resid = x + branch
    n2c[...] = norm_rows(resid, row_of(gain2))[0].astype(BF16)
    stats[0:1, :] = jnp.sum(resid * resid, axis=0, keepdims=True)
    stats[1:2, :] = jnp.sum(branch * branch, axis=0, keepdims=True)


def mlp_body(blk, outs_at, n2s, cots, w_up, w_down, act, dpre, *outs):
    for s, (n2, cot) in enumerate(zip(n2s, cots)):
        rows = pl.ds(s * blk, blk)
        pre = dot_nn(n2[...], w_up[...])
        d_act = dot_nt(cot[...], w_down[...])
        square = pre * pre
        t = jnp.tanh(pre * (GELU_C + GELU_C * GELU_A * square))
        half_up = 0.5 + 0.5 * t
        slope = half_up + pre * (0.5 - 0.5 * t * t) * (GELU_C + 3.0 * GELU_C * GELU_A * square)
        a = (pre * half_up).astype(BF16)
        d = (d_act * slope).astype(BF16)
        act[rows, :] = a
        dpre[rows, :] = d
        (d_out, d_at), (h_out, h_at) = outs_at[s]
        outs[d_out][pl.ds(d_at, blk), :] = dot_nt(d, w_up[...]).astype(BF16)
        outs[h_out][pl.ds(h_at, blk), :] = dot_nn(a, w_down[...]).astype(BF16)


def copy_rows(sources, target):
    at = 0
    for ref in sources:
        target[at : at + ref.shape[0]] = ref[...]
        at += ref.shape[0]


def near_weights_body(act, dpre, n2s, cots, down, up, n2, cot):
    copy_rows(cots, cot)
    copy_rows(n2s, n2)
    down[...] = dot_tn(act[...], cot[...])
    up[...] = dot_tn(dpre[...], n2[...])


def weights_body(quarters, acts, dpres, n2s, cots, down, up, outs, act, dpre, n2, cot, total):
    units = down.shape[0]
    part = units // quarters
    copy_rows(acts, act)
    copy_rows(cots, cot)
    total[:units] = (down[...] + dot_tn(act[...], cot[...])).astype(BF16)
    copy_rows(dpres, dpre)
    copy_rows(n2s, n2)
    total[units:] = (up[...] + dot_tn(dpre[...], n2[...])).astype(BF16)
    lo = lax.rem(lax.axis_index("dp"), quarters)
    for p in range(quarters):
        for k in range(2):
            at = pl.multiple_of(k * units + lax.bitwise_xor(lo, p) * part, 16)
            outs[p][k * part : (k + 1) * part] = total[pl.ds(at, part), :]


def far_sum_body(d_c0, d_c1, n0, n1, h0, h1, joint, rest):
    def both(a, b):
        return (a[...].astype(F32) + b[...].astype(F32)).astype(BF16)

    joint[...] = both(d_c0, d_c1)
    size = n0.shape[0]
    rest[:size] = both(n0, n1)
    rest[size:] = both(h0, h1)


def add_body(count, *refs):
    total = refs[0][...].astype(F32)
    for ref in refs[1:count]:
        total = total + ref[...].astype(F32)
    refs[count][...] = total.astype(refs[count].dtype)


def assemble_body(quarters, *refs):
    ins, down, up, turned = refs[:quarters], *refs[quarters:]
    part = ins[0].shape[0] // 2
    lo = lax.rem(lax.axis_index("dp"), quarters)
    for p in range(quarters):
        at = pl.multiple_of(lax.bitwise_xor(lo, p) * part, 8)
        down[pl.ds(at, part), :] = ins[p][:part].astype(F32)
        turned[pl.ds(at, part), :] = ins[p][part:].astype(F32)
    up[...] = turned[...].T


def back_body(
    half,
    d_n2_0, d_n2_1, d_n2_2, cc, xc, attended, gate, heads, qkv, probs, w_out, gain2,
    d_resid_out, d_qkv, d_att_out, d_logit_out, g_gain2,
):
    blk, width = xc.shape
    scale = 1.0 / math.sqrt(HEAD_DIM)
    gated = gate[...]
    att = attended[...]
    resid = xc[...].astype(F32) + gated * att
    _, unit2, inverse2 = norm_rows(resid, row_of(gain2))
    d_n2 = d_n2_0[...].astype(F32) + d_n2_1[...].astype(F32)
    for at in range(0, d_n2_2.shape[0], blk):
        d_n2 = d_n2 + d_n2_2[at : at + blk].astype(F32)
    back2, g_gain2[...] = norm_back(d_n2, unit2, inverse2, row_of(gain2))
    d_resid = cc[...].astype(F32) + back2
    d_resid_out[...] = d_resid
    d_att = (d_resid * gated).astype(BF16)
    keep = (iota((blk, 1), 0) < half).astype(F32)
    d_gate = keep * jnp.sum(d_resid * att, axis=-1, keepdims=True)
    d_logit_out[...] = d_gate * gated * (1.0 - gated)
    d_att_out[...] = d_att
    d_heads = dot_nt(d_att, w_out[...]).astype(BF16)
    for pair in range(HEADS // 2):
        at = pair * PAIR
        q = qkv[:, at : at + PAIR]
        k = qkv[:, width + at : width + at + PAIR]
        v = qkv[:, 2 * width + at : 2 * width + at + PAIR]
        d_o = d_heads[:, at : at + PAIR]
        zero = jnp.zeros_like(q)
        d_q = d_k = d_v = 0.0
        for e in range(2):
            mask = half_mask((blk, PAIR), e)
            d_oe = jnp.where(mask, d_o, zero)
            prob = probs[2 * pair + e]
            prob_f = prob.astype(F32)
            d_prob = dot_nt(d_oe, v)
            d_score = (
                prob_f * (d_prob - jnp.sum(prob_f * d_prob, axis=-1, keepdims=True))
            ).astype(BF16)
            d_v = d_v + dot_tn(prob, d_oe)
            d_q = d_q + dot_nn(d_score, jnp.where(mask, k, zero))
            d_k = d_k + dot_tn(d_score, jnp.where(mask, q, zero))
        d_qkv[:, at : at + PAIR] = (d_q * scale).astype(BF16)
        d_qkv[:, width + at : width + at + PAIR] = (d_k * scale).astype(BF16)
        d_qkv[:, 2 * width + at : 2 * width + at + PAIR] = d_v.astype(BF16)


def products_body(tsize, heads, n1, d_qkv, d_att, table, *outs):
    width = n1.shape[1]
    me = lax.axis_index("dp") * tsize + lax.axis_index("tensor")
    share = width // (tsize * lax.axis_size("dp"))
    mid = outs[0].shape[0]
    for side in range(2):
        source = lax.bitwise_xor(table[side : side + 1, :], me) * share + table[2:3, :]
        order = (iota((width, width), 0) == source).astype(BF16)
        low = dot_nn(n1[...], order).astype(BF16)
        keep, send = outs[2 * side : 2 * side + 2]
        for k in range(2):
            at = k * width
            if side and k:
                product = dot_tn(dot_nn(heads[...], order).astype(BF16), d_att[...])
            else:
                column = (2 * side + k) * width
                product = dot_tn(low, d_qkv[:, column : column + width])
            product = product.astype(BF16)
            keep[:, at : at + width] = product[:mid]
            send[:, at : at + width] = product[mid:]


def add_split_body(count, pieces, *refs):
    total = refs[0][...].astype(F32)
    for ref in refs[1:count]:
        total = total + ref[...].astype(F32)
    size = total.shape[0] // pieces
    for p in range(pieces):
        refs[count + p][...] = total[p * size : (p + 1) * size].astype(refs[count + p].dtype)


def put_back(pick, rows):
    top = rows.astype(BF16)
    rest = (rows - top.astype(F32)).astype(BF16)
    return dot_nn(pick, top) + dot_nn(pick, rest)


def post_body(
    cap, d_n0, hid_c0, hid_n0, d_nx, hid_c1, hid_n1, rest,
    xc, xn, cn, attended, gate, d_resid_c, d_qkv, d_logit, n1, w_qkv, gain1, gain2, router, g_gain2c, stats1,
    mixed, grad_in, sums,
):
    rows = mixed.shape[0]
    blk = xc.shape[0]
    _, dest_col = places(row_of(cap).astype(F32), rows, rows // 2, blk)
    pick_c = (iota((rows, blk), 1) == dest_col).astype(BF16)
    pick_n = (iota((rows, blk), 1) + blk == dest_col).astype(BF16)
    x_c, x_n = xc[...].astype(F32), xn[...].astype(F32)

    d_n1 = dot_nt(d_qkv[...], w_qkv[...]) + d_logit[...] * row_of(router)
    _, unit1, inverse1 = norm_rows(x_c, row_of(gain1))
    back1, g_gain1 = norm_back(d_n1, unit1, inverse1, row_of(gain1))
    grad_c = d_resid_c[...] + back1

    def summed(first, second, others, start, stop):
        total = first[...].astype(F32) + second[...].astype(F32)
        for o in range(start, stop, blk):
            total = total + others[o : o + blk].astype(F32)
        return total

    third = rest.shape[0] // 3
    d_n2n = summed(d_n0, d_nx, rest, 0, third)
    h_n = summed(hid_n0, hid_n1, rest, third, 2 * third)
    h_c = summed(hid_c0, hid_c1, rest, 2 * third, 3 * third)
    mix_c = (x_c + gate[...] * attended[...] + h_c).astype(BF16)
    mix_n = (x_n + h_n).astype(BF16)
    mixed[...] = (dot_nn(pick_c, mix_c) + dot_nn(pick_n, mix_n)).astype(BF16)
    _, unit, inverse = norm_rows(x_n, row_of(gain2))
    back, g_gain2n = norm_back(d_n2n, unit, inverse, row_of(gain2))
    d_resid_n = cn[...].astype(F32) + back
    grad_in[...] = put_back(pick_c, grad_c) + put_back(pick_n, d_resid_n)

    def over_rows(a):
        return jnp.sum(a, axis=0, keepdims=True)

    sums[...] = jnp.zeros_like(sums)
    sums[0:1, :] = g_gain1
    sums[1:2, :] = over_rows(d_logit[...] * n1[...].astype(F32))
    sums[2:3, :] = g_gain2c[...] + g_gain2n
    sums[3:4, :] = stats1[0:1, :] + over_rows(x_n * x_n)
    sums[4:5, :] = stats1[1:2, :]
    sums[5:6, :] = over_rows(h_c * h_c) + over_rows(h_n * h_n)


CORES = 2
GROUP = 4
W_MLP1 = 20.0


def swap(name, array, axis, size, bits):
    with jax.named_scope(name):
        return lax.ppermute(array, axis, [(t, t ^ bits) for t in range(size)])


def add(name, arrays, after=(), weight=1.0):
    return call(
        lambda *refs: add_body(len(arrays), *refs),
        [(arrays[0].shape, BF16)],
        name,
        after=after,
        weight=weight,
    )(*arrays)[0]


def in_order(name, own, others, place, after, weight):
    if len(others) > 1:
        held = jnp.stack([own, *others])
        own, *others = [
            lax.dynamic_index_in_dim(held, place ^ at, 0, keepdims=False) for at in range(len(held))
        ]
    return add(name, [own, *others], after, weight)


def shards(
    tokens, lengths, capacity, norm1_gain, router, w_qkv, w_out, norm2_gain, w_up, w_down, cotangent
):
    rows, width = tokens.shape
    half = rows // 2
    blk = -(-half // 16) * 16
    units = w_up.shape[1]
    tsize, dsize = lax.axis_size("tensor"), lax.axis_size("dp")
    ysize = tsize // CORES
    others = range(1, ysize)
    cap, gain1, gain2, route = capacity, norm1_gain, norm2_gain, router
    small = (blk, width)

    def far(name, array):
        return [swap("y_" + name, array, "tensor", tsize, dy * CORES) for dy in others]

    def across(name, array):
        return swap("core_" + name, array, "tensor", tsize, 1)

    cap_far, cot_far = far("cap", cap), far("cot", cotangent)
    xc, xn, n2n, cotn, cotc, cotn_core, cotc_core, bias = call(
        pre_body,
        [(small, BF16)] * 7 + [((blk, blk), F32)],
        "pre",
        scratch=[
            pltpu.VMEM(tokens.shape, BF16), pltpu.VMEM(cotangent.shape, BF16), pltpu.VMEM(cap.shape, jnp.int32),
            pltpu.SMEM(lengths.shape, jnp.int32), pltpu.VMEM(gain2.shape, F32), pltpu.SemaphoreType.DMA((5,)),
        ],
        loose=range(5),
        weight=20.0,
    )(tokens, cotangent, cap, lengths, gain2, across("cot", cotangent), across("cap", cap))

    def group(name, pieces):
        return [swap("xz_" + name, pieces[p], "dp", dsize, p) for p in range(1, GROUP)]

    def high(name, pieces):
        return [
            swap("zz_" + name, pieces[p % len(pieces)], "dp", dsize, p * GROUP)
            for p in range(1, dsize // GROUP)
        ]

    n2n_far, n2n_core = far("n2n", n2n), across("n2n", n2n)

    n1, qkv, probs, heads, attended, gate, n2c, stats1 = call(
        lambda *refs: fore_body(half, *refs),
        [
            (small, BF16), ((blk, 3 * width), BF16), ((HEADS, blk, blk), BF16), (small, BF16),
            (small, F32), ((blk, 1), F32), (small, BF16), ((2, width), F32),
        ],
        "fore",
    )(xc, bias, gain1, route, w_qkv, w_out, gain2)

    n2c_far, n2c_core = far("n2c", n2c), across("n2c", n2c)

    def mlp(name, n2s, cots, outs, outs_at, after=(), weight=1.0):
        tall = blk * len(outs_at)
        count = len(n2s)
        return call(
            lambda *refs: mlp_body(
                blk, outs_at, refs[:count], refs[count : 2 * count], *refs[2 * count :]
            ),
            [((tall, units), BF16)] * 2 + [((n * blk, width), BF16) for n in outs],
            name,
            after=after,
            weight=weight,
        )(*n2s, *cots, w_up, w_down)

    n2_near = [n2c, n2n, n2c_core, n2n_core]
    cot_near = [cotc, cotn, cotc_core, cotn_core]
    at_near = [((c, k * blk), (c, (2 + k) * blk)) for c in range(CORES) for k in range(2)]
    act_a, dpre_a, near_0, near_1 = mlp("mlp_near", n2_near, cot_near, [4, 4], at_near)
    near_1 = across("near", near_1)

    def tie(name, arrays, after):
        return list(
            pl.pallas_call(
                lambda *refs: None,
                out_shape=tuple(jax.ShapeDtypeStruct(a.shape, a.dtype) for a in arrays),
                in_specs=[pl.BlockSpec(memory_space=pl.ANY)] * (len(arrays) + len(after)),
                out_specs=tuple(pl.BlockSpec(memory_space=pl.ANY) for _ in arrays),
                input_output_aliases={i: i for i in range(len(arrays))},
                compiler_params=pltpu.CompilerParams(vmem_limit_bytes=2**20),
                name=name,
            )(*arrays, *after)
        )

    count = len(cot_far)
    sorted_far = call(
        lambda *refs: sort_body(count, *refs),
        [(small, BF16)] * (2 * count),
        "sort_far",
        after=[act_a],
    )(*cot_far, *cap_far)
    cotn_far, cotc_far = list(sorted_far[:count]), list(sorted_far[count:])
    n2n_far = tie("tie_n", n2n_far, [cotn_far[0]])
    n2n_all = n2n_far + [across("far_n2n", a) for a in n2n_far]
    cotn_all = cotn_far + [across("far_cotn", a) for a in cotn_far]
    cotc_all = cotc_far + [across("far_cotc", a) for a in cotc_far]

    tall = 4 * blk
    down_near, up_near = call(
        lambda act, dpre, *refs: near_weights_body(act, dpre, refs[:4], refs[4:8], *refs[8:]),
        [((units, width), F32), ((units, width), F32)],
        "weights_near",
        scratch=[pltpu.VMEM((tall, width), BF16)] * 2,
        after=n2n_far[:1],
    )(act_a, dpre_a, *n2_near, *cot_near)

    far_at = range(CORES * (ysize - 1))
    place = lambda s: (s // (ysize - 1), s % (ysize - 1) * blk)
    act_n, dpre_n, far_n0, far_n1 = mlp(
        "mlp_far_n", n2n_all, cotn_all, [2 * (ysize - 1)] * 2,
        [(place(s), (place(s)[0], place(s)[1] + (ysize - 1) * blk)) for s in far_at],
        [down_near],
    )
    far_n1 = across("far_n", far_n1)
    n2c_far = tie("tie_c", n2c_far, [act_n])
    n2c_all = n2c_far + [across("far_n2c", a) for a in n2c_far]
    act_c, dpre_c, d_c0, d_c1, hid_c0, hid_c1 = mlp(
        "mlp_far_c", n2c_all, cotc_all, [ysize - 1] * 4,
        [(place(s), (place(s)[0] + 2, place(s)[1])) for s in far_at],
    )
    d_c1, hid_c1 = across("d_c", d_c1), across("hid_c", hid_c1)

    def send_back(name, joint, groups):
        if ysize == 2:
            return swap("y_" + name, joint, "tensor", tsize, CORES)
        cut = joint.reshape(groups, ysize - 1, blk, width)
        got = [swap("y_" + name, cut[:, dy - 1], "tensor", tsize, dy * CORES) for dy in others]
        return jnp.stack(got, axis=1).reshape(joint.shape)

    mark, rest = call(
        far_sum_body,
        [(((ysize - 1) * blk, width), BF16), ((3 * (ysize - 1) * blk, width), BF16)],
        "far_sum",
    )(d_c0, d_c1, far_n0, far_n1, hid_c0, hid_c1)
    d_c2 = send_back("d_c", mark, 1)
    rest = send_back("rest", rest, 3)

    cots, n2s = cotn_all + cotc_all, n2n_all + n2c_all
    count, tall = len(cots), len(cots) * blk
    part = (units // GROUP * 2, width)

    def weights(*refs):
        acts, dpres, refs = refs[:2], refs[2:4], refs[4:]
        n2s, cots, refs = refs[:count], refs[count : 2 * count], refs[2 * count :]
        weights_body(
            GROUP, acts, dpres, n2s, cots, *refs[:2], refs[2 : 2 + GROUP], *refs[2 + GROUP :]
        )

    quarters = call(
        weights,
        [(part, BF16)] * GROUP,
        "weights",
        scratch=[
            pltpu.VMEM((tall, units), BF16), pltpu.VMEM((tall, units), BF16),
            pltpu.VMEM((tall, width), BF16), pltpu.VMEM((tall, width), BF16),
            pltpu.VMEM((2 * units, width), BF16),
        ],
        after=[mark],
    )(act_n, act_c, dpre_n, dpre_c, *n2s, *cots, down_near, up_near)
    quarters_got = group("mlp", quarters)
    mark = quarters[0]

    shares = tsize * dsize
    share = width // shares
    def owners(y_first):
        table = []
        for core in range(CORES):
            for first in range(ysize if y_first else 2):
                for then in range(2 if y_first else ysize):
                    y, x = (first, then) if y_first else (then, first)
                    for z in range(2):
                        for hi in range(dsize // GROUP):
                            place = (hi * GROUP + z * 2 + x) * tsize + y * CORES + core
                            table += [place] * share
        return table

    table = jnp.array([owners(True), owners(False), list(range(share)) * shares], jnp.int32)
    d_resid_c, d_qkv, d_att, d_logit, g_gain2c = call(
        lambda *refs: back_body(half, *refs),
        [
            (small, F32), ((blk, 3 * width), BF16), (small, BF16), ((blk, 1), F32), ((1, width), F32),
        ],
        "back",
        after=[mark],
        weight=20.0,
    )(
        (near_0, 0, blk), (near_1, 0, blk), d_c2, cotc, xc, attended, gate, heads, qkv, probs,
        w_out, gain2,
    )
    left, left_got, right, right_got = call(
        lambda *refs: products_body(tsize, *refs),
        [((width // 2, 2 * width), BF16)] * 4,
        "products",
    )(heads, n1, d_qkv, d_att, table)
    left_got, right_got = across("left", left_got), across("right", right_got)

    mine = add("mlp_1", [quarters[0], *quarters_got], after=[left, rest], weight=W_MLP1)
    mine_got = high("mlp", [mine])

    def sums_of(name, *sets, after=(), along=(), weight=1.0):
        given = [a for arrays, _ in sets for a in arrays]

        def body(*refs):
            ins, outs = list(refs[: len(given)]), list(refs[len(given) + len(along) :])
            for i in range(len(along)):
                outs[-len(along) + i][...] = refs[len(given) + i][...]
            for arrays, count in sets:
                add_split_body(len(arrays), count, *ins[: len(arrays)], *outs[:count])
                del ins[: len(arrays)], outs[:count]

        shapes = []
        for arrays, count in sets:
            rows, columns = arrays[0].shape
            shapes += [((rows // count, columns), BF16)] * count
        shapes += [(a.shape, a.dtype) for a in along]
        return call(body, shapes, name, after=after, weight=weight)(*given, *along)

    *left, right, right_got = sums_of(
        "att_1", ([left, left_got], ysize), ([right, right_got], 2), after=[mine]
    )
    left_got = [swap("y_left", left[p], "tensor", tsize, p * CORES) for p in others]
    right_got = swap("x_right", right_got, "dp", dsize, 1)

    mixed, grad_input, sums = call(
        post_body,
        [((rows, width), BF16), ((rows, width), F32), ((8, width), F32)],
        "post",
        after=[right],
    )(
        cap, (near_0, 1, blk), (near_0, 2, blk), (near_0, 3, blk), (near_1, 1, blk), (near_1, 2, blk),
        (near_1, 3, blk), rest,
        xc, xn, cotn, attended, gate, d_resid_c, d_qkv, d_logit, n1, w_qkv, gain1, gain2, route, g_gain2c,
        stats1,
    )

    right = sums_of("right_2", ([right, right_got], ysize), after=[sums], weight=0.0)
    right_got = [swap("y_right", right[p], "tensor", tsize, p * CORES) for p in others]
    left, left_got = sums_of("left_2", ([left[0], *left_got], 2), after=[right[0]], weight=0.0)
    left_got = swap("x_left", left_got, "dp", dsize, 1)
    step = 1
    while step < tsize:
        sums = sums + swap("sums", sums, "tensor", tsize, step)
        step *= 2
    def join_body(*refs):
        ins, (kept, sent, along) = refs[:-3], refs[-3:]
        along[...] = ins[-1][...]
        size = kept.shape[0]
        middle = kept.shape[1] // 2
        for columns, group in ((slice(0, middle), ins[:2]), (slice(middle, 2 * middle), ins[2:-1])):
            total = group[0][...].astype(F32)
            for ref in group[1:]:
                total = total + ref[...].astype(F32)
            kept[:, columns] = total[:size].astype(BF16)
            sent[:, columns] = total[size:].astype(BF16)

    half_shape = (left.shape[0] // 2, 4 * width)
    att, att_got, sums = call(
        join_body, [(half_shape, BF16), (half_shape, BF16), (sums.shape, F32)], "att_3", weight=0.0
    )(left, left_got, right[0], *right_got, sums)
    att_got = swap("z_att", att_got, "dp", dsize, 2)
    mine = in_order("mlp_2", mine, mine_got, lax.axis_index("dp") // GROUP, [att], 20.0)
    pieces = [mine] + group("mlp_back", [mine] * GROUP)
    step = 1
    while step < dsize:
        sums = sums + swap("sums", sums, "dp", dsize, step)
        step *= 2
    *att, sums = sums_of(
        "att_4", ([att, att_got], dsize // GROUP), after=[mine], along=[sums], weight=0.0
    )
    att_got = high("att", att)
    g_down, g_up = call(
        lambda *refs: assemble_body(GROUP, *refs),
        [((units, width), F32), ((width, units), F32)],
        "assemble",
        weight=20.0,
        scratch=[pltpu.VMEM((units, width), F32)],
    )(*pieces)
    held = att[0].astype(F32)
    for a in att_got:
        held = held + a.astype(F32)
    count = rows * width * dsize * tsize
    norms = jnp.sqrt(jnp.sum(sums[3:6], axis=-1) / count)
    return (
        mixed,
        grad_input,
        sums[0],
        sums[1],
        held[:, : 3 * width],
        held[:, 3 * width :],
        sums[2],
        g_up,
        g_down,
        norms,
    )


def solution(mesh):
    return jax.shard_map(
        shards,
        mesh=mesh,
        in_specs=(
            P(("dp", "tensor"), None),
            P(("dp", "tensor"), None),
            P(("dp", "tensor")),
            P(),
            P(),
            P(),
            P(),
            P(),
            P(None, "tensor"),
            P("tensor", None),
            P(("dp", "tensor"), None),
        ),
        out_specs=(
            P(("dp", "tensor"), None),
            P(("dp", "tensor"), None),
            P(),
            P(),
            P(("dp", "tensor"), None),
            P(("dp", "tensor"), None),
            P(),
            P(None, "tensor"),
            P("tensor", None),
            P(),
        ),
        check_vma=False,
    )
```

```python
import math

import jax
import jax.numpy as jnp
from jax import lax
from jax.experimental import pallas as pl
from jax.experimental.pallas import tpu as pltpu
from jax.sharding import PartitionSpec as P

HEADS = 12
HEAD_DIM = 64
PAIR = 2 * HEAD_DIM
EPSILON = 1e-06
NEGATIVE = -1000000000.0
GELU_C = math.sqrt(2.0 / math.pi)
GELU_A = 0.044715
F32 = jnp.float32
BF16 = jnp.bfloat16
VMEM_LIMIT = 24


def dot_nn(a, b):
    return lax.dot_general(a, b, (((1,), (0,)), ((), ())), preferred_element_type=F32)


def dot_nt(a, b):
    return lax.dot_general(a, b, (((1,), (1,)), ((), ())), preferred_element_type=F32)


def dot_tn(a, b):
    return lax.dot_general(a, b, (((0,), (0,)), ((), ())), preferred_element_type=F32)


def iota(shape, dim):
    return lax.broadcasted_iota(jnp.int32, shape, dim)


def row_of(ref):
    return ref[...].reshape(1, ref.shape[0])


def norm_rows(rows, gain):
    center = rows - jnp.mean(rows, axis=-1, keepdims=True)
    inverse = lax.rsqrt(jnp.mean(center * center, axis=-1, keepdims=True) + EPSILON)
    unit = center * inverse
    return unit * gain, unit, inverse


def norm_back(grad_out, unit, inverse, gain):
    scaled = grad_out * gain
    mean_grad = jnp.mean(scaled, axis=-1, keepdims=True)
    mean_cross = jnp.mean(scaled * unit, axis=-1, keepdims=True)
    grad_in = inverse * (scaled - mean_grad - unit * mean_cross)
    return grad_in, jnp.sum(grad_out * unit, axis=0, keepdims=True)


class Pair(list):
    pass


def call(body, outs, name, scratch=(), loose=(), after=(), weight=1.0, limit=VMEM_LIMIT):
    vmem = pl.BlockSpec(memory_space=pltpu.VMEM)
    anywhere = pl.BlockSpec(memory_space=pl.ANY)

    def run(*args):
        flat = []
        for a in args:
            flat += a if isinstance(a, Pair) else [a[0] if isinstance(a, tuple) else a]
        given = list({id(a): a for a in flat}.values())
        index = [[id(g) for g in given].index(id(a)) for a in flat]

        def inner(*refs):
            held = []
            for a in args:
                at = index[sum(len(h) if isinstance(h, tuple) else 1 for h in held)]
                if isinstance(a, Pair):
                    nxt = index[sum(len(h) if isinstance(h, tuple) else 1 for h in held) + 1]
                    held.append((refs[at], refs[nxt]))
                elif isinstance(a, tuple):
                    held.append(refs[at].at[pl.ds(a[1] * a[2], a[2])])
                else:
                    held.append(refs[at])
            body(*held, *refs[len(given) + len(after) :])

        spaces = [anywhere if any(index[j] == i for j in loose) else vmem for i in range(len(given))]
        return pl.pallas_call(
            inner,
            out_shape=tuple(jax.ShapeDtypeStruct(s, d) for s, d in outs),
            in_specs=spaces + [anywhere] * len(after),
            out_specs=tuple(vmem for _ in outs),
            scratch_shapes=list(scratch),
            compiler_params=pltpu.CompilerParams(vmem_limit_bytes=limit * 2**20),
            cost_estimate=pl.CostEstimate(
                flops=1 + int(weight * 1e9), bytes_accessed=1, transcendentals=0
            ),
            name=name,
        )(*given, *after)

    return run


def places(cap, rows, half, blk):
    k, j = iota((rows, rows), 0), iota((rows, rows), 1)
    cap_col = jnp.sum(jnp.where(k == j, cap, 0.0), axis=1, keepdims=True)
    rank_row = jnp.sum(jnp.where(k < j, cap_col, 0.0), axis=0, keepdims=True)
    rank_col = jnp.sum(jnp.where(j < k, cap, 0.0), axis=1, keepdims=True)
    at_row = iota((1, rows), 1).astype(F32)
    at_col = iota((rows, 1), 0).astype(F32)
    dest_row = jnp.where(cap > 0.5, rank_row, blk + at_row - rank_row)
    dest_col = jnp.where(cap_col > 0.5, rank_col, blk + at_col - rank_col)
    return dest_row.astype(jnp.int32), dest_col.astype(jnp.int32)


def sorted_rows(cot, cap, blk):
    rows = cot.shape[0]
    dest_row, _ = places(row_of(cap).astype(F32), rows, rows // 2, blk)
    pick = (iota((2 * blk, rows), 0) == dest_row).astype(BF16)
    c = dot_nn(pick, cot[...]).astype(BF16)
    return c[blk:], c[:blk]


def pre_body(
    tok_far, cot_far, cap_far, lens_far, gain2_far, cot_core, cap_core,
    xc, xn, n2n, cotn, cotc, cotn_core, cotc_core, bias,
    tok, cot, cap, lens, gain2, sems,
):
    pairs = ((cap_far, cap), (tok_far, tok), (lens_far, lens), (gain2_far, gain2), (cot_far, cot))
    copies = [pltpu.make_async_copy(a, b, sems.at[i]) for i, (a, b) in enumerate(pairs)]
    for c in copies:
        c.start()
    cotn_core[...], cotc_core[...] = sorted_rows(cot_core, cap_core, xc.shape[0])
    for c in copies:
        c.wait()
    rows = tok.shape[0]
    blk = xc.shape[0]
    dest_row, _ = places(row_of(cap).astype(F32), rows, rows // 2, blk)
    pick = (iota((2 * blk, rows), 0) == dest_row).astype(BF16)
    x = dot_nn(pick, tok[...])
    xc[...] = x[:blk].astype(BF16)
    xn[...] = x[blk:].astype(BF16)
    n2n[...] = norm_rows(x[blk:], row_of(gain2))[0].astype(BF16)
    c = dot_nn(pick, cot[...]).astype(BF16)
    cotn[...] = c[blk:]
    cotc[...] = c[:blk]
    position = iota((1, rows), 1)
    crop = jnp.ones((1, rows), F32)
    end = 0
    for s in range(lens.shape[1]):
        end = end + lens[0, s]
        crop = crop + (position >= end).astype(F32)
    crop_col = jnp.sum(jnp.where(iota((blk, rows), 0) == dest_row, crop, 0.0), axis=1, keepdims=True)
    crop_row = jnp.sum(
        jnp.where(iota((blk, blk), 0) == iota((blk, blk), 1), crop_col, 0.0), axis=0, keepdims=True
    )
    bias[...] = jnp.where(crop_col == crop_row, 0.0, NEGATIVE)


def sort_body(count, *refs):
    for cot, cap, left, right, out_c in zip(*(refs[k * count : (k + 1) * count] for k in range(5))):
        rows, out_c[...] = sorted_rows(cot, cap, out_c.shape[0])
        middle = left.shape[1]
        left[...], right[...] = rows[:, :middle], rows[:, middle:]


def halve_body(count, *refs):
    for array, left, right in zip(*(refs[k * count : (k + 1) * count] for k in range(3))):
        middle = left.shape[1]
        left[...], right[...] = array[:, :middle], array[:, middle:]


def half_mask(shape, e):
    return (iota(shape, 1) < HEAD_DIM) == (e == 0)


def fore_body(
    half,
    xc, bias, gain1, router, w_qkv, w_out, gain2,
    n1, qkv, probs, heads, attended, gate, n2c, stats,
):
    blk, width = xc.shape
    x = xc[...].astype(F32)
    low = norm_rows(x, row_of(gain1))[0].astype(BF16)
    n1[...] = low
    logit = jnp.sum(low.astype(F32) * row_of(router), axis=-1, keepdims=True)
    gated = jnp.where(iota((blk, 1), 0) < half, jax.nn.sigmoid(logit), 0.0)
    gate[...] = gated
    qkv[...] = dot_nn(low, w_qkv[...]).astype(BF16)
    scale = 1.0 / math.sqrt(HEAD_DIM)
    for pair in range(HEADS // 2):
        at = pair * PAIR
        q = qkv[:, at : at + PAIR]
        k = qkv[:, width + at : width + at + PAIR]
        v = qkv[:, 2 * width + at : 2 * width + at + PAIR]
        total = None
        for e in range(2):
            mask = half_mask((blk, PAIR), e)
            zero = jnp.zeros_like(q)
            scores = dot_nt(jnp.where(mask, q, zero), k) * scale + bias[...]
            exponent = jnp.exp(scores - jnp.max(scores, axis=-1, keepdims=True))
            prob = (exponent / jnp.sum(exponent, axis=-1, keepdims=True)).astype(BF16)
            probs[2 * pair + e] = prob
            part = dot_nn(prob, jnp.where(mask, v, zero))
            total = part if total is None else total + part
        heads[:, at : at + PAIR] = total.astype(BF16)
    att = dot_nn(heads[...], w_out[...])
    attended[...] = att
    branch = gated * att
    resid = x + branch
    n2c[...] = norm_rows(resid, row_of(gain2))[0].astype(BF16)
    stats[0:1, :] = jnp.sum(resid * resid, axis=0, keepdims=True)
    stats[1:2, :] = jnp.sum(branch * branch, axis=0, keepdims=True)


def mlp_body(blk, outs_at, n2s, cots, w_up, w_down, act, dpre, *outs):
    for s, (n2, cot) in enumerate(zip(n2s, cots)):
        rows = pl.ds(s * blk, blk)
        pre = dot_nn(whole(n2), w_up[...])
        d_act = dot_nt(whole(cot), w_down[...])
        square = pre * pre
        t = jnp.tanh(pre * (GELU_C + GELU_C * GELU_A * square))
        half_up = 0.5 + 0.5 * t
        slope = half_up + pre * (0.5 - 0.5 * t * t) * (GELU_C + 3.0 * GELU_C * GELU_A * square)
        a = (pre * half_up).astype(BF16)
        d = (d_act * slope).astype(BF16)
        act[rows, :] = a
        dpre[rows, :] = d
        (d_out, d_at), (h_out, h_at) = outs_at[s]
        outs[d_out][pl.ds(d_at, blk), :] = dot_nt(d, w_up[...]).astype(BF16)
        outs[h_out][pl.ds(h_at, blk), :] = dot_nn(a, w_down[...]).astype(BF16)


def copy_rows(sources, target):
    at = 0
    for ref in sources:
        rows = whole(ref)
        target[at : at + rows.shape[0]] = rows
        at += rows.shape[0]


def whole(ref):
    if isinstance(ref, tuple):
        return jnp.concatenate([r[...] for r in ref], axis=1)
    return ref[...]


def near_weights_body(act, dpre, n2s, cots, down, up, n2, cot):
    copy_rows(cots, cot)
    copy_rows(n2s, n2)
    down[...] = dot_tn(act[...], cot[...])
    up[...] = dot_tn(n2[...], dpre[...])


def weights_body(quarters, acts, dpres, n2s, cots, down, up, outs, act, dpre, n2, cot, total, grad_up):
    units = down.shape[0]
    part = units // quarters
    copy_rows(acts, act)
    copy_rows(cots, cot)
    total[...] = (down[...] + dot_tn(act[...], cot[...])).astype(BF16)
    copy_rows(dpres, dpre)
    copy_rows(n2s, n2)
    grad_up[...] = (up[...] + dot_tn(n2[...], dpre[...])).astype(BF16)
    lo = lax.rem(lax.axis_index("dp"), quarters)
    for p in range(quarters):
        first = lax.bitwise_xor(lo, p) * part
        outs[p][:part] = total[pl.ds(pl.multiple_of(first, 16), part), :]
        blocks = grad_up.shape[0] // units
        for k in range(blocks):
            at = pl.multiple_of(first * blocks + k * part, 16)
            outs[p][part:, k * units : (k + 1) * units] = grad_up[pl.ds(at, part), :]


def far_sum_body(d_c0, d_c1, n0, n1, h0, h1, joint, rest):
    def both(a, b):
        return (a[...].astype(F32) + b[...].astype(F32)).astype(BF16)

    joint[...] = both(d_c0, d_c1)
    size = n0.shape[0]
    rest[:size] = both(n0, n1)
    rest[size:] = both(h0, h1)


def add_body(count, *refs):
    total = refs[0][...].astype(F32)
    for ref in refs[1:count]:
        total = total + ref[...].astype(F32)
    refs[count][...] = total.astype(refs[count].dtype)


def spread_body(own, other, both):
    size = own.shape[0]
    both[:size] = own[...]
    both[size:] = other[...]


def assemble_body(downs, ups, down, up):
    part = downs[0].shape[0]
    units = up.shape[1]
    blocks = up.shape[0] // units
    lo = lax.rem(lax.axis_index("dp"), len(downs))
    for p in range(len(downs)):
        first = lax.bitwise_xor(lo, p) * part
        down[pl.ds(pl.multiple_of(first, 8), part), :] = downs[p][...].astype(F32)
        for k in range(blocks):
            at = pl.multiple_of(first * blocks + k * part, 8)
            up[pl.ds(at, part), :] = ups[p][:, k * units : (k + 1) * units].astype(F32)


def back_body(
    half,
    d_n2_0, d_n2_1, d_n2_2, cc, xc, attended, gate, heads, qkv, probs, w_out, gain2,
    d_resid_out, d_qkv, d_att_out, d_logit_out, g_gain2,
):
    blk, width = xc.shape
    scale = 1.0 / math.sqrt(HEAD_DIM)
    gated = gate[...]
    att = attended[...]
    resid = xc[...].astype(F32) + gated * att
    _, unit2, inverse2 = norm_rows(resid, row_of(gain2))
    d_n2 = d_n2_0[...].astype(F32) + d_n2_1[...].astype(F32)
    for at in range(0, d_n2_2.shape[0], blk):
        d_n2 = d_n2 + d_n2_2[at : at + blk].astype(F32)
    back2, g_gain2[...] = norm_back(d_n2, unit2, inverse2, row_of(gain2))
    d_resid = cc[...].astype(F32) + back2
    d_resid_out[...] = d_resid
    d_att = (d_resid * gated).astype(BF16)
    keep = (iota((blk, 1), 0) < half).astype(F32)
    d_gate = keep * jnp.sum(d_resid * att, axis=-1, keepdims=True)
    d_logit_out[...] = d_gate * gated * (1.0 - gated)
    d_att_out[...] = d_att
    d_heads = dot_nt(d_att, w_out[...]).astype(BF16)
    for pair in range(HEADS // 2):
        at = pair * PAIR
        q = qkv[:, at : at + PAIR]
        k = qkv[:, width + at : width + at + PAIR]
        v = qkv[:, 2 * width + at : 2 * width + at + PAIR]
        d_o = d_heads[:, at : at + PAIR]
        zero = jnp.zeros_like(q)
        d_q = d_k = d_v = 0.0
        for e in range(2):
            mask = half_mask((blk, PAIR), e)
            d_oe = jnp.where(mask, d_o, zero)
            prob = probs[2 * pair + e]
            prob_f = prob.astype(F32)
            d_prob = dot_nt(d_oe, v)
            d_score = (
                prob_f * (d_prob - jnp.sum(prob_f * d_prob, axis=-1, keepdims=True))
            ).astype(BF16)
            d_v = d_v + dot_tn(prob, d_oe)
            d_q = d_q + dot_nn(d_score, jnp.where(mask, k, zero))
            d_k = d_k + dot_tn(d_score, jnp.where(mask, q, zero))
        d_qkv[:, at : at + PAIR] = (d_q * scale).astype(BF16)
        d_qkv[:, width + at : width + at + PAIR] = (d_k * scale).astype(BF16)
        d_qkv[:, 2 * width + at : 2 * width + at + PAIR] = d_v.astype(BF16)


def products_body(tsize, heads, n1, d_qkv, d_att, table, *outs):
    width = n1.shape[1]
    me = lax.axis_index("dp") * tsize + lax.axis_index("tensor")
    share = width // (tsize * lax.axis_size("dp"))
    mid = outs[0].shape[0]
    for side in range(2):
        source = lax.bitwise_xor(table[side : side + 1, :], me) * share + table[2:3, :]
        order = (iota((width, width), 0) == source).astype(BF16)
        low = dot_nn(n1[...], order).astype(BF16)
        keep, send = outs[2 * side : 2 * side + 2]
        for k in range(2):
            at = k * width
            if side and k:
                product = dot_tn(dot_nn(heads[...], order).astype(BF16), d_att[...])
            else:
                column = (2 * side + k) * width
                product = dot_tn(low, d_qkv[:, column : column + width])
            product = product.astype(BF16)
            keep[:, at : at + width] = product[:mid]
            send[:, at : at + width] = product[mid:]


def to_pair(sums):
    top = sums.astype(BF16)
    return jnp.concatenate([top, (sums - top.astype(F32)).astype(BF16)], axis=0)


def from_pair(pair):
    size = pair.shape[0] // 2
    return pair[:size].astype(F32) + pair[size:].astype(F32)


def add_split_body(count, pieces, *refs):
    total = refs[0][...].astype(F32)
    for ref in refs[1:count]:
        total = total + ref[...].astype(F32)
    size = total.shape[0] // pieces
    for p in range(pieces):
        refs[count + p][...] = total[p * size : (p + 1) * size].astype(refs[count + p].dtype)


def put_back(pick, rows):
    top = rows.astype(BF16)
    rest = (rows - top.astype(F32)).astype(BF16)
    return dot_nn(pick, top) + dot_nn(pick, rest)


def post_body(
    cap, d_n0, hid_c0, hid_n0, d_nx, hid_c1, hid_n1, rest,
    xc, xn, cn, attended, gate, d_resid_c, d_qkv, d_logit, n1, w_qkv, gain1, gain2, router, g_gain2c, stats1,
    mixed, grad_in, sums,
):
    rows = mixed.shape[0]
    blk = xc.shape[0]
    _, dest_col = places(row_of(cap).astype(F32), rows, rows // 2, blk)
    pick_c = (iota((rows, blk), 1) == dest_col).astype(BF16)
    pick_n = (iota((rows, blk), 1) + blk == dest_col).astype(BF16)
    x_c, x_n = xc[...].astype(F32), xn[...].astype(F32)

    d_n1 = dot_nt(d_qkv[...], w_qkv[...]) + d_logit[...] * row_of(router)
    _, unit1, inverse1 = norm_rows(x_c, row_of(gain1))
    back1, g_gain1 = norm_back(d_n1, unit1, inverse1, row_of(gain1))
    grad_c = d_resid_c[...] + back1

    def summed(first, second, others, start, stop):
        total = first[...].astype(F32) + second[...].astype(F32)
        for o in range(start, stop, blk):
            total = total + others[o : o + blk].astype(F32)
        return total

    third = rest.shape[0] // 3
    d_n2n = summed(d_n0, d_nx, rest, 0, third)
    h_n = summed(hid_n0, hid_n1, rest, third, 2 * third)
    h_c = summed(hid_c0, hid_c1, rest, 2 * third, 3 * third)
    mix_c = (x_c + gate[...] * attended[...] + h_c).astype(BF16)
    mix_n = (x_n + h_n).astype(BF16)
    mixed[...] = (dot_nn(pick_c, mix_c) + dot_nn(pick_n, mix_n)).astype(BF16)
    _, unit, inverse = norm_rows(x_n, row_of(gain2))
    back, g_gain2n = norm_back(d_n2n, unit, inverse, row_of(gain2))
    d_resid_n = cn[...].astype(F32) + back
    grad_in[...] = put_back(pick_c, grad_c) + put_back(pick_n, d_resid_n)

    def over_rows(a):
        return jnp.sum(a, axis=0, keepdims=True)

    sums[...] = jnp.zeros_like(sums)
    sums[0:1, :] = g_gain1
    sums[1:2, :] = over_rows(d_logit[...] * n1[...].astype(F32))
    sums[2:3, :] = g_gain2c[...] + g_gain2n
    sums[3:4, :] = stats1[0:1, :] + over_rows(x_n * x_n)
    sums[4:5, :] = stats1[1:2, :]
    sums[5:6, :] = over_rows(h_c * h_c) + over_rows(h_n * h_n)


CORES = 2
GROUP = 4
PARTS = 1
W_MLP1 = 12.0
W_MLP2 = 0.0
W_LAST = 5.0


def swap(name, array, axis, size, bits):
    with jax.named_scope(name):
        return lax.ppermute(array, axis, [(t, t ^ bits) for t in range(size)])


def add(name, arrays, after=(), weight=1.0):
    return call(
        lambda *refs: add_body(len(arrays), *refs),
        [(arrays[0].shape, BF16)],
        name,
        after=after,
        weight=weight,
    )(*arrays)[0]


def in_order(name, own, others, place, count, after):
    if len(others) > 1:
        held = jnp.stack([own, *others])
        own, *others = [
            lax.dynamic_index_in_dim(held, place ^ at, 0, keepdims=False) for at in range(len(held))
        ]
    part = (own.shape[0] // count, own.shape[1])
    return call(
        lambda *refs: add_split_body(1 + len(others), count, *refs),
        [(part, BF16)] * count,
        name,
        after=after,
        weight=W_MLP2,
    )(own, *others)


def shards(
    tokens, lengths, capacity, norm1_gain, router, w_qkv, w_out, norm2_gain, w_up, w_down, cotangent
):
    rows, width = tokens.shape
    half = rows // 2
    blk = -(-half // 16) * 16
    units = w_up.shape[1]
    tsize, dsize = lax.axis_size("tensor"), lax.axis_size("dp")
    ysize = tsize // CORES
    others = range(1, ysize)
    cap, gain1, gain2, route = capacity, norm1_gain, norm2_gain, router
    small = (blk, width)

    def far(name, array):
        return [swap("y_" + name, array, "tensor", tsize, dy * CORES) for dy in others]

    def across(name, array):
        return swap("core_" + name, array, "tensor", tsize, 1)

    cap_far, cot_far = far("cap", cap), far("cot", cotangent)
    xc, xn, n2n, cotn, cotc, cotn_core, cotc_core, bias = call(
        pre_body,
        [(small, BF16)] * 7 + [((blk, blk), F32)],
        "pre",
        scratch=[
            pltpu.VMEM(tokens.shape, BF16), pltpu.VMEM(cotangent.shape, BF16), pltpu.VMEM(cap.shape, jnp.int32),
            pltpu.SMEM(lengths.shape, jnp.int32), pltpu.VMEM(gain2.shape, F32), pltpu.SemaphoreType.DMA((5,)),
        ],
        loose=range(5),
        after=cap_far,
        weight=20.0,
    )(tokens, cotangent, cap, lengths, gain2, across("cot", cotangent), across("cap", cap))

    def group(name, pieces):
        return [swap("xz_" + name, pieces[p], "dp", dsize, p) for p in range(1, GROUP)]

    def high(name, pieces):
        return [
            swap("zz_" + name, pieces[p % len(pieces)], "dp", dsize, p * GROUP)
            for p in range(1, dsize // GROUP)
        ]

    n2n_far, n2n_core = far("n2n", n2n), across("n2n", n2n)

    n1, qkv, probs, heads, attended, gate, n2c, stats1 = call(
        lambda *refs: fore_body(half, *refs),
        [
            (small, BF16), ((blk, 3 * width), BF16), ((HEADS, blk, blk), BF16), (small, BF16),
            (small, F32), ((blk, 1), F32), (small, BF16), ((2, width), F32),
        ],
        "fore",
    )(xc, bias, gain1, route, w_qkv, w_out, gain2)

    n2c_far, n2c_core = far("n2c", n2c), across("n2c", n2c)

    def mlp(name, n2s, cots, outs, outs_at, after=(), weight=1.0):
        tall = blk * len(outs_at)
        count = len(n2s)
        return call(
            lambda *refs: mlp_body(
                blk, outs_at, refs[:count], refs[count : 2 * count], *refs[2 * count :]
            ),
            [((tall, units), BF16)] * 2 + [((n * blk, width), BF16) for n in outs],
            name,
            after=after,
            weight=weight,
        )(*n2s, *cots, w_up, w_down)

    n2_near = [n2c, n2n, n2c_core, n2n_core]
    cot_near = [cotc, cotn, cotc_core, cotn_core]
    at_near = [((c, k * blk), (c, (2 + k) * blk)) for c in range(CORES) for k in range(2)]
    act_a, dpre_a, near_0, near_1 = mlp("mlp_near", n2_near, cot_near, [4, 4], at_near)
    near_1 = across("near", near_1)

    def tie(name, arrays, after):
        return list(
            pl.pallas_call(
                lambda *refs: None,
                out_shape=tuple(jax.ShapeDtypeStruct(a.shape, a.dtype) for a in arrays),
                in_specs=[pl.BlockSpec(memory_space=pl.ANY)] * (len(arrays) + len(after)),
                out_specs=tuple(pl.BlockSpec(memory_space=pl.ANY) for _ in arrays),
                input_output_aliases={i: i for i in range(len(arrays))},
                compiler_params=pltpu.CompilerParams(vmem_limit_bytes=2**20),
                name=name,
            )(*arrays, *after)
        )

    count = len(cot_far)
    slim = (blk, width // 2)
    sorted_far = call(
        lambda *refs: sort_body(count, *refs),
        [(slim, BF16)] * (2 * count) + [(small, BF16)] * count,
        "sort_far",
        after=[act_a],
        weight=0.0,
    )(*cot_far, *cap_far)
    cotn_far = [Pair(sorted_far[i : 2 * count : count]) for i in range(count)]
    cotc_far = list(sorted_far[2 * count :])
    cotn_all = cotn_far + [Pair([across("far_cotn", a) for a in p]) for p in cotn_far]
    halves = call(
        lambda *refs: halve_body(count, *refs),
        [(slim, BF16)] * (2 * count),
        "halve_n2n",
        after=[a for p in cotn_all[count:] for a in p],
        weight=0.0,
    )(*n2n_far)
    n2n_far = [Pair(halves[i::count]) for i in range(count)]
    n2n_all = n2n_far + [Pair([across("far_n2n", a) for a in p]) for p in n2n_far]
    cotc_all = cotc_far + [across("far_cotc", a) for a in cotc_far]

    tall = 4 * blk
    down_near, up_near = call(
        lambda act, dpre, *refs: near_weights_body(act, dpre, refs[:4], refs[4:8], *refs[8:]),
        [((units, width), F32), ((width, units), F32)],
        "weights_near",
        scratch=[pltpu.VMEM((tall, width), BF16)] * 2,
        after=n2n_far[0][:1],
        weight=0.0,
    )(act_a, dpre_a, *n2_near, *cot_near)


    far_at = range(CORES * (ysize - 1))
    place = lambda s: (s // (ysize - 1), s % (ysize - 1) * blk)
    act_n, dpre_n, far_n0, far_n1 = mlp(
        "mlp_far_n", n2n_all, cotn_all, [2 * (ysize - 1)] * 2,
        [(place(s), (place(s)[0], place(s)[1] + (ysize - 1) * blk)) for s in far_at],
        [down_near], 0.0,
    )
    far_n1 = across("far_n", far_n1)
    n2c_far = tie("tie_c", n2c_far, [act_n, *cotc_all[count:]])
    n2c_all = n2c_far + [across("far_n2c", a) for a in n2c_far]
    act_c, dpre_c, d_c0, hid_c0, d_c1, hid_c1 = mlp(
        "mlp_far_c", n2c_all, cotc_all, [ysize - 1] * 4,
        [((2 * c, at), (2 * c + 1, at)) for c, at in map(place, far_at)],
    )
    d_c1, hid_c1 = across("d_c", d_c1), across("hid_c", hid_c1)

    def send_back(name, joint, groups):
        if ysize == 2:
            return swap("y_" + name, joint, "tensor", tsize, CORES)
        cut = joint.reshape(groups, ysize - 1, blk, width)
        got = [swap("y_" + name, cut[:, dy - 1], "tensor", tsize, dy * CORES) for dy in others]
        return jnp.stack(got, axis=1).reshape(joint.shape)

    joint, rest = call(
        far_sum_body,
        [(((ysize - 1) * blk, width), BF16), ((3 * (ysize - 1) * blk, width), BF16)],
        "far_sum",
    )(d_c0, d_c1, far_n0, far_n1, hid_c0, hid_c1)
    d_c2 = send_back("d_c", joint, 1)
    rest = send_back("rest", rest, 3)

    cots, n2s = cotn_all + cotc_all, n2n_all + n2c_all
    count, tall = len(cots), len(cots) * blk
    part = (units // GROUP * 2, width)

    def weights(*refs):
        acts, dpres, refs = refs[:2], refs[2:4], refs[4:]
        n2s, cots, refs = refs[:count], refs[count : 2 * count], refs[2 * count :]
        weights_body(
            GROUP, acts, dpres, n2s, cots, *refs[:2], refs[2 : 2 + GROUP], *refs[2 + GROUP :]
        )

    quarters = call(
        weights,
        [(part, BF16)] * GROUP,
        "weights",
        scratch=[
            pltpu.VMEM((tall, units), BF16), pltpu.VMEM((tall, units), BF16),
            pltpu.VMEM((tall, width), BF16), pltpu.VMEM((tall, width), BF16),
            pltpu.VMEM((units, width), BF16), pltpu.VMEM((width, units), BF16),
        ],
        after=[joint, near_1],
    )(act_n, act_c, dpre_n, dpre_c, *n2s, *cots, down_near, up_near)
    quarters_got = group("mlp", quarters)
    mark = quarters[0]

    shares = tsize * dsize
    share = width // shares
    def owners(y_first):
        table = []
        for core in range(CORES):
            for first in range(ysize if y_first else 2):
                for then in range(2 if y_first else ysize):
                    y, x = (first, then) if y_first else (then, first)
                    for z in range(2):
                        for hi in range(dsize // GROUP):
                            place = (hi * GROUP + z * 2 + x) * tsize + y * CORES + core
                            table += [place] * share
        return table

    table = jnp.array([owners(True), owners(False), list(range(share)) * shares], jnp.int32)
    d_resid_c, d_qkv, d_att, d_logit, g_gain2c = call(
        lambda *refs: back_body(half, *refs),
        [
            (small, F32), ((blk, 3 * width), BF16), (small, BF16), ((blk, 1), F32), ((1, width), F32),
        ],
        "back",
        after=[mark],
        weight=20.0,
    )(
        (near_0, 0, blk), (near_1, 0, blk), d_c2, cotc, xc, attended, gate, heads, qkv, probs,
        w_out, gain2,
    )
    left, left_got, right, right_got = call(
        lambda *refs: products_body(tsize, *refs),
        [((width // 2, 2 * width), BF16)] * 4,
        "products",
    )(heads, n1, d_qkv, d_att, table)
    left_got, right_got = across("left", left_got), across("right", right_got)

    def sums_of(name, *sets, after=(), along=(), weight=1.0):
        given = [a for arrays, _ in sets for a in arrays]

        def body(*refs):
            ins, outs = list(refs[: len(given)]), list(refs[len(given) + len(along) :])
            if along:
                outs[-1][...] = refs[len(given)][...] + refs[len(given) + 1][...]
            for arrays, count in sets:
                add_split_body(len(arrays), count, *ins[: len(arrays)], *outs[:count])
                del ins[: len(arrays)], outs[:count]

        shapes = []
        for arrays, count in sets:
            rows, columns = arrays[0].shape
            shapes += [((rows // count, columns), BF16)] * count
        shapes += [(a.shape, a.dtype) for a in along[:1]]
        return call(body, shapes, name, after=after, weight=weight)(*given, *along)

    mine = sums_of(
        "mlp_1", ([quarters[0], *quarters_got], PARTS), after=[left], weight=W_MLP1
    )
    mine_got = [high("mlp", [a]) for a in mine]

    *left, right, right_got = sums_of(
        "att_1", ([left, left_got], ysize), ([right, right_got], 2), after=[mine[0], rest]
    )
    left_got = [swap("y_left", left[p], "tensor", tsize, p * CORES) for p in others]
    right_got = swap("x_right", right_got, "dp", dsize, 1)

    mixed, grad_input, sums = call(
        post_body,
        [((rows, width), BF16), ((rows, width), F32), ((8, width), F32)],
        "post",
        after=[right],
        weight=20.0,
    )(
        cap, (near_0, 1, blk), (near_0, 2, blk), (near_0, 3, blk), (near_1, 1, blk), (near_1, 2, blk),
        (near_1, 3, blk), rest,
        xc, xn, cotn, attended, gate, d_resid_c, d_qkv, d_logit, n1, w_qkv, gain1, gain2, route, g_gain2c,
        stats1,
    )

    step = 1
    while step < tsize // 2:
        sums = sums + swap("sums", sums, "tensor", tsize, step)
        step *= 2
    sums_got = swap("sums", sums, "tensor", tsize, step)

    right = sums_of("right_2", ([right, right_got], ysize), after=[sums], weight=0.0)
    right_got = [swap("y_right", right[p], "tensor", tsize, p * CORES) for p in others]
    low_rows = 2 * sums.shape[0]

    def left_body(*refs):
        *ins, a, b, kept, sent, sums_out = refs
        total = ins[0][...].astype(F32)
        for ref in ins[1:]:
            total = total + ref[...].astype(F32)
        size = kept.shape[0]
        kept[...] = total[:size].astype(BF16)
        sent[:size] = total[size:].astype(BF16)
        sent[size:] = jnp.zeros_like(sent[size:])
        sums_out[...] = to_pair(a[...] + b[...])
        sent[size:, : sums_out.shape[1]] = sums_out[...]

    size = left[0].shape[0] // 2
    left, left_got, sums = call(
        left_body,
        [((size, 2 * width), BF16), ((size + low_rows, 2 * width), BF16), ((low_rows, width), BF16)],
        "left_2",
        after=[right[0]],
        weight=0.0,
    )(left[0], *left_got, sums, sums_got)
    left_got = swap("x_left", left_got, "dp", dsize, 1)

    mine = in_order("mlp_2", mine[0], mine_got[0], lax.axis_index("dp") // GROUP, 2, [left])
    mine_got = [swap("zx_down", mine[0], "dp", dsize, 2), swap("xz_up", mine[1], "dp", dsize, 1)]

    highs = dsize // GROUP

    def join_body(*refs):
        (left, left_got, *rights), sums, outs = refs[: -2 * highs - 1], refs[-2 * highs - 1], refs[-2 * highs :]
        size = left.shape[0]
        middle = left.shape[1]
        pair = to_pair(from_pair(sums[...]) + from_pair(left_got[size:, : sums.shape[1]]))
        totals = [left[...].astype(F32) + left_got[:size].astype(F32), rights[0][...].astype(F32)]
        for ref in rights[1:]:
            totals[1] = totals[1] + ref[...].astype(F32)
        for p, out in enumerate(outs):
            for k, total in enumerate(totals):
                out[:share, k * middle : (k + 1) * middle] = total[p * share : (p + 1) * share].astype(BF16)
            out[:low_rows, 2 * middle :] = pair

    att = call(
        join_body,
        [((max(share, low_rows), 5 * width), BF16)] * (2 * highs),
        "att_3",
        after=[mine[0]],
        weight=0.0,
    )(left, left_got, right[0], *right_got, sums)
    att_got = [
        swap("z_att", att[p], "dp", dsize, p // highs * 2 + p % highs * GROUP)
        for p in range(1, 2 * highs)
    ]

    def spread(name, own, other, after):
        return call(
            spread_body, [((2 * own.shape[0], own.shape[1]), BF16)], name, after=after, weight=0.0
        )(own, other)[0]

    down_rest = spread("down_pair", mine[0], mine_got[0], att[:1])
    up_rest = spread("up_pair", mine[1], mine_got[1], [down_rest])
    down_rest = swap("zx_down", down_rest, "dp", dsize, 1)
    up_rest = swap("xz_up", up_rest, "dp", dsize, 2)
    count = rows * width * dsize * tsize

    def att_body(*refs):
        ins, outs = refs[: 2 * highs], refs[2 * highs :]
        out_qkv, out_proj, out_gain1, out_router, out_gain2, norms = outs
        total = ins[0][:share, : 4 * width].astype(F32)
        for ref in ins[1:]:
            total = total + ref[:share, : 4 * width].astype(F32)
        out_qkv[...] = total[:, : 3 * width]
        out_proj[...] = total[:, 3 * width :]
        sums = [from_pair(ref[:low_rows, 4 * width :]) for ref in ins]
        while len(sums) > 1:
            sums = [a + b for a, b in zip(sums[::2], sums[1::2])]
        for k, out in enumerate((out_gain1, out_router, out_gain2)):
            out[...] = sums[0][k : k + 1, :].reshape(width)
        norms[...] = jnp.sqrt(jnp.sum(sums[0][3:6, :], axis=-1) / count)

    g_qkv, g_proj, g_gain1, g_router, g_gain2, norms = call(
        att_body,
        [((share, 3 * width), F32), ((share, width), F32)] + [((width,), F32)] * 3 + [((3,), F32)],
        "att_4",
        weight=20.0,
    )(att[0], *att_got)

    part = mine[0].shape[0]
    g_down, g_up = call(
        lambda a0, a2, a13, b0, b1, b23, *refs: assemble_body(
            (a0, a13.at[pl.ds(0, part)], a2, a13.at[pl.ds(part, part)]),
            (b0, b1, b23.at[pl.ds(0, part)], b23.at[pl.ds(part, part)]),
            *refs,
        ),
        [((units, width), F32), ((width, units), F32)],
        "assemble",
        weight=W_LAST,
        after=[g_proj],
    )(mine[0], mine_got[0], down_rest, mine[1], mine_got[1], up_rest)

    return (
        mixed, grad_input, g_gain1, g_router, g_qkv, g_proj, g_gain2, g_up, g_down, norms,
    )


def solution(mesh):
    return jax.shard_map(
        shards,
        mesh=mesh,
        in_specs=(
            P(("dp", "tensor"), None),
            P(("dp", "tensor"), None),
            P(("dp", "tensor")),
            P(),
            P(),
            P(),
            P(),
            P(),
            P(None, "tensor"),
            P("tensor", None),
            P(("dp", "tensor"), None),
        ),
        out_specs=(
            P(("dp", "tensor"), None),
            P(("dp", "tensor"), None),
            P(),
            P(),
            P(("dp", "tensor"), None),
            P(("dp", "tensor"), None),
            P(),
            P(None, "tensor"),
            P("tensor", None),
            P(),
        ),
        check_vma=False,
    )
```

```python
import math

import jax
import jax.numpy as jnp
from jax import lax
from jax.experimental import pallas as pl
from jax.experimental.pallas import tpu as pltpu
from jax.sharding import PartitionSpec as P

HEADS = 12
HEAD_DIM = 64
PAIR = 2 * HEAD_DIM
EPSILON = 1e-06
NEGATIVE = -1000000000.0
GELU_C = math.sqrt(2.0 / math.pi)
GELU_A = 0.044715
F32 = jnp.float32
BF16 = jnp.bfloat16
VMEM_LIMIT = 24


def dot_nn(a, b):
    return lax.dot_general(a, b, (((1,), (0,)), ((), ())), preferred_element_type=F32)


def dot_nt(a, b):
    return lax.dot_general(a, b, (((1,), (1,)), ((), ())), preferred_element_type=F32)


def dot_tn(a, b):
    return lax.dot_general(a, b, (((0,), (0,)), ((), ())), preferred_element_type=F32)


def iota(shape, dim):
    return lax.broadcasted_iota(jnp.int32, shape, dim)


def row_of(ref):
    return ref[...].reshape(1, ref.shape[0])


def norm_rows(rows, gain):
    center = rows - jnp.mean(rows, axis=-1, keepdims=True)
    inverse = lax.rsqrt(jnp.mean(center * center, axis=-1, keepdims=True) + EPSILON)
    unit = center * inverse
    return unit * gain, unit, inverse


def norm_back(grad_out, unit, inverse, gain):
    scaled = grad_out * gain
    mean_grad = jnp.mean(scaled, axis=-1, keepdims=True)
    mean_cross = jnp.mean(scaled * unit, axis=-1, keepdims=True)
    grad_in = inverse * (scaled - mean_grad - unit * mean_cross)
    return grad_in, jnp.sum(grad_out * unit, axis=0, keepdims=True)


class Pair(list):
    pass


def call(body, outs, name, scratch=(), loose=(), after=(), weight=1.0, limit=VMEM_LIMIT, loose_outs=False):
    vmem = pl.BlockSpec(memory_space=pltpu.VMEM)
    anywhere = pl.BlockSpec(memory_space=pl.ANY)

    def run(*args):
        flat = []
        for a in args:
            flat += a if isinstance(a, Pair) else [a[0] if isinstance(a, tuple) else a]
        given = list({id(a): a for a in flat}.values())
        index = [[id(g) for g in given].index(id(a)) for a in flat]

        def inner(*refs):
            held = []
            for a in args:
                at = index[sum(len(h) if isinstance(h, tuple) else 1 for h in held)]
                if isinstance(a, Pair):
                    nxt = index[sum(len(h) if isinstance(h, tuple) else 1 for h in held) + 1]
                    held.append((refs[at], refs[nxt]))
                elif isinstance(a, tuple):
                    held.append(refs[at].at[pl.ds(a[1] * a[2], a[2])])
                else:
                    held.append(refs[at])
            body(*held, *refs[len(given) + len(after) :])

        spaces = [anywhere if any(index[j] == i for j in loose) else vmem for i in range(len(given))]
        return pl.pallas_call(
            inner,
            out_shape=tuple(jax.ShapeDtypeStruct(s, d) for s, d in outs),
            in_specs=spaces + [anywhere] * len(after),
            out_specs=tuple(anywhere if loose_outs else vmem for _ in outs),
            scratch_shapes=list(scratch),
            compiler_params=pltpu.CompilerParams(vmem_limit_bytes=limit * 2**20),
            cost_estimate=pl.CostEstimate(
                flops=1 + int(weight * 1e9), bytes_accessed=1, transcendentals=0
            ),
            name=name,
        )(*given, *after)

    return run


def places(cap, rows, half, blk):
    k, j = iota((rows, rows), 0), iota((rows, rows), 1)
    cap_col = jnp.sum(jnp.where(k == j, cap, 0.0), axis=1, keepdims=True)
    rank_row = jnp.sum(jnp.where(k < j, cap_col, 0.0), axis=0, keepdims=True)
    rank_col = jnp.sum(jnp.where(j < k, cap, 0.0), axis=1, keepdims=True)
    at_row = iota((1, rows), 1).astype(F32)
    at_col = iota((rows, 1), 0).astype(F32)
    dest_row = jnp.where(cap > 0.5, rank_row, blk + at_row - rank_row)
    dest_col = jnp.where(cap_col > 0.5, rank_col, blk + at_col - rank_col)
    return dest_row.astype(jnp.int32), dest_col.astype(jnp.int32)


def sorted_rows(cot, cap, blk):
    rows = cot.shape[0]
    dest_row, _ = places(row_of(cap).astype(F32), rows, rows // 2, blk)
    pick = (iota((2 * blk, rows), 0) == dest_row).astype(BF16)
    c = dot_nn(pick, cot[...]).astype(BF16)
    return c[blk:], c[:blk]


def pre_body(
    tok_far, cot_far, cap_far, lens_far, gain2_far, cot_core, cap_core,
    xc, xn, n2n, cotn, cotc, cotn_core, cotc_core, bias,
    tok, cot, cap, lens, gain2, sems,
):
    pairs = ((cap_far, cap), (tok_far, tok), (lens_far, lens), (gain2_far, gain2), (cot_far, cot))
    copies = [pltpu.make_async_copy(a, b, sems.at[i]) for i, (a, b) in enumerate(pairs)]
    for c in copies:
        c.start()
    cotn_core[...], cotc_core[...] = sorted_rows(cot_core, cap_core, xc.shape[0])
    for c in copies:
        c.wait()
    rows = tok.shape[0]
    blk = xc.shape[0]
    dest_row, _ = places(row_of(cap).astype(F32), rows, rows // 2, blk)
    pick = (iota((2 * blk, rows), 0) == dest_row).astype(BF16)
    x = dot_nn(pick, tok[...])
    xc[...] = x[:blk].astype(BF16)
    xn[...] = x[blk:].astype(BF16)
    n2n[...] = norm_rows(x[blk:], row_of(gain2))[0].astype(BF16)
    c = dot_nn(pick, cot[...]).astype(BF16)
    cotn[...] = c[blk:]
    cotc[...] = c[:blk]
    position = iota((1, rows), 1)
    crop = jnp.ones((1, rows), F32)
    end = 0
    for s in range(lens.shape[1]):
        end = end + lens[0, s]
        crop = crop + (position >= end).astype(F32)
    crop_col = jnp.sum(jnp.where(iota((blk, rows), 0) == dest_row, crop, 0.0), axis=1, keepdims=True)
    crop_row = jnp.sum(
        jnp.where(iota((blk, blk), 0) == iota((blk, blk), 1), crop_col, 0.0), axis=0, keepdims=True
    )
    bias[...] = jnp.where(crop_col == crop_row, 0.0, NEGATIVE)


def sort_body(count, *refs):
    for cot, cap, left, right, out_c in zip(*(refs[k * count : (k + 1) * count] for k in range(5))):
        rows, out_c[...] = sorted_rows(cot, cap, out_c.shape[0])
        middle = left.shape[1]
        left[...], right[...] = rows[:, :middle], rows[:, middle:]


def halve_body(count, *refs):
    for array, left, right in zip(*(refs[k * count : (k + 1) * count] for k in range(3))):
        middle = left.shape[1]
        left[...], right[...] = array[:, :middle], array[:, middle:]


def half_mask(shape, e):
    return (iota(shape, 1) < HEAD_DIM) == (e == 0)


def fore_body(
    half,
    xc, bias, gain1, router, w_qkv, w_out, gain2,
    n1, qkv, probs, heads, attended, gate, n2c, stats,
):
    blk, width = xc.shape
    x = xc[...].astype(F32)
    low = norm_rows(x, row_of(gain1))[0].astype(BF16)
    n1[...] = low
    logit = jnp.sum(low.astype(F32) * row_of(router), axis=-1, keepdims=True)
    gated = jnp.where(iota((blk, 1), 0) < half, jax.nn.sigmoid(logit), 0.0)
    gate[...] = gated
    qkv[...] = dot_nn(low, w_qkv[...]).astype(BF16)
    scale = 1.0 / math.sqrt(HEAD_DIM)
    for pair in range(HEADS // 2):
        at = pair * PAIR
        q = qkv[:, at : at + PAIR]
        k = qkv[:, width + at : width + at + PAIR]
        v = qkv[:, 2 * width + at : 2 * width + at + PAIR]
        total = None
        for e in range(2):
            mask = half_mask((blk, PAIR), e)
            zero = jnp.zeros_like(q)
            scores = dot_nt(jnp.where(mask, q, zero), k) * scale + bias[...]
            exponent = jnp.exp(scores - jnp.max(scores, axis=-1, keepdims=True))
            prob = (exponent / jnp.sum(exponent, axis=-1, keepdims=True)).astype(BF16)
            probs[2 * pair + e] = prob
            part = dot_nn(prob, jnp.where(mask, v, zero))
            total = part if total is None else total + part
        heads[:, at : at + PAIR] = total.astype(BF16)
    att = dot_nn(heads[...], w_out[...])
    attended[...] = att
    branch = gated * att
    resid = x + branch
    n2c[...] = norm_rows(resid, row_of(gain2))[0].astype(BF16)
    stats[0:1, :] = jnp.sum(resid * resid, axis=0, keepdims=True)
    stats[1:2, :] = jnp.sum(branch * branch, axis=0, keepdims=True)


def mlp_body(blk, outs_at, n2s, cots, w_up, w_down, act, dpre, *outs):
    for s, (n2, cot) in enumerate(zip(n2s, cots)):
        rows = pl.ds(s * blk, blk)
        pre = dot_nn(whole(n2), w_up[...])
        d_act = dot_nt(whole(cot), w_down[...])
        square = pre * pre
        t = jnp.tanh(pre * (GELU_C + GELU_C * GELU_A * square))
        half_up = 0.5 + 0.5 * t
        slope = half_up + pre * (0.5 - 0.5 * t * t) * (GELU_C + 3.0 * GELU_C * GELU_A * square)
        a = (pre * half_up).astype(BF16)
        d = (d_act * slope).astype(BF16)
        act[rows, :] = a
        dpre[rows, :] = d
        (d_out, d_at), (h_out, h_at) = outs_at[s]
        outs[d_out][pl.ds(d_at, blk), :] = dot_nt(d, w_up[...]).astype(BF16)
        outs[h_out][pl.ds(h_at, blk), :] = dot_nn(a, w_down[...]).astype(BF16)


def copy_rows(sources, target):
    at = 0
    for ref in sources:
        rows = whole(ref)
        target[at : at + rows.shape[0]] = rows
        at += rows.shape[0]


def whole(ref):
    if isinstance(ref, tuple):
        return jnp.concatenate([r[...] for r in ref], axis=1)
    return ref[...]


def near_weights_body(act, dpre, n2s, cots, down, up, n2, cot):
    copy_rows(cots, cot)
    copy_rows(n2s, n2)
    down[...] = dot_tn(act[...], cot[...])
    up[...] = dot_tn(n2[...], dpre[...])


def weights_body(quarters, acts, dpres, n2s, cots, down, up, outs, act, dpre, n2, cot, total, grad_up):
    units = down.shape[0]
    part = units // quarters
    copy_rows(acts, act)
    copy_rows(cots, cot)
    total[...] = (down[...] + dot_tn(act[...], cot[...])).astype(BF16)
    copy_rows(dpres, dpre)
    copy_rows(n2s, n2)
    grad_up[...] = (up[...] + dot_tn(n2[...], dpre[...])).astype(BF16)
    lo = lax.rem(lax.axis_index("dp"), quarters)
    down_keep, down_send, up_keep, up_send = outs
    blocks = grad_up.shape[0] // units
    for p in range(quarters):
        first = lax.bitwise_xor(lo, p) * part
        target, at = (down_keep, down_send)[p % 2], p // 2 * part
        target[at : at + part] = total[pl.ds(pl.multiple_of(first, 16), part), :]
        target, at = (up_keep, up_send)[p // 2], p % 2 * part
        for k in range(blocks):
            row = pl.multiple_of(first * blocks + k * part, 16)
            target[at : at + part, k * units : (k + 1) * units] = grad_up[pl.ds(row, part), :]


def halves_body(down, down_got, up, up_got, kept, down_send, up_send):
    size = down_send.shape[0]
    a = down[...].astype(F32) + down_got[...].astype(F32)
    b = up[...].astype(F32) + up_got[...].astype(F32)
    kept[:size] = a[:size]
    kept[size:] = b[:size]
    down_send[...] = a[size:].astype(BF16)
    up_send[...] = b[size:].astype(BF16)


def own_body(kept, down_got, up_got, mine):
    size = down_got.shape[0]
    mine[:size] = (kept[:size] + down_got[...].astype(F32)).astype(BF16)
    mine[size:] = (kept[size:] + up_got[...].astype(F32)).astype(BF16)


def far_sum_body(d_c0, d_c1, n0, n1, h0, h1, joint, rest):
    def both(a, b):
        return (a[...].astype(F32) + b[...].astype(F32)).astype(BF16)

    joint[...] = both(d_c0, d_c1)
    size = n0.shape[0]
    rest[:size] = both(n0, n1)
    rest[size:] = both(h0, h1)


def add_body(count, *refs):
    total = refs[0][...].astype(F32)
    for ref in refs[1:count]:
        total = total + ref[...].astype(F32)
    refs[count][...] = total.astype(refs[count].dtype)


def spread_body(a, b, a_got, b_got, *outs):
    for own, other, both in ((a, a_got, outs[0]), (b, b_got, outs[1])):
        size = own.shape[0]
        both[:size] = own[...]
        both[size:] = other[...]


def assemble_body(long, short, down_far, up_far, mark, down, up, sems):
    units = up.shape[1]
    part = units // len(long)
    blocks = up.shape[0] // units
    lo = lax.rem(lax.axis_index("dp"), len(long))
    firsts = [lax.bitwise_xor(lo, p) * part for p in range(len(long))]
    for first, rows in zip(firsts, long):
        down[pl.ds(pl.multiple_of(first, 8), part), :] = rows[:part].astype(F32)
    down_copy = pltpu.make_async_copy(down, down_far, sems.at[0])
    down_copy.start()
    for first, *pieces in zip(firsts, long, short):
        offset = 0
        for rows in (pieces[0][part:].astype(F32), pieces[1][...].astype(F32)):
            for k in range(blocks):
                at = pl.multiple_of(first * blocks + k * part + offset, 8)
                up[pl.ds(at, rows.shape[0]), :] = rows[:, k * units : (k + 1) * units]
            offset += rows.shape[0]
    up_copy = pltpu.make_async_copy(up, up_far, sems.at[1])
    up_copy.start()
    down_copy.wait()
    up_copy.wait()


def back_body(
    half,
    d_n2_0, d_n2_1, d_n2_2, cc, xc, attended, gate, heads, qkv, probs, w_out, gain2,
    d_resid_out, d_qkv, d_att_out, d_logit_out, g_gain2,
):
    blk, width = xc.shape
    scale = 1.0 / math.sqrt(HEAD_DIM)
    gated = gate[...]
    att = attended[...]
    resid = xc[...].astype(F32) + gated * att
    _, unit2, inverse2 = norm_rows(resid, row_of(gain2))
    d_n2 = d_n2_0[...].astype(F32) + d_n2_1[...].astype(F32)
    for at in range(0, d_n2_2.shape[0], blk):
        d_n2 = d_n2 + d_n2_2[at : at + blk].astype(F32)
    back2, g_gain2[...] = norm_back(d_n2, unit2, inverse2, row_of(gain2))
    d_resid = cc[...].astype(F32) + back2
    d_resid_out[...] = d_resid
    d_att = (d_resid * gated).astype(BF16)
    keep = (iota((blk, 1), 0) < half).astype(F32)
    d_gate = keep * jnp.sum(d_resid * att, axis=-1, keepdims=True)
    d_logit_out[...] = d_gate * gated * (1.0 - gated)
    d_att_out[...] = d_att
    d_heads = dot_nt(d_att, w_out[...]).astype(BF16)
    for pair in range(HEADS // 2):
        at = pair * PAIR
        q = qkv[:, at : at + PAIR]
        k = qkv[:, width + at : width + at + PAIR]
        v = qkv[:, 2 * width + at : 2 * width + at + PAIR]
        d_o = d_heads[:, at : at + PAIR]
        zero = jnp.zeros_like(q)
        d_q = d_k = d_v = 0.0
        for e in range(2):
            mask = half_mask((blk, PAIR), e)
            d_oe = jnp.where(mask, d_o, zero)
            prob = probs[2 * pair + e]
            prob_f = prob.astype(F32)
            d_prob = dot_nt(d_oe, v)
            d_score = (
                prob_f * (d_prob - jnp.sum(prob_f * d_prob, axis=-1, keepdims=True))
            ).astype(BF16)
            d_v = d_v + dot_tn(prob, d_oe)
            d_q = d_q + dot_nn(d_score, jnp.where(mask, k, zero))
            d_k = d_k + dot_tn(d_score, jnp.where(mask, q, zero))
        d_qkv[:, at : at + PAIR] = (d_q * scale).astype(BF16)
        d_qkv[:, width + at : width + at + PAIR] = (d_k * scale).astype(BF16)
        d_qkv[:, 2 * width + at : 2 * width + at + PAIR] = d_v.astype(BF16)


def products_body(tsize, heads, n1, d_qkv, d_att, table, *outs):
    width = n1.shape[1]
    me = lax.axis_index("dp") * tsize + lax.axis_index("tensor")
    share = width // (tsize * lax.axis_size("dp"))
    mid = outs[0].shape[0]
    for side in range(2):
        source = lax.bitwise_xor(table[side : side + 1, :], me) * share + table[2:3, :]
        order = (iota((width, width), 0) == source).astype(BF16)
        low = dot_nn(n1[...], order).astype(BF16)
        keep, send = outs[2 * side : 2 * side + 2]
        for k in range(2):
            at = k * width
            if side and k:
                product = dot_tn(dot_nn(heads[...], order).astype(BF16), d_att[...])
            else:
                column = (2 * side + k) * width
                product = dot_tn(low, d_qkv[:, column : column + width])
            product = product.astype(BF16)
            keep[:, at : at + width] = product[:mid]
            send[:, at : at + width] = product[mid:]


def to_pair(sums):
    top = sums.astype(BF16)
    return jnp.concatenate([top, (sums - top.astype(F32)).astype(BF16)], axis=0)


def fold_pair(sums):
    top = sums.astype(BF16).astype(F32)
    third = sums.shape[1] // 3
    both = [top, sums - top]
    blocks = [jnp.concatenate([a[:, k * third : (k + 1) * third] for a in both], axis=1) for k in range(3)]
    return jnp.concatenate(blocks, axis=0).astype(BF16)


def unfold_pair(folded):
    rows, third = folded.shape[0] // 3, folded.shape[1] // 2
    both = folded[:, :third].astype(F32) + folded[:, third:].astype(F32)
    return jnp.concatenate([both[k * rows : (k + 1) * rows] for k in range(3)], axis=1)


def from_pair(pair):
    size = pair.shape[0] // 2
    return pair[:size].astype(F32) + pair[size:].astype(F32)


def add_split_body(count, pieces, *refs):
    total = refs[0][...].astype(F32)
    for ref in refs[1:count]:
        total = total + ref[...].astype(F32)
    size = total.shape[0] // pieces
    for p in range(pieces):
        refs[count + p][...] = total[p * size : (p + 1) * size].astype(refs[count + p].dtype)


def put_back(pick, rows):
    top = rows.astype(BF16)
    rest = (rows - top.astype(F32)).astype(BF16)
    return dot_nn(pick, top) + dot_nn(pick, rest)


def post_body(
    cap, d_n0, hid_c0, hid_n0, d_nx, hid_c1, hid_n1, rest,
    xc, xn, cn, attended, gate, d_resid_c, d_qkv, d_logit, n1, w_qkv, gain1, gain2, router, g_gain2c, stats1,
    mixed, grad_in, sums,
):
    rows = mixed.shape[0]
    blk = xc.shape[0]
    _, dest_col = places(row_of(cap).astype(F32), rows, rows // 2, blk)
    pick_c = (iota((rows, blk), 1) == dest_col).astype(BF16)
    pick_n = (iota((rows, blk), 1) + blk == dest_col).astype(BF16)
    x_c, x_n = xc[...].astype(F32), xn[...].astype(F32)

    d_n1 = dot_nt(d_qkv[...], w_qkv[...]) + d_logit[...] * row_of(router)
    _, unit1, inverse1 = norm_rows(x_c, row_of(gain1))
    back1, g_gain1 = norm_back(d_n1, unit1, inverse1, row_of(gain1))
    grad_c = d_resid_c[...] + back1

    def summed(first, second, others, start, stop):
        total = first[...].astype(F32) + second[...].astype(F32)
        for o in range(start, stop, blk):
            total = total + others[o : o + blk].astype(F32)
        return total

    third = rest.shape[0] // 3
    d_n2n = summed(d_n0, d_nx, rest, 0, third)
    h_n = summed(hid_n0, hid_n1, rest, third, 2 * third)
    h_c = summed(hid_c0, hid_c1, rest, 2 * third, 3 * third)
    mix_c = (x_c + gate[...] * attended[...] + h_c).astype(BF16)
    mix_n = (x_n + h_n).astype(BF16)
    mixed[...] = (dot_nn(pick_c, mix_c) + dot_nn(pick_n, mix_n)).astype(BF16)
    _, unit, inverse = norm_rows(x_n, row_of(gain2))
    back, g_gain2n = norm_back(d_n2n, unit, inverse, row_of(gain2))
    d_resid_n = cn[...].astype(F32) + back
    grad_in[...] = put_back(pick_c, grad_c) + put_back(pick_n, d_resid_n)

    def over_rows(a):
        return jnp.sum(a, axis=0, keepdims=True)

    sums[...] = jnp.zeros_like(sums)
    sums[0:1, :] = g_gain1
    sums[1:2, :] = over_rows(d_logit[...] * n1[...].astype(F32))
    sums[2:3, :] = g_gain2c[...] + g_gain2n
    sums[3:4, :] = stats1[0:1, :] + over_rows(x_n * x_n)
    sums[4:5, :] = stats1[1:2, :]
    sums[5:6, :] = over_rows(h_c * h_c) + over_rows(h_n * h_n)


CORES = 2
GROUP = 4
PARTS = 1
W_MLP1 = 10.0
W_MLP2 = 0.0
W_LAST = 5.0
W_ATT4 = 20.0


def swap(name, array, axis, size, bits):
    with jax.named_scope(name):
        return lax.ppermute(array, axis, [(t, t ^ bits) for t in range(size)])


def add(name, arrays, after=(), weight=1.0):
    return call(
        lambda *refs: add_body(len(arrays), *refs),
        [(arrays[0].shape, BF16)],
        name,
        after=after,
        weight=weight,
    )(*arrays)[0]


def in_order(name, own, others, place, cut, after):
    if len(others) > 1:
        held = jnp.stack([own, *others])
        own, *others = [
            lax.dynamic_index_in_dim(held, place ^ at, 0, keepdims=False) for at in range(len(held))
        ]

    def body(*refs):
        total = refs[0][...].astype(F32)
        for ref in refs[1:-2]:
            total = total + ref[...].astype(F32)
        refs[-2][...] = total[:cut].astype(BF16)
        refs[-1][...] = total[cut:].astype(BF16)

    rows, columns = own.shape
    return call(
        body, [((cut, columns), BF16), ((rows - cut, columns), BF16)], name, after=after, weight=W_MLP2
    )(own, *others)


def shards(
    tokens, lengths, capacity, norm1_gain, router, w_qkv, w_out, norm2_gain, w_up, w_down, cotangent
):
    rows, width = tokens.shape
    half = rows // 2
    blk = -(-half // 16) * 16
    units = w_up.shape[1]
    tsize, dsize = lax.axis_size("tensor"), lax.axis_size("dp")
    ysize = tsize // CORES
    others = range(1, ysize)
    cap, gain1, gain2, route = capacity, norm1_gain, norm2_gain, router
    small = (blk, width)

    def far(name, array):
        return [swap("y_" + name, array, "tensor", tsize, dy * CORES) for dy in others]

    def across(name, array):
        return swap("core_" + name, array, "tensor", tsize, 1)

    cap_far, cot_far = far("cap", cap), far("cot", cotangent)
    xc, xn, n2n, cotn, cotc, cotn_core, cotc_core, bias = call(
        pre_body,
        [(small, BF16)] * 7 + [((blk, blk), F32)],
        "pre",
        scratch=[
            pltpu.VMEM(tokens.shape, BF16), pltpu.VMEM(cotangent.shape, BF16), pltpu.VMEM(cap.shape, jnp.int32),
            pltpu.SMEM(lengths.shape, jnp.int32), pltpu.VMEM(gain2.shape, F32), pltpu.SemaphoreType.DMA((5,)),
        ],
        loose=range(5),
        after=cap_far,
        weight=20.0,
    )(tokens, cotangent, cap, lengths, gain2, across("cot", cotangent), across("cap", cap))

    def group(name, pieces):
        return [swap("xz_" + name, pieces[p], "dp", dsize, p) for p in range(1, GROUP)]

    def high(name, pieces):
        return [
            swap("zz_" + name, pieces[p % len(pieces)], "dp", dsize, p * GROUP)
            for p in range(1, dsize // GROUP)
        ]

    n2n_far, n2n_core = far("n2n", n2n), across("n2n", n2n)

    n1, qkv, probs, heads, attended, gate, n2c, stats1 = call(
        lambda *refs: fore_body(half, *refs),
        [
            (small, BF16), ((blk, 3 * width), BF16), ((HEADS, blk, blk), BF16), (small, BF16),
            (small, F32), ((blk, 1), F32), (small, BF16), ((2, width), F32),
        ],
        "fore",
    )(xc, bias, gain1, route, w_qkv, w_out, gain2)

    n2c_far, n2c_core = far("n2c", n2c), across("n2c", n2c)

    def mlp(name, n2s, cots, outs, outs_at, after=(), weight=1.0):
        tall = blk * len(outs_at)
        count = len(n2s)
        return call(
            lambda *refs: mlp_body(
                blk, outs_at, refs[:count], refs[count : 2 * count], *refs[2 * count :]
            ),
            [((tall, units), BF16)] * 2 + [((n * blk, width), BF16) for n in outs],
            name,
            after=after,
            weight=weight,
        )(*n2s, *cots, w_up, w_down)

    n2_near = [n2c, n2n, n2c_core, n2n_core]
    cot_near = [cotc, cotn, cotc_core, cotn_core]
    at_near = [((c, k * blk), (c, (2 + k) * blk)) for c in range(CORES) for k in range(2)]
    act_a, dpre_a, near_0, near_1 = mlp("mlp_near", n2_near, cot_near, [4, 4], at_near)
    near_1 = across("near", near_1)

    def tie(name, arrays, after):
        return list(
            pl.pallas_call(
                lambda *refs: None,
                out_shape=tuple(jax.ShapeDtypeStruct(a.shape, a.dtype) for a in arrays),
                in_specs=[pl.BlockSpec(memory_space=pl.ANY)] * (len(arrays) + len(after)),
                out_specs=tuple(pl.BlockSpec(memory_space=pl.ANY) for _ in arrays),
                input_output_aliases={i: i for i in range(len(arrays))},
                compiler_params=pltpu.CompilerParams(vmem_limit_bytes=2**20),
                name=name,
            )(*arrays, *after)
        )

    count = len(cot_far)
    slim = (blk, width // 2)
    sorted_far = call(
        lambda *refs: sort_body(count, *refs),
        [(slim, BF16)] * (2 * count) + [(small, BF16)] * count,
        "sort_far",
        after=[act_a],
        weight=0.0,
    )(*cot_far, *cap_far)
    cotn_far = [Pair(sorted_far[i : 2 * count : count]) for i in range(count)]
    cotc_far = list(sorted_far[2 * count :])
    cotn_all = cotn_far + [Pair([across("far_cotn", a) for a in p]) for p in cotn_far]
    halves = call(
        lambda *refs: halve_body(count, *refs),
        [(slim, BF16)] * (2 * count),
        "halve_n2n",
        after=[a for p in cotn_all[count:] for a in p],
        weight=0.0,
    )(*n2n_far)
    n2n_far = [Pair(halves[i::count]) for i in range(count)]
    n2n_all = n2n_far + [Pair([across("far_n2n", a) for a in p]) for p in n2n_far]
    cotc_all = cotc_far + [across("far_cotc", a) for a in cotc_far]

    tall = 4 * blk
    down_near, up_near = call(
        lambda act, dpre, *refs: near_weights_body(act, dpre, refs[:4], refs[4:8], *refs[8:]),
        [((units, width), F32), ((width, units), F32)],
        "weights_near",
        scratch=[pltpu.VMEM((tall, width), BF16)] * 2,
        after=n2n_far[0][:1],
        weight=0.0,
    )(act_a, dpre_a, *n2_near, *cot_near)


    far_at = range(CORES * (ysize - 1))
    place = lambda s: (s // (ysize - 1), s % (ysize - 1) * blk)
    act_n, dpre_n, far_n0, far_n1 = mlp(
        "mlp_far_n", n2n_all, cotn_all, [2 * (ysize - 1)] * 2,
        [(place(s), (place(s)[0], place(s)[1] + (ysize - 1) * blk)) for s in far_at],
        [down_near], 0.0,
    )
    far_n1 = across("far_n", far_n1)
    n2c_far = tie("tie_c", n2c_far, [act_n, *cotc_all[count:]])
    n2c_all = n2c_far + [across("far_n2c", a) for a in n2c_far]
    act_c, dpre_c, d_c0, hid_c0, d_c1, hid_c1 = mlp(
        "mlp_far_c", n2c_all, cotc_all, [ysize - 1] * 4,
        [((2 * c, at), (2 * c + 1, at)) for c, at in map(place, far_at)],
    )
    d_c1, hid_c1 = across("d_c", d_c1), across("hid_c", hid_c1)

    def send_back(name, joint, groups):
        if ysize == 2:
            return swap("y_" + name, joint, "tensor", tsize, CORES)
        cut = joint.reshape(groups, ysize - 1, blk, width)
        got = [swap("y_" + name, cut[:, dy - 1], "tensor", tsize, dy * CORES) for dy in others]
        return jnp.stack(got, axis=1).reshape(joint.shape)

    cots, n2s = cotn_all + cotc_all, n2n_all + n2c_all
    count, tall = len(cots), len(cots) * blk
    part = units // GROUP

    def weights(*refs):
        acts, dpres, refs = refs[:2], refs[2:4], refs[4:]
        n2s, cots, refs = refs[:count], refs[count : 2 * count], refs[2 * count :]
        weights_body(
            GROUP, acts, dpres, n2s, cots, *refs[:2], refs[2:6], *refs[6:]
        )

    down_keep, down_got, up_keep, up_got = call(
        weights,
        [((2 * part, width), BF16)] * 4,
        "weights",
        scratch=[
            pltpu.VMEM((tall, units), BF16), pltpu.VMEM((tall, units), BF16),
            pltpu.VMEM((tall, width), BF16), pltpu.VMEM((tall, width), BF16),
            pltpu.VMEM((units, width), BF16), pltpu.VMEM((width, units), BF16),
        ],
        after=[],
    )(act_n, act_c, dpre_n, dpre_c, *n2s, *cots, down_near, up_near)
    mark = down_keep
    down_got = swap("xz_down", down_got, "dp", dsize, 1)
    up_got = swap("zx_up", up_got, "dp", dsize, 2)
    joint, rest = call(
        far_sum_body,
        [(((ysize - 1) * blk, width), BF16), ((3 * (ysize - 1) * blk, width), BF16)],
        "far_sum",
        after=[mark],
    )(d_c0, d_c1, far_n0, far_n1, hid_c0, hid_c1)
    d_c2 = send_back("d_c", joint, 1)
    rest = send_back("rest", rest, 3)

    mark = joint

    shares = tsize * dsize
    share = width // shares
    def owners(y_first):
        table = []
        for core in range(CORES):
            for first in range(ysize if y_first else 2):
                for then in range(2 if y_first else ysize):
                    y, x = (first, then) if y_first else (then, first)
                    for z in range(2):
                        for hi in range(dsize // GROUP):
                            place = (hi * GROUP + z * 2 + x) * tsize + y * CORES + core
                            table += [place] * share
        return table

    table = jnp.array([owners(True), owners(False), list(range(share)) * shares], jnp.int32)
    d_resid_c, d_qkv, d_att, d_logit, g_gain2c = call(
        lambda *refs: back_body(half, *refs),
        [
            (small, F32), ((blk, 3 * width), BF16), (small, BF16), ((blk, 1), F32), ((1, width), F32),
        ],
        "back",
        after=[mark],
        weight=20.0,
    )(
        (near_0, 0, blk), (near_1, 0, blk), d_c2, cotc, xc, attended, gate, heads, qkv, probs,
        w_out, gain2,
    )
    kept, down_got, up_got = call(
        halves_body,
        [((2 * part, width), F32), ((part, width), BF16), ((part, width), BF16)],
        "mlp_0",
        after=[d_resid_c],
        weight=0.0,
    )(down_keep, down_got, up_keep, up_got)
    mark = kept
    down_got = swap("xz_down", down_got, "dp", dsize, 2)
    up_got = swap("zx_up", up_got, "dp", dsize, 1)

    left, left_got, right, right_got = call(
        lambda *refs: products_body(tsize, *refs),
        [((width // 2, 2 * width), BF16)] * 4,
        "products",
        after=[mark],
    )(heads, n1, d_qkv, d_att, table)
    left_got, right_got = across("left", left_got), across("right", right_got)

    def sums_of(name, *sets, after=(), along=(), weight=1.0):
        given = [a for arrays, _ in sets for a in arrays]

        def body(*refs):
            ins, outs = list(refs[: len(given)]), list(refs[len(given) + len(along) :])
            if along:
                outs[-1][...] = refs[len(given)][...] + refs[len(given) + 1][...]
            for arrays, count in sets:
                add_split_body(len(arrays), count, *ins[: len(arrays)], *outs[:count])
                del ins[: len(arrays)], outs[:count]

        shapes = []
        for arrays, count in sets:
            rows, columns = arrays[0].shape
            shapes += [((rows // count, columns), BF16)] * count
        shapes += [(a.shape, a.dtype) for a in along[:1]]
        return call(body, shapes, name, after=after, weight=weight)(*given, *along)

    mine = call(
        own_body, [((2 * part, width), BF16)], "mlp_1", after=[left], weight=W_MLP1
    )(kept, down_got, up_got)
    mine_got = [high("mlp", mine)]

    *left, right, right_got = sums_of(
        "att_1", ([left, left_got], ysize), ([right, right_got], 2), after=[mine[0], rest]
    )
    left_got = [swap("y_left", left[p], "tensor", tsize, p * CORES) for p in others]
    right_got = swap("x_right", right_got, "dp", dsize, 1)

    mixed, grad_input, sums = call(
        post_body,
        [((rows, width), BF16), ((rows, width), F32), ((8, width), F32)],
        "post",
        after=[right],
        weight=20.0,
    )(
        cap, (near_0, 1, blk), (near_0, 2, blk), (near_0, 3, blk), (near_1, 1, blk), (near_1, 2, blk),
        (near_1, 3, blk), rest,
        xc, xn, cotn, attended, gate, d_resid_c, d_qkv, d_logit, n1, w_qkv, gain1, gain2, route, g_gain2c,
        stats1,
    )

    step = 1
    while step < tsize // 2:
        sums = sums + swap("sums", sums, "tensor", tsize, step)
        step *= 2
    sums_got = swap("sums", sums, "tensor", tsize, step)

    right = sums_of("right_2", ([right, right_got], ysize), after=[sums], weight=0.0)
    right_got = [swap("y_right", right[p], "tensor", tsize, p * CORES) for p in others]
    low_rows = 2 * sums.shape[0]

    def left_body(*refs):
        *ins, a, b, kept, sent, sums_out = refs
        total = ins[0][...].astype(F32)
        for ref in ins[1:]:
            total = total + ref[...].astype(F32)
        size = kept.shape[0]
        kept[...] = total[:size].astype(BF16)
        sent[:size] = total[size:].astype(BF16)
        sent[size:] = jnp.zeros_like(sent[size:])
        sums_out[...] = to_pair(a[...] + b[...])
        sent[size:, : sums_out.shape[1]] = sums_out[...]

    size = left[0].shape[0] // 2
    left, left_got, sums = call(
        left_body,
        [((size, 2 * width), BF16), ((size + low_rows, 2 * width), BF16), ((low_rows, width), BF16)],
        "left_2",
        after=[right[0]],
        weight=0.0,
    )(left[0], *left_got, sums, sums_got)
    left_got = swap("x_left", left_got, "dp", dsize, 1)

    cut = 2 * part * 2 // 3
    mine = in_order("mlp_2", mine[0], mine_got[0], lax.axis_index("dp") // GROUP, cut, [left])
    mine_got = [swap("zx_long", mine[0], "dp", dsize, 2), swap("xz_short", mine[1], "dp", dsize, 1)]

    highs = dsize // GROUP

    def join_body(*refs):
        (left, left_got, *rights), sums, outs = refs[: -2 * highs - 1], refs[-2 * highs - 1], refs[-2 * highs :]
        size = left.shape[0]
        middle = left.shape[1]
        pair = fold_pair(from_pair(sums[...]) + from_pair(left_got[size:, : sums.shape[1]]))
        totals = [left[...].astype(F32) + left_got[:size].astype(F32), rights[0][...].astype(F32)]
        for ref in rights[1:]:
            totals[1] = totals[1] + ref[...].astype(F32)
        for p, out in enumerate(outs):
            for k, total in enumerate(totals):
                out[:share, k * middle : (k + 1) * middle] = total[p * share : (p + 1) * share].astype(BF16)
            out[: pair.shape[0], 2 * middle :] = pair

    att = call(
        join_body,
        [((max(share, low_rows * 3 // 2), 4 * width + width * 2 // 3), BF16)] * (2 * highs),
        "att_3",
        after=[mine[0]],
        weight=20.0,
    )(left, left_got, right[0], *right_got, sums)
    long_rest, short_rest = call(
        spread_body,
        [((2 * a.shape[0], width), BF16) for a in mine],
        "pairs",
        after=att[:1],
        weight=0.0,
    )(*mine, *mine_got)
    att = [att[0]] + tie("tie_att", att[1:], [long_rest])
    att_got = [
        swap("z_att", att[p], "dp", dsize, p // highs * 2 + p % highs * GROUP)
        for p in range(1, 2 * highs)
    ]
    long_rest = swap("zx_long", long_rest, "dp", dsize, 1)
    short_rest = swap("xz_short", short_rest, "dp", dsize, 2)

    g_down, g_up, mark = call(
        lambda a0, a2, a13, b0, b1, b23, *refs: assemble_body(
            (a0, a13.at[pl.ds(0, cut)], a2, a13.at[pl.ds(cut, cut)]),
            (b0, b1, b23.at[pl.ds(0, 2 * part - cut)], b23.at[pl.ds(2 * part - cut, 2 * part - cut)]),
            *refs,
        ),
        [((units, width), F32), ((width, units), F32), ((8, 128), F32)],
        "assemble",
        scratch=[
            pltpu.VMEM((units, width), F32), pltpu.VMEM((width, units), F32), pltpu.SemaphoreType.DMA((2,)),
        ],
        weight=W_LAST,
        loose_outs=True,
        after=att[1:2],
    )(mine[0], mine_got[0], long_rest, mine[1], mine_got[1], short_rest)

    count = rows * width * dsize * tsize

    def att_body(*refs):
        ins, outs = refs[: 2 * highs], refs[2 * highs :]
        out_qkv, out_proj, out_gain1, out_router, out_gain2, norms = outs
        total = ins[0][:share, : 4 * width].astype(F32)
        for ref in ins[1:]:
            total = total + ref[:share, : 4 * width].astype(F32)
        out_qkv[...] = total[:, : 3 * width]
        out_proj[...] = total[:, 3 * width :]
        sums = [unfold_pair(ref[: low_rows * 3 // 2, 4 * width :]) for ref in ins]
        while len(sums) > 1:
            sums = [a + b for a, b in zip(sums[::2], sums[1::2])]
        for k, out in enumerate((out_gain1, out_router, out_gain2)):
            out[...] = sums[0][k : k + 1, :].reshape(width)
        norms[...] = jnp.sqrt(jnp.sum(sums[0][3:6, :], axis=-1) / count)

    g_qkv, g_proj, g_gain1, g_router, g_gain2, norms = call(
        att_body,
        [((share, 3 * width), F32), ((share, width), F32)] + [((width,), F32)] * 3 + [((3,), F32)],
        "att_4",
        weight=W_ATT4,
        after=[mark],
    )(att[0], *att_got)

    return (
        mixed, grad_input, g_gain1, g_router, g_qkv, g_proj, g_gain2, g_up, g_down, norms,
    )


def solution(mesh):
    return jax.shard_map(
        shards,
        mesh=mesh,
        in_specs=(
            P(("dp", "tensor"), None),
            P(("dp", "tensor"), None),
            P(("dp", "tensor")),
            P(),
            P(),
            P(),
            P(),
            P(),
            P(None, "tensor"),
            P("tensor", None),
            P(("dp", "tensor"), None),
        ),
        out_specs=(
            P(("dp", "tensor"), None),
            P(("dp", "tensor"), None),
            P(),
            P(),
            P(("dp", "tensor"), None),
            P(("dp", "tensor"), None),
            P(),
            P(None, "tensor"),
            P("tensor", None),
            P(),
        ),
        check_vma=False,
    )
```

```python
import math

import jax
import jax.numpy as jnp
from jax import lax
from jax.experimental import pallas as pl
from jax.experimental.pallas import tpu as pltpu
from jax.sharding import PartitionSpec as P

HEADS = 12
HEAD_DIM = 64
PAIR = 2 * HEAD_DIM
EPSILON = 1e-06
NEGATIVE = -1000000000.0
GELU_C = math.sqrt(2.0 / math.pi)
GELU_A = 0.044715
F32 = jnp.float32
BF16 = jnp.bfloat16
VMEM_LIMIT = 24


def dot_nn(a, b):
    return lax.dot_general(a, b, (((1,), (0,)), ((), ())), preferred_element_type=F32)


def dot_nt(a, b):
    return lax.dot_general(a, b, (((1,), (1,)), ((), ())), preferred_element_type=F32)


def dot_tn(a, b):
    return lax.dot_general(a, b, (((0,), (0,)), ((), ())), preferred_element_type=F32)


def iota(shape, dim):
    return lax.broadcasted_iota(jnp.int32, shape, dim)


def row_of(ref):
    return ref[...].reshape(1, ref.shape[0])


def norm_rows(rows, gain):
    center = rows - jnp.mean(rows, axis=-1, keepdims=True)
    inverse = lax.rsqrt(jnp.mean(center * center, axis=-1, keepdims=True) + EPSILON)
    unit = center * inverse
    return unit * gain, unit, inverse


def norm_back(grad_out, unit, inverse, gain):
    scaled = grad_out * gain
    mean_grad = jnp.mean(scaled, axis=-1, keepdims=True)
    mean_cross = jnp.mean(scaled * unit, axis=-1, keepdims=True)
    grad_in = inverse * (scaled - mean_grad - unit * mean_cross)
    return grad_in, jnp.sum(grad_out * unit, axis=0, keepdims=True)


class Pair(list):
    pass


def call(body, outs, name, scratch=(), loose=(), after=(), weight=1.0, limit=VMEM_LIMIT, loose_outs=False):
    vmem = pl.BlockSpec(memory_space=pltpu.VMEM)
    anywhere = pl.BlockSpec(memory_space=pl.ANY)

    def run(*args):
        flat = []
        for a in args:
            flat += a if isinstance(a, Pair) else [a[0] if isinstance(a, tuple) else a]
        given = list({id(a): a for a in flat}.values())
        index = [[id(g) for g in given].index(id(a)) for a in flat]

        def inner(*refs):
            held = []
            for a in args:
                at = index[sum(len(h) if isinstance(h, tuple) else 1 for h in held)]
                if isinstance(a, Pair):
                    nxt = index[sum(len(h) if isinstance(h, tuple) else 1 for h in held) + 1]
                    held.append((refs[at], refs[nxt]))
                elif isinstance(a, tuple):
                    held.append(refs[at].at[pl.ds(a[1] * a[2], a[2])])
                else:
                    held.append(refs[at])
            body(*held, *refs[len(given) + len(after) :])

        spaces = [anywhere if any(index[j] == i for j in loose) else vmem for i in range(len(given))]
        return pl.pallas_call(
            inner,
            out_shape=tuple(jax.ShapeDtypeStruct(s, d) for s, d in outs),
            in_specs=spaces + [anywhere] * len(after),
            out_specs=tuple(anywhere if loose_outs else vmem for _ in outs),
            scratch_shapes=list(scratch),
            compiler_params=pltpu.CompilerParams(vmem_limit_bytes=limit * 2**20),
            cost_estimate=pl.CostEstimate(
                flops=1 + int(weight * 1e9), bytes_accessed=1, transcendentals=0
            ),
            name=name,
        )(*given, *after)

    return run


def places(cap, rows, half, blk):
    k, j = iota((rows, rows), 0), iota((rows, rows), 1)
    cap_col = jnp.sum(jnp.where(k == j, cap, 0.0), axis=1, keepdims=True)
    rank_row = jnp.sum(jnp.where(k < j, cap_col, 0.0), axis=0, keepdims=True)
    rank_col = jnp.sum(jnp.where(j < k, cap, 0.0), axis=1, keepdims=True)
    at_row = iota((1, rows), 1).astype(F32)
    at_col = iota((rows, 1), 0).astype(F32)
    dest_row = jnp.where(cap > 0.5, rank_row, blk + at_row - rank_row)
    dest_col = jnp.where(cap_col > 0.5, rank_col, blk + at_col - rank_col)
    return dest_row.astype(jnp.int32), dest_col.astype(jnp.int32)


def sorted_rows(cot, cap, blk):
    rows = cot.shape[0]
    dest_row, _ = places(row_of(cap).astype(F32), rows, rows // 2, blk)
    pick = (iota((2 * blk, rows), 0) == dest_row).astype(BF16)
    c = dot_nn(pick, cot[...]).astype(BF16)
    return c[blk:], c[:blk]


def pre_body(
    tok_far, cot_far, cap_far, lens_far, gain2_far, cot_core, cap_core,
    xc, xn, n2n, cotn, cotc, cotn_core, cotc_core, bias,
    tok, cot, cap, lens, gain2, sems,
):
    pairs = ((cap_far, cap), (tok_far, tok), (lens_far, lens), (gain2_far, gain2), (cot_far, cot))
    copies = [pltpu.make_async_copy(a, b, sems.at[i]) for i, (a, b) in enumerate(pairs)]
    for c in copies:
        c.start()
    cotn_core[...], cotc_core[...] = sorted_rows(cot_core, cap_core, xc.shape[0])
    for c in copies:
        c.wait()
    rows = tok.shape[0]
    blk = xc.shape[0]
    dest_row, _ = places(row_of(cap).astype(F32), rows, rows // 2, blk)
    pick = (iota((2 * blk, rows), 0) == dest_row).astype(BF16)
    x = dot_nn(pick, tok[...])
    xc[...] = x[:blk].astype(BF16)
    xn[...] = x[blk:].astype(BF16)
    n2n[...] = norm_rows(x[blk:], row_of(gain2))[0].astype(BF16)
    c = dot_nn(pick, cot[...]).astype(BF16)
    cotn[...] = c[blk:]
    cotc[...] = c[:blk]
    position = iota((1, rows), 1)
    crop = jnp.ones((1, rows), F32)
    end = 0
    for s in range(lens.shape[1]):
        end = end + lens[0, s]
        crop = crop + (position >= end).astype(F32)
    crop_col = jnp.sum(jnp.where(iota((blk, rows), 0) == dest_row, crop, 0.0), axis=1, keepdims=True)
    crop_row = jnp.sum(
        jnp.where(iota((blk, blk), 0) == iota((blk, blk), 1), crop_col, 0.0), axis=0, keepdims=True
    )
    bias[...] = jnp.where(crop_col == crop_row, 0.0, NEGATIVE)


def sort_body(count, *refs):
    for cot, cap, left, right, out_c in zip(*(refs[k * count : (k + 1) * count] for k in range(5))):
        rows, out_c[...] = sorted_rows(cot, cap, out_c.shape[0])
        middle = left.shape[1]
        left[...], right[...] = rows[:, :middle], rows[:, middle:]


def halve_body(count, *refs):
    for array, left, right in zip(*(refs[k * count : (k + 1) * count] for k in range(3))):
        middle = left.shape[1]
        left[...], right[...] = array[:, :middle], array[:, middle:]


def half_mask(shape, e):
    return (iota(shape, 1) < HEAD_DIM) == (e == 0)


def fore_body(
    half,
    xc, bias, gain1, router, w_qkv, w_out, gain2,
    n1, qkv, probs, heads, attended, gate, n2c, stats,
):
    blk, width = xc.shape
    x = xc[...].astype(F32)
    low = norm_rows(x, row_of(gain1))[0].astype(BF16)
    n1[...] = low
    logit = jnp.sum(low.astype(F32) * row_of(router), axis=-1, keepdims=True)
    gated = jnp.where(iota((blk, 1), 0) < half, jax.nn.sigmoid(logit), 0.0)
    gate[...] = gated
    qkv[...] = dot_nn(low, w_qkv[...]).astype(BF16)
    scale = 1.0 / math.sqrt(HEAD_DIM)
    for pair in range(HEADS // 2):
        at = pair * PAIR
        q = qkv[:, at : at + PAIR]
        k = qkv[:, width + at : width + at + PAIR]
        v = qkv[:, 2 * width + at : 2 * width + at + PAIR]
        total = None
        for e in range(2):
            mask = half_mask((blk, PAIR), e)
            zero = jnp.zeros_like(q)
            scores = dot_nt(jnp.where(mask, q, zero), k) * scale + bias[...]
            exponent = jnp.exp(scores - jnp.max(scores, axis=-1, keepdims=True))
            prob = (exponent / jnp.sum(exponent, axis=-1, keepdims=True)).astype(BF16)
            probs[2 * pair + e] = prob
            part = dot_nn(prob, jnp.where(mask, v, zero))
            total = part if total is None else total + part
        heads[:, at : at + PAIR] = total.astype(BF16)
    att = dot_nn(heads[...], w_out[...])
    attended[...] = att
    branch = gated * att
    resid = x + branch
    n2c[...] = norm_rows(resid, row_of(gain2))[0].astype(BF16)
    stats[0:1, :] = jnp.sum(resid * resid, axis=0, keepdims=True)
    stats[1:2, :] = jnp.sum(branch * branch, axis=0, keepdims=True)


def mlp_body(blk, outs_at, n2s, cots, w_up, w_down, act, dpre, *outs):
    for s, (n2, cot) in enumerate(zip(n2s, cots)):
        rows = pl.ds(s * blk, blk)
        pre = dot_nn(whole(n2), w_up[...])
        d_act = dot_nt(whole(cot), w_down[...])
        square = pre * pre
        t = jnp.tanh(pre * (GELU_C + GELU_C * GELU_A * square))
        half_up = 0.5 + 0.5 * t
        slope = half_up + pre * (0.5 - 0.5 * t * t) * (GELU_C + 3.0 * GELU_C * GELU_A * square)
        a = (pre * half_up).astype(BF16)
        d = (d_act * slope).astype(BF16)
        act[rows, :] = a
        dpre[rows, :] = d
        (d_out, d_at), (h_out, h_at) = outs_at[s]
        outs[d_out][pl.ds(d_at, blk), :] = dot_nt(d, w_up[...]).astype(BF16)
        outs[h_out][pl.ds(h_at, blk), :] = dot_nn(a, w_down[...]).astype(BF16)


def copy_rows(sources, target):
    at = 0
    for ref in sources:
        rows = whole(ref)
        target[at : at + rows.shape[0]] = rows
        at += rows.shape[0]


def whole(ref):
    if isinstance(ref, tuple):
        return jnp.concatenate([r[...] for r in ref], axis=1)
    return ref[...]


def near_weights_body(act, dpre, n2s, cots, down, up, n2, cot):
    copy_rows(cots, cot)
    copy_rows(n2s, n2)
    down[...] = dot_tn(act[...], cot[...])
    up[...] = dot_tn(n2[...], dpre[...])


def weights_body(quarters, acts, dpres, n2s, cots, down, up, outs, act, dpre, n2, cot, total, grad_up):
    units = down.shape[0]
    part = units // quarters
    copy_rows(acts, act)
    copy_rows(cots, cot)
    total[...] = (down[...] + dot_tn(act[...], cot[...])).astype(BF16)
    copy_rows(dpres, dpre)
    copy_rows(n2s, n2)
    grad_up[...] = (up[...] + dot_tn(n2[...], dpre[...])).astype(BF16)
    lo = lax.rem(lax.axis_index("dp"), quarters)
    down_keep, down_send, up_keep, up_send = outs
    blocks = grad_up.shape[0] // units
    for p in range(quarters):
        first = lax.bitwise_xor(lo, p) * part
        target, at = (down_keep, down_send)[p % 2], p // 2 * part
        target[at : at + part] = total[pl.ds(pl.multiple_of(first, 16), part), :]
        target, at = (up_keep, up_send)[p // 2], p % 2 * part
        for k in range(blocks):
            row = pl.multiple_of(first * blocks + k * part, 16)
            target[at : at + part, k * units : (k + 1) * units] = grad_up[pl.ds(row, part), :]


def halves_body(down, down_got, up, up_got, kept, down_send, up_send):
    size = down_send.shape[0]
    a = down[...].astype(F32) + down_got[...].astype(F32)
    b = up[...].astype(F32) + up_got[...].astype(F32)
    kept[:size] = a[:size]
    kept[size:] = b[:size]
    down_send[...] = a[size:].astype(BF16)
    up_send[...] = b[size:].astype(BF16)


def own_body(kept, down_got, up_got, mine):
    size = down_got.shape[0]
    mine[:size] = (kept[:size] + down_got[...].astype(F32)).astype(BF16)
    mine[size:] = (kept[size:] + up_got[...].astype(F32)).astype(BF16)


def far_sum_body(d_c0, d_c1, n0, n1, h0, h1, joint, rest):
    def both(a, b):
        return (a[...].astype(F32) + b[...].astype(F32)).astype(BF16)

    joint[...] = both(d_c0, d_c1)
    size = n0.shape[0]
    rest[:size] = both(n0, n1)
    rest[size:] = both(h0, h1)


def add_body(count, *refs):
    total = refs[0][...].astype(F32)
    for ref in refs[1:count]:
        total = total + ref[...].astype(F32)
    refs[count][...] = total.astype(refs[count].dtype)


def spread_body(a, b, a_got, b_got, *outs):
    for own, other, both in ((a, a_got, outs[0]), (b, b_got, outs[1])):
        size = own.shape[0]
        both[:size] = own[...]
        both[size:] = other[...]


def assemble_body(long, short, down_far, up_far, mark, down, up, sems):
    units = up.shape[1]
    part = units // len(long)
    blocks = up.shape[0] // units
    lo = lax.rem(lax.axis_index("dp"), len(long))
    firsts = [lax.bitwise_xor(lo, p) * part for p in range(len(long))]
    for first, rows in zip(firsts, long):
        down[pl.ds(pl.multiple_of(first, 8), part), :] = rows[:part].astype(F32)
    down_copy = pltpu.make_async_copy(down, down_far, sems.at[0])
    down_copy.start()
    for first, *pieces in zip(firsts, long, short):
        offset = 0
        for rows in (pieces[0][part:].astype(F32), pieces[1][...].astype(F32)):
            for k in range(blocks):
                at = pl.multiple_of(first * blocks + k * part + offset, 8)
                up[pl.ds(at, rows.shape[0]), :] = rows[:, k * units : (k + 1) * units]
            offset += rows.shape[0]
    up_copy = pltpu.make_async_copy(up, up_far, sems.at[1])
    up_copy.start()
    down_copy.wait()
    up_copy.wait()


def back_body(
    half,
    d_n2_0, d_n2_1, d_n2_2, cc, xc, attended, gate, heads, qkv, probs, w_out, gain2,
    d_resid_out, d_qkv, d_att_out, d_logit_out, g_gain2,
):
    blk, width = xc.shape
    scale = 1.0 / math.sqrt(HEAD_DIM)
    gated = gate[...]
    att = attended[...]
    resid = xc[...].astype(F32) + gated * att
    _, unit2, inverse2 = norm_rows(resid, row_of(gain2))
    d_n2 = d_n2_0[...].astype(F32) + d_n2_1[...].astype(F32)
    for at in range(0, d_n2_2.shape[0], blk):
        d_n2 = d_n2 + d_n2_2[at : at + blk].astype(F32)
    back2, g_gain2[...] = norm_back(d_n2, unit2, inverse2, row_of(gain2))
    d_resid = cc[...].astype(F32) + back2
    d_resid_out[...] = d_resid
    d_att = (d_resid * gated).astype(BF16)
    keep = (iota((blk, 1), 0) < half).astype(F32)
    d_gate = keep * jnp.sum(d_resid * att, axis=-1, keepdims=True)
    d_logit_out[...] = d_gate * gated * (1.0 - gated)
    d_att_out[...] = d_att
    d_heads = dot_nt(d_att, w_out[...]).astype(BF16)
    for pair in range(HEADS // 2):
        at = pair * PAIR
        q = qkv[:, at : at + PAIR]
        k = qkv[:, width + at : width + at + PAIR]
        v = qkv[:, 2 * width + at : 2 * width + at + PAIR]
        d_o = d_heads[:, at : at + PAIR]
        zero = jnp.zeros_like(q)
        d_q = d_k = d_v = 0.0
        for e in range(2):
            mask = half_mask((blk, PAIR), e)
            d_oe = jnp.where(mask, d_o, zero)
            prob = probs[2 * pair + e]
            prob_f = prob.astype(F32)
            d_prob = dot_nt(d_oe, v)
            d_score = (
                prob_f * (d_prob - jnp.sum(prob_f * d_prob, axis=-1, keepdims=True))
            ).astype(BF16)
            d_v = d_v + dot_tn(prob, d_oe)
            d_q = d_q + dot_nn(d_score, jnp.where(mask, k, zero))
            d_k = d_k + dot_tn(d_score, jnp.where(mask, q, zero))
        d_qkv[:, at : at + PAIR] = (d_q * scale).astype(BF16)
        d_qkv[:, width + at : width + at + PAIR] = (d_k * scale).astype(BF16)
        d_qkv[:, 2 * width + at : 2 * width + at + PAIR] = d_v.astype(BF16)


def products_body(tsize, heads, n1, d_qkv, d_att, table, *outs):
    width = n1.shape[1]
    me = lax.axis_index("dp") * tsize + lax.axis_index("tensor")
    share = width // (tsize * lax.axis_size("dp"))
    mid = outs[0].shape[0]
    for side in range(2):
        source = lax.bitwise_xor(table[side : side + 1, :], me) * share + table[2:3, :]
        order = (iota((width, width), 0) == source).astype(BF16)
        low = dot_nn(n1[...], order).astype(BF16)
        keep, send = outs[2 * side : 2 * side + 2]
        for k in range(2):
            at = k * width
            if side and k:
                product = dot_tn(dot_nn(heads[...], order).astype(BF16), d_att[...])
            else:
                column = (2 * side + k) * width
                product = dot_tn(low, d_qkv[:, column : column + width])
            product = product.astype(BF16)
            keep[:, at : at + width] = product[:mid]
            send[:, at : at + width] = product[mid:]


def to_pair(sums):
    top = sums.astype(BF16)
    return jnp.concatenate([top, (sums - top.astype(F32)).astype(BF16)], axis=0)


def fold_pair(sums):
    top = sums.astype(BF16).astype(F32)
    third = sums.shape[1] // 3
    both = [top, sums - top]
    blocks = [jnp.concatenate([a[:, k * third : (k + 1) * third] for a in both], axis=1) for k in range(3)]
    return jnp.concatenate(blocks, axis=0).astype(BF16)


def unfold_pair(folded):
    rows, third = folded.shape[0] // 3, folded.shape[1] // 2
    both = folded[:, :third].astype(F32) + folded[:, third:].astype(F32)
    return jnp.concatenate([both[k * rows : (k + 1) * rows] for k in range(3)], axis=1)


def from_pair(pair):
    size = pair.shape[0] // 2
    return pair[:size].astype(F32) + pair[size:].astype(F32)


def add_split_body(count, pieces, *refs):
    total = refs[0][...].astype(F32)
    for ref in refs[1:count]:
        total = total + ref[...].astype(F32)
    size = total.shape[0] // pieces
    for p in range(pieces):
        refs[count + p][...] = total[p * size : (p + 1) * size].astype(refs[count + p].dtype)


def put_back(pick, rows):
    top = rows.astype(BF16)
    rest = (rows - top.astype(F32)).astype(BF16)
    return dot_nn(pick, top) + dot_nn(pick, rest)


def post_body(
    cap, d_n0, hid_c0, hid_n0, d_nx, hid_c1, hid_n1, rest,
    xc, xn, cn, attended, gate, d_resid_c, d_qkv, d_logit, n1, w_qkv, gain1, gain2, router, g_gain2c, stats1,
    mixed, grad_in, sums,
):
    rows = mixed.shape[0]
    blk = xc.shape[0]
    _, dest_col = places(row_of(cap).astype(F32), rows, rows // 2, blk)
    pick_c = (iota((rows, blk), 1) == dest_col).astype(BF16)
    pick_n = (iota((rows, blk), 1) + blk == dest_col).astype(BF16)
    x_c, x_n = xc[...].astype(F32), xn[...].astype(F32)

    d_n1 = dot_nt(d_qkv[...], w_qkv[...]) + d_logit[...] * row_of(router)
    _, unit1, inverse1 = norm_rows(x_c, row_of(gain1))
    back1, g_gain1 = norm_back(d_n1, unit1, inverse1, row_of(gain1))
    grad_c = d_resid_c[...] + back1

    def summed(first, second, others, start, stop):
        total = first[...].astype(F32) + second[...].astype(F32)
        for o in range(start, stop, blk):
            total = total + others[o : o + blk].astype(F32)
        return total

    third = rest.shape[0] // 3
    d_n2n = summed(d_n0, d_nx, rest, 0, third)
    h_n = summed(hid_n0, hid_n1, rest, third, 2 * third)
    h_c = summed(hid_c0, hid_c1, rest, 2 * third, 3 * third)
    mix_c = (x_c + gate[...] * attended[...] + h_c).astype(BF16)
    mix_n = (x_n + h_n).astype(BF16)
    mixed[...] = (dot_nn(pick_c, mix_c) + dot_nn(pick_n, mix_n)).astype(BF16)
    _, unit, inverse = norm_rows(x_n, row_of(gain2))
    back, g_gain2n = norm_back(d_n2n, unit, inverse, row_of(gain2))
    d_resid_n = cn[...].astype(F32) + back
    grad_in[...] = put_back(pick_c, grad_c) + put_back(pick_n, d_resid_n)

    def over_rows(a):
        return jnp.sum(a, axis=0, keepdims=True)

    sums[...] = jnp.zeros_like(sums)
    sums[0:1, :] = g_gain1
    sums[1:2, :] = over_rows(d_logit[...] * n1[...].astype(F32))
    sums[2:3, :] = g_gain2c[...] + g_gain2n
    sums[3:4, :] = stats1[0:1, :] + over_rows(x_n * x_n)
    sums[4:5, :] = stats1[1:2, :]
    sums[5:6, :] = over_rows(h_c * h_c) + over_rows(h_n * h_n)


CORES = 2
GROUP = 4
PARTS = 1
W_MLP1 = 10.0
W_MLP2 = 0.0
W_LAST = 5.0
W_ATT4 = 20.0


def swap(name, array, axis, size, bits):
    with jax.named_scope(name):
        return lax.ppermute(array, axis, [(t, t ^ bits) for t in range(size)])


def add(name, arrays, after=(), weight=1.0):
    return call(
        lambda *refs: add_body(len(arrays), *refs),
        [(arrays[0].shape, BF16)],
        name,
        after=after,
        weight=weight,
    )(*arrays)[0]


def in_order(name, own, others, place, cut, after):
    if len(others) > 1:
        held = jnp.stack([own, *others])
        own, *others = [
            lax.dynamic_index_in_dim(held, place ^ at, 0, keepdims=False) for at in range(len(held))
        ]

    def body(*refs):
        total = refs[0][...].astype(F32)
        for ref in refs[1:-2]:
            total = total + ref[...].astype(F32)
        refs[-2][...] = total[:cut].astype(BF16)
        refs[-1][...] = total[cut:].astype(BF16)

    rows, columns = own.shape
    return call(
        body, [((cut, columns), BF16), ((rows - cut, columns), BF16)], name, after=after, weight=W_MLP2
    )(own, *others)


def shards(
    tokens, lengths, capacity, norm1_gain, router, w_qkv, w_out, norm2_gain, w_up, w_down, cotangent
):
    rows, width = tokens.shape
    half = rows // 2
    blk = -(-half // 16) * 16
    units = w_up.shape[1]
    tsize, dsize = lax.axis_size("tensor"), lax.axis_size("dp")
    ysize = tsize // CORES
    others = range(1, ysize)
    cap, gain1, gain2, route = capacity, norm1_gain, norm2_gain, router
    small = (blk, width)

    def far(name, array):
        return [swap("y_" + name, array, "tensor", tsize, dy * CORES) for dy in others]

    def across(name, array):
        return swap("core_" + name, array, "tensor", tsize, 1)

    cap_far, cot_far = far("cap", cap), far("cot", cotangent)
    xc, xn, n2n, cotn, cotc, cotn_core, cotc_core, bias = call(
        pre_body,
        [(small, BF16)] * 7 + [((blk, blk), F32)],
        "pre",
        scratch=[
            pltpu.VMEM(tokens.shape, BF16), pltpu.VMEM(cotangent.shape, BF16), pltpu.VMEM(cap.shape, jnp.int32),
            pltpu.SMEM(lengths.shape, jnp.int32), pltpu.VMEM(gain2.shape, F32), pltpu.SemaphoreType.DMA((5,)),
        ],
        loose=range(5),
        after=cap_far,
        weight=20.0,
    )(tokens, cotangent, cap, lengths, gain2, across("cot", cotangent), across("cap", cap))

    def group(name, pieces):
        return [swap("xz_" + name, pieces[p], "dp", dsize, p) for p in range(1, GROUP)]

    def high(name, pieces):
        return [
            swap("zz_" + name, pieces[p % len(pieces)], "dp", dsize, p * GROUP)
            for p in range(1, dsize // GROUP)
        ]

    n2n_far, n2n_core = far("n2n", n2n), across("n2n", n2n)

    n1, qkv, probs, heads, attended, gate, n2c, stats1 = call(
        lambda *refs: fore_body(half, *refs),
        [
            (small, BF16), ((blk, 3 * width), BF16), ((HEADS, blk, blk), BF16), (small, BF16),
            (small, F32), ((blk, 1), F32), (small, BF16), ((2, width), F32),
        ],
        "fore",
    )(xc, bias, gain1, route, w_qkv, w_out, gain2)

    n2c_far, n2c_core = far("n2c", n2c), across("n2c", n2c)

    def mlp(name, n2s, cots, outs, outs_at, after=(), weight=1.0):
        tall = blk * len(outs_at)
        count = len(n2s)
        return call(
            lambda *refs: mlp_body(
                blk, outs_at, refs[:count], refs[count : 2 * count], *refs[2 * count :]
            ),
            [((tall, units), BF16)] * 2 + [((n * blk, width), BF16) for n in outs],
            name,
            after=after,
            weight=weight,
        )(*n2s, *cots, w_up, w_down)

    n2_near = [n2c, n2n, n2c_core, n2n_core]
    cot_near = [cotc, cotn, cotc_core, cotn_core]
    at_near = [((c, k * blk), (c, (2 + k) * blk)) for c in range(CORES) for k in range(2)]
    act_a, dpre_a, near_0, near_1 = mlp("mlp_near", n2_near, cot_near, [4, 4], at_near)
    near_1 = across("near", near_1)

    def tie(name, arrays, after):
        return list(
            pl.pallas_call(
                lambda *refs: None,
                out_shape=tuple(jax.ShapeDtypeStruct(a.shape, a.dtype) for a in arrays),
                in_specs=[pl.BlockSpec(memory_space=pl.ANY)] * (len(arrays) + len(after)),
                out_specs=tuple(pl.BlockSpec(memory_space=pl.ANY) for _ in arrays),
                input_output_aliases={i: i for i in range(len(arrays))},
                compiler_params=pltpu.CompilerParams(vmem_limit_bytes=2**20),
                name=name,
            )(*arrays, *after)
        )

    count = len(cot_far)
    slim = (blk, width // 2)
    sorted_far = call(
        lambda *refs: sort_body(count, *refs),
        [(slim, BF16)] * (2 * count) + [(small, BF16)] * count,
        "sort_far",
        after=[act_a],
        weight=0.0,
    )(*cot_far, *cap_far)
    cotn_far = [Pair(sorted_far[i : 2 * count : count]) for i in range(count)]
    cotc_far = list(sorted_far[2 * count :])
    cotn_all = cotn_far + [Pair([across("far_cotn", a) for a in p]) for p in cotn_far]
    halves = call(
        lambda *refs: halve_body(count, *refs),
        [(slim, BF16)] * (2 * count),
        "halve_n2n",
        after=[a for p in cotn_all[count:] for a in p],
        weight=0.0,
    )(*n2n_far)
    n2n_far = [Pair(halves[i::count]) for i in range(count)]
    n2n_all = n2n_far + [Pair([across("far_n2n", a) for a in p]) for p in n2n_far]
    cotc_all = cotc_far + [across("far_cotc", a) for a in cotc_far]

    tall = 4 * blk
    down_near, up_near = call(
        lambda act, dpre, *refs: near_weights_body(act, dpre, refs[:4], refs[4:8], *refs[8:]),
        [((units, width), F32), ((width, units), F32)],
        "weights_near",
        scratch=[pltpu.VMEM((tall, width), BF16)] * 2,
        after=n2n_far[0][:1],
        weight=0.0,
    )(act_a, dpre_a, *n2_near, *cot_near)


    far_at = range(CORES * (ysize - 1))
    place = lambda s: (s // (ysize - 1), s % (ysize - 1) * blk)
    act_n, dpre_n, far_n0, far_n1 = mlp(
        "mlp_far_n", n2n_all, cotn_all, [2 * (ysize - 1)] * 2,
        [(place(s), (place(s)[0], place(s)[1] + (ysize - 1) * blk)) for s in far_at],
        [down_near], 0.0,
    )
    far_n1 = across("far_n", far_n1)
    n2c_far = tie("tie_c", n2c_far, [act_n, *cotc_all[count:]])
    n2c_all = n2c_far + [across("far_n2c", a) for a in n2c_far]
    def far_c(name, n2s, cots, after=()):
        outs_at = [((0, i * blk), (1, i * blk)) for i in range(len(n2s))]
        return mlp(name, n2s, cots, [len(n2s)] * 2, outs_at, after)

    count = ysize - 1
    act_c0, dpre_c0, d_c0, hid_c0 = far_c("mlp_far_c0", n2c_all[:count], cotc_all[:count])
    act_c1, dpre_c1, d_c1, hid_c1 = far_c("mlp_far_c1", n2c_all[count:], cotc_all[count:], [act_c0])
    d_c1, hid_c1 = across("d_c", d_c1), across("hid_c", hid_c1)

    def send_back(name, joint, groups):
        if ysize == 2:
            return swap("y_" + name, joint, "tensor", tsize, CORES)
        cut = joint.reshape(groups, ysize - 1, blk, width)
        got = [swap("y_" + name, cut[:, dy - 1], "tensor", tsize, dy * CORES) for dy in others]
        return jnp.stack(got, axis=1).reshape(joint.shape)

    cots, n2s = cotn_all + cotc_all, n2n_all + n2c_all
    count, tall = len(cots), len(cots) * blk
    part = units // GROUP

    def weights(*refs):
        acts, dpres, refs = refs[:3], refs[3:6], refs[6:]
        n2s, cots, refs = refs[:count], refs[count : 2 * count], refs[2 * count :]
        weights_body(
            GROUP, acts, dpres, n2s, cots, *refs[:2], refs[2:6], *refs[6:]
        )

    down_keep, down_got, up_keep, up_got = call(
        weights,
        [((2 * part, width), BF16)] * 4,
        "weights",
        scratch=[
            pltpu.VMEM((tall, units), BF16), pltpu.VMEM((tall, units), BF16),
            pltpu.VMEM((tall, width), BF16), pltpu.VMEM((tall, width), BF16),
            pltpu.VMEM((units, width), BF16), pltpu.VMEM((width, units), BF16),
        ],
        after=[],
    )(act_n, act_c0, act_c1, dpre_n, dpre_c0, dpre_c1, *n2s, *cots, down_near, up_near)
    mark = down_keep
    down_got = swap("xz_down", down_got, "dp", dsize, 1)
    up_got = swap("zx_up", up_got, "dp", dsize, 2)
    joint, rest = call(
        far_sum_body,
        [(((ysize - 1) * blk, width), BF16), ((3 * (ysize - 1) * blk, width), BF16)],
        "far_sum",
        after=[mark],
    )(d_c0, d_c1, far_n0, far_n1, hid_c0, hid_c1)
    d_c2 = send_back("d_c", joint, 1)
    rest = send_back("rest", rest, 3)

    mark = joint

    shares = tsize * dsize
    share = width // shares
    def owners(y_first):
        table = []
        for core in range(CORES):
            for first in range(ysize if y_first else 2):
                for then in range(2 if y_first else ysize):
                    y, x = (first, then) if y_first else (then, first)
                    for z in range(2):
                        for hi in range(dsize // GROUP):
                            place = (hi * GROUP + z * 2 + x) * tsize + y * CORES + core
                            table += [place] * share
        return table

    table = jnp.array([owners(True), owners(False), list(range(share)) * shares], jnp.int32)
    d_resid_c, d_qkv, d_att, d_logit, g_gain2c = call(
        lambda *refs: back_body(half, *refs),
        [
            (small, F32), ((blk, 3 * width), BF16), (small, BF16), ((blk, 1), F32), ((1, width), F32),
        ],
        "back",
        after=[mark],
        weight=20.0,
    )(
        (near_0, 0, blk), (near_1, 0, blk), d_c2, cotc, xc, attended, gate, heads, qkv, probs,
        w_out, gain2,
    )
    kept, down_got, up_got = call(
        halves_body,
        [((2 * part, width), F32), ((part, width), BF16), ((part, width), BF16)],
        "mlp_0",
        after=[d_resid_c],
        weight=0.0,
    )(down_keep, down_got, up_keep, up_got)
    mark = kept
    down_got = swap("xz_down", down_got, "dp", dsize, 2)
    up_got = swap("zx_up", up_got, "dp", dsize, 1)

    left, left_got, right, right_got = call(
        lambda *refs: products_body(tsize, *refs),
        [((width // 2, 2 * width), BF16)] * 4,
        "products",
        after=[mark],
    )(heads, n1, d_qkv, d_att, table)
    left_got, right_got = across("left", left_got), across("right", right_got)

    def sums_of(name, *sets, after=(), along=(), weight=1.0):
        given = [a for arrays, _ in sets for a in arrays]

        def body(*refs):
            ins, outs = list(refs[: len(given)]), list(refs[len(given) + len(along) :])
            if along:
                outs[-1][...] = refs[len(given)][...] + refs[len(given) + 1][...]
            for arrays, count in sets:
                add_split_body(len(arrays), count, *ins[: len(arrays)], *outs[:count])
                del ins[: len(arrays)], outs[:count]

        shapes = []
        for arrays, count in sets:
            rows, columns = arrays[0].shape
            shapes += [((rows // count, columns), BF16)] * count
        shapes += [(a.shape, a.dtype) for a in along[:1]]
        return call(body, shapes, name, after=after, weight=weight)(*given, *along)

    mine = call(
        own_body, [((2 * part, width), BF16)], "mlp_1", after=[left], weight=W_MLP1
    )(kept, down_got, up_got)
    mine_got = [high("mlp", mine)]

    *left, right, right_got = sums_of(
        "att_1", ([left, left_got], ysize), ([right, right_got], 2), after=[mine[0], rest]
    )
    left_got = [swap("y_left", left[p], "tensor", tsize, p * CORES) for p in others]
    right_got = swap("x_right", right_got, "dp", dsize, 1)

    mixed, grad_input, sums = call(
        post_body,
        [((rows, width), BF16), ((rows, width), F32), ((8, width), F32)],
        "post",
        after=[right],
        weight=20.0,
    )(
        cap, (near_0, 1, blk), (near_0, 2, blk), (near_0, 3, blk), (near_1, 1, blk), (near_1, 2, blk),
        (near_1, 3, blk), rest,
        xc, xn, cotn, attended, gate, d_resid_c, d_qkv, d_logit, n1, w_qkv, gain1, gain2, route, g_gain2c,
        stats1,
    )

    step = 1
    while step < tsize // 2:
        sums = sums + swap("sums", sums, "tensor", tsize, step)
        step *= 2
    sums_got = swap("sums", sums, "tensor", tsize, step)

    right = sums_of("right_2", ([right, right_got], ysize), after=[sums], weight=0.0)
    right_got = [swap("y_right", right[p], "tensor", tsize, p * CORES) for p in others]
    low_rows = 2 * sums.shape[0]

    def left_body(*refs):
        *ins, a, b, kept, sent, sums_out = refs
        total = ins[0][...].astype(F32)
        for ref in ins[1:]:
            total = total + ref[...].astype(F32)
        size = kept.shape[0]
        kept[...] = total[:size].astype(BF16)
        sent[:size] = total[size:].astype(BF16)
        sent[size:] = jnp.zeros_like(sent[size:])
        sums_out[...] = to_pair(a[...] + b[...])
        sent[size:, : sums_out.shape[1]] = sums_out[...]

    size = left[0].shape[0] // 2
    left, left_got, sums = call(
        left_body,
        [((size, 2 * width), BF16), ((size + low_rows, 2 * width), BF16), ((low_rows, width), BF16)],
        "left_2",
        after=[right[0]],
        weight=0.0,
    )(left[0], *left_got, sums, sums_got)
    left_got = swap("x_left", left_got, "dp", dsize, 1)

    cut = 2 * part * 2 // 3
    mine = in_order("mlp_2", mine[0], mine_got[0], lax.axis_index("dp") // GROUP, cut, [left])
    mine_got = [swap("zx_long", mine[0], "dp", dsize, 2), swap("xz_short", mine[1], "dp", dsize, 1)]

    highs = dsize // GROUP

    def join_body(*refs):
        (left, left_got, *rights), sums, outs = refs[: -2 * highs - 1], refs[-2 * highs - 1], refs[-2 * highs :]
        size = left.shape[0]
        middle = left.shape[1]
        pair = fold_pair(from_pair(sums[...]) + from_pair(left_got[size:, : sums.shape[1]]))
        totals = [left[...].astype(F32) + left_got[:size].astype(F32), rights[0][...].astype(F32)]
        for ref in rights[1:]:
            totals[1] = totals[1] + ref[...].astype(F32)
        for p, out in enumerate(outs):
            for k, total in enumerate(totals):
                out[:share, k * middle : (k + 1) * middle] = total[p * share : (p + 1) * share].astype(BF16)
            out[: pair.shape[0], 2 * middle :] = pair

    att = call(
        join_body,
        [((max(share, low_rows * 3 // 2), 4 * width + width * 2 // 3), BF16)] * (2 * highs),
        "att_3",
        after=[mine[0]],
        weight=20.0,
    )(left, left_got, right[0], *right_got, sums)
    long_rest, short_rest = call(
        spread_body,
        [((2 * a.shape[0], width), BF16) for a in mine],
        "pairs",
        after=att[:1],
        weight=0.0,
    )(*mine, *mine_got)
    att = [att[0]] + tie("tie_att", att[1:], [long_rest])
    att_got = [
        swap("z_att", att[p], "dp", dsize, p // highs * 2 + p % highs * GROUP)
        for p in range(1, 2 * highs)
    ]
    long_rest = swap("zx_long", long_rest, "dp", dsize, 1)
    short_rest = swap("xz_short", short_rest, "dp", dsize, 2)

    g_down, g_up, mark = call(
        lambda a0, a2, a13, b0, b1, b23, *refs: assemble_body(
            (a0, a13.at[pl.ds(0, cut)], a2, a13.at[pl.ds(cut, cut)]),
            (b0, b1, b23.at[pl.ds(0, 2 * part - cut)], b23.at[pl.ds(2 * part - cut, 2 * part - cut)]),
            *refs,
        ),
        [((units, width), F32), ((width, units), F32), ((8, 128), F32)],
        "assemble",
        scratch=[
            pltpu.VMEM((units, width), F32), pltpu.VMEM((width, units), F32), pltpu.SemaphoreType.DMA((2,)),
        ],
        weight=W_LAST,
        loose_outs=True,
        after=att[1:2],
    )(mine[0], mine_got[0], long_rest, mine[1], mine_got[1], short_rest)

    count = rows * width * dsize * tsize

    def att_body(*refs):
        ins, outs = refs[: 2 * highs], refs[2 * highs :]
        out_qkv, out_proj, out_gain1, out_router, out_gain2, norms = outs
        total = ins[0][:share, : 4 * width].astype(F32)
        for ref in ins[1:]:
            total = total + ref[:share, : 4 * width].astype(F32)
        out_qkv[...] = total[:, : 3 * width]
        out_proj[...] = total[:, 3 * width :]
        sums = [unfold_pair(ref[: low_rows * 3 // 2, 4 * width :]) for ref in ins]
        while len(sums) > 1:
            sums = [a + b for a, b in zip(sums[::2], sums[1::2])]
        for k, out in enumerate((out_gain1, out_router, out_gain2)):
            out[...] = sums[0][k : k + 1, :].reshape(width)
        norms[...] = jnp.sqrt(jnp.sum(sums[0][3:6, :], axis=-1) / count)

    g_qkv, g_proj, g_gain1, g_router, g_gain2, norms = call(
        att_body,
        [((share, 3 * width), F32), ((share, width), F32)] + [((width,), F32)] * 3 + [((3,), F32)],
        "att_4",
        weight=W_ATT4,
        after=[mark],
    )(att[0], *att_got)

    return (
        mixed, grad_input, g_gain1, g_router, g_qkv, g_proj, g_gain2, g_up, g_down, norms,
    )


def solution(mesh):
    return jax.shard_map(
        shards,
        mesh=mesh,
        in_specs=(
            P(("dp", "tensor"), None),
            P(("dp", "tensor"), None),
            P(("dp", "tensor")),
            P(),
            P(),
            P(),
            P(),
            P(),
            P(None, "tensor"),
            P("tensor", None),
            P(("dp", "tensor"), None),
        ),
        out_specs=(
            P(("dp", "tensor"), None),
            P(("dp", "tensor"), None),
            P(),
            P(),
            P(("dp", "tensor"), None),
            P(("dp", "tensor"), None),
            P(),
            P(None, "tensor"),
            P("tensor", None),
            P(),
        ),
        check_vma=False,
    )
```

```python
import math

import jax
import jax.numpy as jnp
from jax import lax
from jax.experimental import pallas as pl
from jax.experimental.pallas import tpu as pltpu
from jax.sharding import PartitionSpec as P

HEADS = 12
HEAD_DIM = 64
PAIR = 2 * HEAD_DIM
EPSILON = 1e-06
NEGATIVE = -1000000000.0
GELU_C = math.sqrt(2.0 / math.pi)
GELU_A = 0.044715
F32 = jnp.float32
BF16 = jnp.bfloat16
VMEM_LIMIT = 24


def dot_nn(a, b):
    return lax.dot_general(a, b, (((1,), (0,)), ((), ())), preferred_element_type=F32)


def dot_nt(a, b):
    return lax.dot_general(a, b, (((1,), (1,)), ((), ())), preferred_element_type=F32)


def dot_tn(a, b):
    return lax.dot_general(a, b, (((0,), (0,)), ((), ())), preferred_element_type=F32)


def iota(shape, dim):
    return lax.broadcasted_iota(jnp.int32, shape, dim)


def row_of(ref):
    return ref[...].reshape(1, ref.shape[0])


def norm_rows(rows, gain):
    center = rows - jnp.mean(rows, axis=-1, keepdims=True)
    inverse = lax.rsqrt(jnp.mean(center * center, axis=-1, keepdims=True) + EPSILON)
    unit = center * inverse
    return unit * gain, unit, inverse


def norm_back(grad_out, unit, inverse, gain):
    scaled = grad_out * gain
    mean_grad = jnp.mean(scaled, axis=-1, keepdims=True)
    mean_cross = jnp.mean(scaled * unit, axis=-1, keepdims=True)
    grad_in = inverse * (scaled - mean_grad - unit * mean_cross)
    return grad_in, jnp.sum(grad_out * unit, axis=0, keepdims=True)


class Pair(list):
    pass


def call(body, outs, name, scratch=(), loose=(), after=(), weight=1.0, limit=VMEM_LIMIT, loose_outs=False):
    vmem = pl.BlockSpec(memory_space=pltpu.VMEM)
    anywhere = pl.BlockSpec(memory_space=pl.ANY)

    def run(*args):
        flat = []
        for a in args:
            flat += a if isinstance(a, Pair) else [a[0] if isinstance(a, tuple) else a]
        given = list({id(a): a for a in flat}.values())
        index = [[id(g) for g in given].index(id(a)) for a in flat]

        def inner(*refs):
            held = []
            for a in args:
                at = index[sum(len(h) if isinstance(h, tuple) else 1 for h in held)]
                if isinstance(a, Pair):
                    nxt = index[sum(len(h) if isinstance(h, tuple) else 1 for h in held) + 1]
                    held.append((refs[at], refs[nxt]))
                elif isinstance(a, tuple):
                    held.append(refs[at].at[pl.ds(a[1] * a[2], a[2])])
                else:
                    held.append(refs[at])
            body(*held, *refs[len(given) + len(after) :])

        spaces = [anywhere if any(index[j] == i for j in loose) else vmem for i in range(len(given))]
        return pl.pallas_call(
            inner,
            out_shape=tuple(jax.ShapeDtypeStruct(s, d) for s, d in outs),
            in_specs=spaces + [anywhere] * len(after),
            out_specs=tuple(anywhere if loose_outs else vmem for _ in outs),
            scratch_shapes=list(scratch),
            compiler_params=pltpu.CompilerParams(vmem_limit_bytes=limit * 2**20),
            cost_estimate=pl.CostEstimate(
                flops=1 + int(weight * 1e9), bytes_accessed=1, transcendentals=0
            ),
            name=name,
        )(*given, *after)

    return run


def places(cap, rows, half, blk):
    k, j = iota((rows, rows), 0), iota((rows, rows), 1)
    cap_col = jnp.sum(jnp.where(k == j, cap, 0.0), axis=1, keepdims=True)
    rank_row = jnp.sum(jnp.where(k < j, cap_col, 0.0), axis=0, keepdims=True)
    rank_col = jnp.sum(jnp.where(j < k, cap, 0.0), axis=1, keepdims=True)
    at_row = iota((1, rows), 1).astype(F32)
    at_col = iota((rows, 1), 0).astype(F32)
    dest_row = jnp.where(cap > 0.5, rank_row, blk + at_row - rank_row)
    dest_col = jnp.where(cap_col > 0.5, rank_col, blk + at_col - rank_col)
    return dest_row.astype(jnp.int32), dest_col.astype(jnp.int32)


def sorted_rows(cot, cap, blk):
    rows = cot.shape[0]
    dest_row, _ = places(row_of(cap).astype(F32), rows, rows // 2, blk)
    pick = (iota((2 * blk, rows), 0) == dest_row).astype(BF16)
    c = dot_nn(pick, cot[...]).astype(BF16)
    return c[blk:], c[:blk]


def pre_body(
    tok_far, cot_far, cap_far, lens_far, gain2_far, cot_core, cap_core,
    xc, xn, n2n, cotn, cotc, cotn_core, cotc_core, bias,
    tok, cot, cap, lens, gain2, sems,
):
    pairs = ((cap_far, cap), (tok_far, tok), (lens_far, lens), (gain2_far, gain2), (cot_far, cot))
    copies = [pltpu.make_async_copy(a, b, sems.at[i]) for i, (a, b) in enumerate(pairs)]
    for c in copies:
        c.start()
    cotn_core[...], cotc_core[...] = sorted_rows(cot_core, cap_core, xc.shape[0])
    for c in copies:
        c.wait()
    rows = tok.shape[0]
    blk = xc.shape[0]
    dest_row, _ = places(row_of(cap).astype(F32), rows, rows // 2, blk)
    pick = (iota((2 * blk, rows), 0) == dest_row).astype(BF16)
    x = dot_nn(pick, tok[...])
    xc[...] = x[:blk].astype(BF16)
    xn[...] = x[blk:].astype(BF16)
    n2n[...] = norm_rows(x[blk:], row_of(gain2))[0].astype(BF16)
    c = dot_nn(pick, cot[...]).astype(BF16)
    cotn[...] = c[blk:]
    cotc[...] = c[:blk]
    position = iota((1, rows), 1)
    crop = jnp.ones((1, rows), F32)
    end = 0
    for s in range(lens.shape[1]):
        end = end + lens[0, s]
        crop = crop + (position >= end).astype(F32)
    crop_col = jnp.sum(jnp.where(iota((blk, rows), 0) == dest_row, crop, 0.0), axis=1, keepdims=True)
    crop_row = jnp.sum(
        jnp.where(iota((blk, blk), 0) == iota((blk, blk), 1), crop_col, 0.0), axis=0, keepdims=True
    )
    bias[...] = jnp.where(crop_col == crop_row, 0.0, NEGATIVE)


def sort_body(count, *refs):
    for cot, cap, left, right, out_c in zip(*(refs[k * count : (k + 1) * count] for k in range(5))):
        rows, out_c[...] = sorted_rows(cot, cap, out_c.shape[0])
        middle = left.shape[1]
        left[...], right[...] = rows[:, :middle], rows[:, middle:]


def halve_body(count, *refs):
    for array, left, right in zip(*(refs[k * count : (k + 1) * count] for k in range(3))):
        middle = left.shape[1]
        left[...], right[...] = array[:, :middle], array[:, middle:]


def half_mask(shape, e):
    return (iota(shape, 1) < HEAD_DIM) == (e == 0)


def fore_body(
    half,
    xc, bias, gain1, router, w_qkv, w_out, gain2,
    n1, qkv, probs, heads, attended, gate, n2c, stats,
):
    blk, width = xc.shape
    x = xc[...].astype(F32)
    low = norm_rows(x, row_of(gain1))[0].astype(BF16)
    n1[...] = low
    logit = jnp.sum(low.astype(F32) * row_of(router), axis=-1, keepdims=True)
    gated = jnp.where(iota((blk, 1), 0) < half, jax.nn.sigmoid(logit), 0.0)
    gate[...] = gated
    qkv[...] = dot_nn(low, w_qkv[...]).astype(BF16)
    scale = 1.0 / math.sqrt(HEAD_DIM)
    for pair in range(HEADS // 2):
        at = pair * PAIR
        q = qkv[:, at : at + PAIR]
        k = qkv[:, width + at : width + at + PAIR]
        v = qkv[:, 2 * width + at : 2 * width + at + PAIR]
        total = None
        for e in range(2):
            mask = half_mask((blk, PAIR), e)
            zero = jnp.zeros_like(q)
            scores = dot_nt(jnp.where(mask, q, zero), k) * scale + bias[...]
            exponent = jnp.exp(scores - jnp.max(scores, axis=-1, keepdims=True))
            prob = (exponent / jnp.sum(exponent, axis=-1, keepdims=True)).astype(BF16)
            probs[2 * pair + e] = prob
            part = dot_nn(prob, jnp.where(mask, v, zero))
            total = part if total is None else total + part
        heads[:, at : at + PAIR] = total.astype(BF16)
    att = dot_nn(heads[...], w_out[...])
    attended[...] = att
    branch = gated * att
    resid = x + branch
    n2c[...] = norm_rows(resid, row_of(gain2))[0].astype(BF16)
    stats[0:1, :] = jnp.sum(resid * resid, axis=0, keepdims=True)
    stats[1:2, :] = jnp.sum(branch * branch, axis=0, keepdims=True)


def mlp_body(blk, outs_at, n2s, cots, w_up, w_down, act, dpre, *outs):
    for s, (n2, cot) in enumerate(zip(n2s, cots)):
        rows = pl.ds(s * blk, blk)
        pre = dot_nn(whole(n2), w_up[...])
        d_act = dot_nt(whole(cot), w_down[...])
        square = pre * pre
        t = jnp.tanh(pre * (GELU_C + GELU_C * GELU_A * square))
        half_up = 0.5 + 0.5 * t
        slope = half_up + pre * (0.5 - 0.5 * t * t) * (GELU_C + 3.0 * GELU_C * GELU_A * square)
        a = (pre * half_up).astype(BF16)
        d = (d_act * slope).astype(BF16)
        act[rows, :] = a
        dpre[rows, :] = d
        (d_out, d_at), (h_out, h_at) = outs_at[s]
        outs[d_out][pl.ds(d_at, blk), :] = dot_nt(d, w_up[...]).astype(BF16)
        outs[h_out][pl.ds(h_at, blk), :] = dot_nn(a, w_down[...]).astype(BF16)


def copy_rows(sources, target):
    at = 0
    for ref in sources:
        rows = whole(ref)
        target[at : at + rows.shape[0]] = rows
        at += rows.shape[0]


def whole(ref):
    if isinstance(ref, tuple):
        return jnp.concatenate([r[...] for r in ref], axis=1)
    return ref[...]


def near_weights_body(act, dpre, n2s, cots, down, up, n2, cot):
    copy_rows(cots, cot)
    copy_rows(n2s, n2)
    down[...] = dot_tn(act[...], cot[...])
    up[...] = dot_tn(n2[...], dpre[...])


def weights_body(quarters, acts, dpres, n2s, cots, down, up, outs, act, dpre, n2, cot, total, grad_up):
    units = down.shape[0]
    part = units // quarters
    copy_rows(acts, act)
    copy_rows(cots, cot)
    total[...] = (down[...] + dot_tn(act[...], cot[...])).astype(BF16)
    copy_rows(dpres, dpre)
    copy_rows(n2s, n2)
    grad_up[...] = (up[...] + dot_tn(n2[...], dpre[...])).astype(BF16)
    lo = lax.rem(lax.axis_index("dp"), quarters)
    down_keep, down_send, up_keep, up_send = outs
    blocks = grad_up.shape[0] // units
    for p in range(quarters):
        first = lax.bitwise_xor(lo, p) * part
        target, at = (down_keep, down_send)[p % 2], p // 2 * part
        target[at : at + part] = total[pl.ds(pl.multiple_of(first, 16), part), :]
        target, at = (up_keep, up_send)[p // 2], p % 2 * part
        for k in range(blocks):
            row = pl.multiple_of(first * blocks + k * part, 16)
            target[at : at + part, k * units : (k + 1) * units] = grad_up[pl.ds(row, part), :]


def halves_body(down, down_got, up, up_got, kept, down_send, up_send):
    size = down_send.shape[0]
    a = down[...].astype(F32) + down_got[...].astype(F32)
    b = up[...].astype(F32) + up_got[...].astype(F32)
    kept[:size] = a[:size]
    kept[size:] = b[:size]
    down_send[...] = a[size:].astype(BF16)
    up_send[...] = b[size:].astype(BF16)


def own_body(kept, down_got, up_got, mine):
    size = down_got.shape[0]
    mine[:size] = (kept[:size] + down_got[...].astype(F32)).astype(BF16)
    mine[size:] = (kept[size:] + up_got[...].astype(F32)).astype(BF16)


def far_sum_body(d_c0, d_c1, n0, n1, h0, h1, joint, rest):
    def both(a, b):
        return (a[...].astype(F32) + b[...].astype(F32)).astype(BF16)

    joint[...] = both(d_c0, d_c1)
    size = n0.shape[0]
    rest[:size] = both(n0, n1)
    rest[size:] = both(h0, h1)


def add_body(count, *refs):
    total = refs[0][...].astype(F32)
    for ref in refs[1:count]:
        total = total + ref[...].astype(F32)
    refs[count][...] = total.astype(refs[count].dtype)


def spread_body(a, b, a_got, b_got, *outs):
    for own, other, both in ((a, a_got, outs[0]), (b, b_got, outs[1])):
        size = own.shape[0]
        both[:size] = own[...]
        both[size:] = other[...]


def assemble_body(long, short, down_far, up_far, mark, down, up, sems):
    units = up.shape[1]
    part = units // len(long)
    blocks = up.shape[0] // units
    lo = lax.rem(lax.axis_index("dp"), len(long))
    firsts = [lax.bitwise_xor(lo, p) * part for p in range(len(long))]
    for first, rows in zip(firsts, long):
        down[pl.ds(pl.multiple_of(first, 8), part), :] = rows[:part].astype(F32)
    down_copy = pltpu.make_async_copy(down, down_far, sems.at[0])
    down_copy.start()
    for first, *pieces in zip(firsts, long, short):
        offset = 0
        for rows in (pieces[0][part:].astype(F32), pieces[1][...].astype(F32)):
            for k in range(blocks):
                at = pl.multiple_of(first * blocks + k * part + offset, 8)
                up[pl.ds(at, rows.shape[0]), :] = rows[:, k * units : (k + 1) * units]
            offset += rows.shape[0]
    up_copy = pltpu.make_async_copy(up, up_far, sems.at[1])
    up_copy.start()
    down_copy.wait()
    up_copy.wait()


def back_body(
    half,
    d_n2_0, d_n2_1, d_n2_2, cc, xc, attended, gate, heads, qkv, probs, w_out, gain2,
    d_resid_out, d_qkv, d_att_out, d_logit_out, g_gain2,
):
    blk, width = xc.shape
    scale = 1.0 / math.sqrt(HEAD_DIM)
    gated = gate[...]
    att = attended[...]
    resid = xc[...].astype(F32) + gated * att
    _, unit2, inverse2 = norm_rows(resid, row_of(gain2))
    d_n2 = d_n2_0[...].astype(F32) + d_n2_1[...].astype(F32)
    for at in range(0, d_n2_2.shape[0], blk):
        d_n2 = d_n2 + d_n2_2[at : at + blk].astype(F32)
    back2, g_gain2[...] = norm_back(d_n2, unit2, inverse2, row_of(gain2))
    d_resid = cc[...].astype(F32) + back2
    d_resid_out[...] = d_resid
    d_att = (d_resid * gated).astype(BF16)
    keep = (iota((blk, 1), 0) < half).astype(F32)
    d_gate = keep * jnp.sum(d_resid * att, axis=-1, keepdims=True)
    d_logit_out[...] = d_gate * gated * (1.0 - gated)
    d_att_out[...] = d_att
    d_heads = dot_nt(d_att, w_out[...]).astype(BF16)
    for pair in range(HEADS // 2):
        at = pair * PAIR
        q = qkv[:, at : at + PAIR]
        k = qkv[:, width + at : width + at + PAIR]
        v = qkv[:, 2 * width + at : 2 * width + at + PAIR]
        d_o = d_heads[:, at : at + PAIR]
        zero = jnp.zeros_like(q)
        d_q = d_k = d_v = 0.0
        for e in range(2):
            mask = half_mask((blk, PAIR), e)
            d_oe = jnp.where(mask, d_o, zero)
            prob = probs[2 * pair + e]
            prob_f = prob.astype(F32)
            d_prob = dot_nt(d_oe, v)
            d_score = (
                prob_f * (d_prob - jnp.sum(prob_f * d_prob, axis=-1, keepdims=True))
            ).astype(BF16)
            d_v = d_v + dot_tn(prob, d_oe)
            d_q = d_q + dot_nn(d_score, jnp.where(mask, k, zero))
            d_k = d_k + dot_tn(d_score, jnp.where(mask, q, zero))
        d_qkv[:, at : at + PAIR] = (d_q * scale).astype(BF16)
        d_qkv[:, width + at : width + at + PAIR] = (d_k * scale).astype(BF16)
        d_qkv[:, 2 * width + at : 2 * width + at + PAIR] = d_v.astype(BF16)


def products_body(tsize, heads, n1, d_qkv, d_att, table, *outs):
    width = n1.shape[1]
    me = lax.axis_index("dp") * tsize + lax.axis_index("tensor")
    share = width // (tsize * lax.axis_size("dp"))
    mid = outs[0].shape[0]
    for side in range(2):
        source = lax.bitwise_xor(table[side : side + 1, :], me) * share + table[2:3, :]
        order = (iota((width, width), 0) == source).astype(BF16)
        low = dot_nn(n1[...], order).astype(BF16)
        keep, send = outs[2 * side : 2 * side + 2]
        for k in range(2):
            at = k * width
            if side and k:
                product = dot_tn(dot_nn(heads[...], order).astype(BF16), d_att[...])
            else:
                column = (2 * side + k) * width
                product = dot_tn(low, d_qkv[:, column : column + width])
            product = product.astype(BF16)
            keep[:, at : at + width] = product[:mid]
            send[:, at : at + width] = product[mid:]


def to_pair(sums):
    top = sums.astype(BF16)
    return jnp.concatenate([top, (sums - top.astype(F32)).astype(BF16)], axis=0)


def fold_pair(sums):
    used = sums[:SUMS]
    top = used.astype(BF16).astype(F32)
    middle = sums.shape[1] // 2
    blocks = [a[:, k : k + middle] for a in (top, used - top) for k in (0, middle)]
    return jnp.concatenate(blocks, axis=0).astype(BF16)


def unfold_pair(folded):
    wide = folded.astype(F32)
    a, b, c, d = (wide[k * SUMS : (k + 1) * SUMS] for k in range(4))
    return jnp.concatenate([a + c, b + d], axis=1)


def from_pair(pair):
    size = pair.shape[0] // 2
    return pair[:size].astype(F32) + pair[size:].astype(F32)


def add_split_body(count, pieces, *refs):
    total = refs[0][...].astype(F32)
    for ref in refs[1:count]:
        total = total + ref[...].astype(F32)
    size = total.shape[0] // pieces
    for p in range(pieces):
        refs[count + p][...] = total[p * size : (p + 1) * size].astype(refs[count + p].dtype)


def put_back(pick, rows):
    top = rows.astype(BF16)
    rest = (rows - top.astype(F32)).astype(BF16)
    return dot_nn(pick, top) + dot_nn(pick, rest)


def post_body(
    cap, d_n0, hid_c0, hid_n0, d_nx, hid_c1, hid_n1, rest,
    xc, xn, cn, attended, gate, d_resid_c, d_qkv, d_logit, n1, w_qkv, gain1, gain2, router, g_gain2c, stats1,
    mixed, grad_in, sums,
):
    rows = mixed.shape[0]
    blk = xc.shape[0]
    _, dest_col = places(row_of(cap).astype(F32), rows, rows // 2, blk)
    pick_c = (iota((rows, blk), 1) == dest_col).astype(BF16)
    pick_n = (iota((rows, blk), 1) + blk == dest_col).astype(BF16)
    x_c, x_n = xc[...].astype(F32), xn[...].astype(F32)

    d_n1 = dot_nt(d_qkv[...], w_qkv[...]) + d_logit[...] * row_of(router)
    _, unit1, inverse1 = norm_rows(x_c, row_of(gain1))
    back1, g_gain1 = norm_back(d_n1, unit1, inverse1, row_of(gain1))
    grad_c = d_resid_c[...] + back1

    def summed(first, second, others, start, stop):
        total = first[...].astype(F32) + second[...].astype(F32)
        for o in range(start, stop, blk):
            total = total + others[o : o + blk].astype(F32)
        return total

    third = rest.shape[0] // 3
    d_n2n = summed(d_n0, d_nx, rest, 0, third)
    h_n = summed(hid_n0, hid_n1, rest, third, 2 * third)
    h_c = summed(hid_c0, hid_c1, rest, 2 * third, 3 * third)
    mix_c = (x_c + gate[...] * attended[...] + h_c).astype(BF16)
    mix_n = (x_n + h_n).astype(BF16)
    mixed[...] = (dot_nn(pick_c, mix_c) + dot_nn(pick_n, mix_n)).astype(BF16)
    _, unit, inverse = norm_rows(x_n, row_of(gain2))
    back, g_gain2n = norm_back(d_n2n, unit, inverse, row_of(gain2))
    d_resid_n = cn[...].astype(F32) + back
    grad_in[...] = put_back(pick_c, grad_c) + put_back(pick_n, d_resid_n)

    def over_rows(a):
        return jnp.sum(a, axis=0, keepdims=True)

    sums[...] = jnp.zeros_like(sums)
    sums[0:1, :] = g_gain1
    sums[1:2, :] = over_rows(d_logit[...] * n1[...].astype(F32))
    sums[2:3, :] = g_gain2c[...] + g_gain2n
    sums[3:4, :] = stats1[0:1, :] + over_rows(x_n * x_n)
    sums[4:5, :] = stats1[1:2, :]
    sums[5:6, :] = over_rows(h_c * h_c) + over_rows(h_n * h_n)


CORES = 2
GROUP = 4
SUMS = 6
PARTS = 1
W_MLP1 = 10.0
W_MLP2 = 0.0
W_LAST = 5.0
W_ATT4 = 20.0


def swap(name, array, axis, size, bits):
    with jax.named_scope(name):
        return lax.ppermute(array, axis, [(t, t ^ bits) for t in range(size)])


def add(name, arrays, after=(), weight=1.0):
    return call(
        lambda *refs: add_body(len(arrays), *refs),
        [(arrays[0].shape, BF16)],
        name,
        after=after,
        weight=weight,
    )(*arrays)[0]


def in_order(name, own, others, place, cut, after):
    if len(others) > 1:
        held = jnp.stack([own, *others])
        own, *others = [
            lax.dynamic_index_in_dim(held, place ^ at, 0, keepdims=False) for at in range(len(held))
        ]

    def body(*refs):
        total = refs[0][...].astype(F32)
        for ref in refs[1:-2]:
            total = total + ref[...].astype(F32)
        refs[-2][...] = total[:cut].astype(BF16)
        refs[-1][...] = total[cut:].astype(BF16)

    rows, columns = own.shape
    return call(
        body, [((cut, columns), BF16), ((rows - cut, columns), BF16)], name, after=after, weight=W_MLP2
    )(own, *others)


def shards(
    tokens, lengths, capacity, norm1_gain, router, w_qkv, w_out, norm2_gain, w_up, w_down, cotangent
):
    rows, width = tokens.shape
    half = rows // 2
    blk = -(-half // 16) * 16
    units = w_up.shape[1]
    tsize, dsize = lax.axis_size("tensor"), lax.axis_size("dp")
    ysize = tsize // CORES
    others = range(1, ysize)
    cap, gain1, gain2, route = capacity, norm1_gain, norm2_gain, router
    small = (blk, width)

    def far(name, array):
        return [swap("y_" + name, array, "tensor", tsize, dy * CORES) for dy in others]

    def across(name, array):
        return swap("core_" + name, array, "tensor", tsize, 1)

    cap_far, cot_far = far("cap", cap), far("cot", cotangent)
    xc, xn, n2n, cotn, cotc, cotn_core, cotc_core, bias = call(
        pre_body,
        [(small, BF16)] * 7 + [((blk, blk), F32)],
        "pre",
        scratch=[
            pltpu.VMEM(tokens.shape, BF16), pltpu.VMEM(cotangent.shape, BF16), pltpu.VMEM(cap.shape, jnp.int32),
            pltpu.SMEM(lengths.shape, jnp.int32), pltpu.VMEM(gain2.shape, F32), pltpu.SemaphoreType.DMA((5,)),
        ],
        loose=range(5),
        after=cap_far,
        weight=20.0,
    )(tokens, cotangent, cap, lengths, gain2, across("cot", cotangent), across("cap", cap))

    def group(name, pieces):
        return [swap("xz_" + name, pieces[p], "dp", dsize, p) for p in range(1, GROUP)]

    def high(name, pieces):
        return [
            swap("zz_" + name, pieces[p % len(pieces)], "dp", dsize, p * GROUP)
            for p in range(1, dsize // GROUP)
        ]

    n2n_far, n2n_core = far("n2n", n2n), across("n2n", n2n)

    n1, qkv, probs, heads, attended, gate, n2c, stats1 = call(
        lambda *refs: fore_body(half, *refs),
        [
            (small, BF16), ((blk, 3 * width), BF16), ((HEADS, blk, blk), BF16), (small, BF16),
            (small, F32), ((blk, 1), F32), (small, BF16), ((2, width), F32),
        ],
        "fore",
    )(xc, bias, gain1, route, w_qkv, w_out, gain2)

    n2c_far, n2c_core = far("n2c", n2c), across("n2c", n2c)

    def mlp(name, n2s, cots, outs, outs_at, after=(), weight=1.0):
        tall = blk * len(outs_at)
        count = len(n2s)
        return call(
            lambda *refs: mlp_body(
                blk, outs_at, refs[:count], refs[count : 2 * count], *refs[2 * count :]
            ),
            [((tall, units), BF16)] * 2 + [((n * blk, width), BF16) for n in outs],
            name,
            after=after,
            weight=weight,
        )(*n2s, *cots, w_up, w_down)

    n2_near = [n2c, n2n, n2c_core, n2n_core]
    cot_near = [cotc, cotn, cotc_core, cotn_core]
    at_near = [((c, k * blk), (c, (2 + k) * blk)) for c in range(CORES) for k in range(2)]
    act_a, dpre_a, near_0, near_1 = mlp("mlp_near", n2_near, cot_near, [4, 4], at_near)
    near_1 = across("near", near_1)

    def tie(name, arrays, after):
        return list(
            pl.pallas_call(
                lambda *refs: None,
                out_shape=tuple(jax.ShapeDtypeStruct(a.shape, a.dtype) for a in arrays),
                in_specs=[pl.BlockSpec(memory_space=pl.ANY)] * (len(arrays) + len(after)),
                out_specs=tuple(pl.BlockSpec(memory_space=pl.ANY) for _ in arrays),
                input_output_aliases={i: i for i in range(len(arrays))},
                compiler_params=pltpu.CompilerParams(vmem_limit_bytes=2**20),
                name=name,
            )(*arrays, *after)
        )

    count = len(cot_far)
    slim = (blk, width // 2)
    sorted_far = call(
        lambda *refs: sort_body(count, *refs),
        [(slim, BF16)] * (2 * count) + [(small, BF16)] * count,
        "sort_far",
        after=[act_a],
        weight=0.0,
    )(*cot_far, *cap_far)
    cotn_far = [Pair(sorted_far[i : 2 * count : count]) for i in range(count)]
    cotc_far = list(sorted_far[2 * count :])
    cotn_all = cotn_far + [Pair([across("far_cotn", a) for a in p]) for p in cotn_far]
    halves = call(
        lambda *refs: halve_body(count, *refs),
        [(slim, BF16)] * (2 * count),
        "halve_n2n",
        after=[a for p in cotn_all[count:] for a in p],
        weight=0.0,
    )(*n2n_far)
    n2n_far = [Pair(halves[i::count]) for i in range(count)]
    n2n_all = n2n_far + [Pair([across("far_n2n", a) for a in p]) for p in n2n_far]
    cotc_all = cotc_far + [across("far_cotc", a) for a in cotc_far]

    tall = 4 * blk
    down_near, up_near = call(
        lambda act, dpre, *refs: near_weights_body(act, dpre, refs[:4], refs[4:8], *refs[8:]),
        [((units, width), F32), ((width, units), F32)],
        "weights_near",
        scratch=[pltpu.VMEM((tall, width), BF16)] * 2,
        after=n2n_far[0][:1],
        weight=0.0,
    )(act_a, dpre_a, *n2_near, *cot_near)


    far_at = range(CORES * (ysize - 1))
    place = lambda s: (s // (ysize - 1), s % (ysize - 1) * blk)
    act_n, dpre_n, far_n0, far_n1 = mlp(
        "mlp_far_n", n2n_all, cotn_all, [2 * (ysize - 1)] * 2,
        [(place(s), (place(s)[0], place(s)[1] + (ysize - 1) * blk)) for s in far_at],
        [down_near], 0.0,
    )
    far_n1 = across("far_n", far_n1)
    n2c_far = tie("tie_c", n2c_far, [act_n, *cotc_all[count:]])
    n2c_all = n2c_far + [across("far_n2c", a) for a in n2c_far]
    def far_c(name, n2s, cots, after=()):
        outs_at = [((0, i * blk), (1, i * blk)) for i in range(len(n2s))]
        return mlp(name, n2s, cots, [len(n2s)] * 2, outs_at, after)

    count = ysize - 1
    act_c0, dpre_c0, d_c0, hid_c0 = far_c("mlp_far_c0", n2c_all[:count], cotc_all[:count])
    act_c1, dpre_c1, d_c1, hid_c1 = far_c("mlp_far_c1", n2c_all[count:], cotc_all[count:], [act_c0])
    d_c1, hid_c1 = across("d_c", d_c1), across("hid_c", hid_c1)

    def send_back(name, joint, groups):
        if ysize == 2:
            return swap("y_" + name, joint, "tensor", tsize, CORES)
        cut = joint.reshape(groups, ysize - 1, blk, width)
        got = [swap("y_" + name, cut[:, dy - 1], "tensor", tsize, dy * CORES) for dy in others]
        return jnp.stack(got, axis=1).reshape(joint.shape)

    cots, n2s = cotn_all + cotc_all, n2n_all + n2c_all
    count, tall = len(cots), len(cots) * blk
    part = units // GROUP

    def weights(*refs):
        acts, dpres, refs = refs[:3], refs[3:6], refs[6:]
        n2s, cots, refs = refs[:count], refs[count : 2 * count], refs[2 * count :]
        weights_body(
            GROUP, acts, dpres, n2s, cots, *refs[:2], refs[2:6], *refs[6:]
        )

    down_keep, down_got, up_keep, up_got = call(
        weights,
        [((2 * part, width), BF16)] * 4,
        "weights",
        scratch=[
            pltpu.VMEM((tall, units), BF16), pltpu.VMEM((tall, units), BF16),
            pltpu.VMEM((tall, width), BF16), pltpu.VMEM((tall, width), BF16),
            pltpu.VMEM((units, width), BF16), pltpu.VMEM((width, units), BF16),
        ],
        after=[],
    )(act_n, act_c0, act_c1, dpre_n, dpre_c0, dpre_c1, *n2s, *cots, down_near, up_near)
    mark = down_keep
    down_got = swap("xz_down", down_got, "dp", dsize, 1)
    up_got = swap("zx_up", up_got, "dp", dsize, 2)
    joint, rest = call(
        far_sum_body,
        [(((ysize - 1) * blk, width), BF16), ((3 * (ysize - 1) * blk, width), BF16)],
        "far_sum",
        after=[mark],
    )(d_c0, d_c1, far_n0, far_n1, hid_c0, hid_c1)
    d_c2 = send_back("d_c", joint, 1)
    rest = send_back("rest", rest, 3)

    mark = joint

    shares = tsize * dsize
    share = width // shares
    def owners(y_first):
        table = []
        for core in range(CORES):
            for first in range(ysize if y_first else 2):
                for then in range(2 if y_first else ysize):
                    y, x = (first, then) if y_first else (then, first)
                    for z in range(2):
                        for hi in range(dsize // GROUP):
                            place = (hi * GROUP + z * 2 + x) * tsize + y * CORES + core
                            table += [place] * share
        return table

    table = jnp.array([owners(True), owners(False), list(range(share)) * shares], jnp.int32)
    d_resid_c, d_qkv, d_att, d_logit, g_gain2c = call(
        lambda *refs: back_body(half, *refs),
        [
            (small, F32), ((blk, 3 * width), BF16), (small, BF16), ((blk, 1), F32), ((1, width), F32),
        ],
        "back",
        after=[mark],
        weight=20.0,
    )(
        (near_0, 0, blk), (near_1, 0, blk), d_c2, cotc, xc, attended, gate, heads, qkv, probs,
        w_out, gain2,
    )
    kept, down_got, up_got = call(
        halves_body,
        [((2 * part, width), F32), ((part, width), BF16), ((part, width), BF16)],
        "mlp_0",
        after=[d_resid_c],
        weight=0.0,
    )(down_keep, down_got, up_keep, up_got)
    mark = kept
    down_got = swap("xz_down", down_got, "dp", dsize, 2)
    up_got = swap("zx_up", up_got, "dp", dsize, 1)

    left, left_got, right, right_got = call(
        lambda *refs: products_body(tsize, *refs),
        [((width // 2, 2 * width), BF16)] * 4,
        "products",
        after=[mark],
    )(heads, n1, d_qkv, d_att, table)
    left_got, right_got = across("left", left_got), across("right", right_got)

    def sums_of(name, *sets, after=(), along=(), weight=1.0):
        given = [a for arrays, _ in sets for a in arrays]

        def body(*refs):
            ins, outs = list(refs[: len(given)]), list(refs[len(given) + len(along) :])
            if along:
                outs[-1][...] = refs[len(given)][...] + refs[len(given) + 1][...]
            for arrays, count in sets:
                add_split_body(len(arrays), count, *ins[: len(arrays)], *outs[:count])
                del ins[: len(arrays)], outs[:count]

        shapes = []
        for arrays, count in sets:
            rows, columns = arrays[0].shape
            shapes += [((rows // count, columns), BF16)] * count
        shapes += [(a.shape, a.dtype) for a in along[:1]]
        return call(body, shapes, name, after=after, weight=weight)(*given, *along)

    mine = call(
        own_body, [((2 * part, width), BF16)], "mlp_1", after=[left], weight=W_MLP1
    )(kept, down_got, up_got)
    mine_got = [high("mlp", mine)]

    *left, right, right_got = sums_of(
        "att_1", ([left, left_got], ysize), ([right, right_got], 2), after=[mine[0], rest]
    )
    left_got = [swap("y_left", left[p], "tensor", tsize, p * CORES) for p in others]
    right_got = swap("x_right", right_got, "dp", dsize, 1)

    mixed, grad_input, sums = call(
        post_body,
        [((rows, width), BF16), ((rows, width), F32), ((8, width), F32)],
        "post",
        after=[right],
        weight=20.0,
    )(
        cap, (near_0, 1, blk), (near_0, 2, blk), (near_0, 3, blk), (near_1, 1, blk), (near_1, 2, blk),
        (near_1, 3, blk), rest,
        xc, xn, cotn, attended, gate, d_resid_c, d_qkv, d_logit, n1, w_qkv, gain1, gain2, route, g_gain2c,
        stats1,
    )

    step = 1
    while step < tsize // 2:
        sums = sums + swap("sums", sums, "tensor", tsize, step)
        step *= 2
    sums_got = swap("sums", sums, "tensor", tsize, step)

    right = sums_of("right_2", ([right, right_got], ysize), after=[sums], weight=0.0)
    right_got = [swap("y_right", right[p], "tensor", tsize, p * CORES) for p in others]
    low_rows = 2 * sums.shape[0]

    def left_body(*refs):
        *ins, a, b, kept, sent, sums_out = refs
        total = ins[0][...].astype(F32)
        for ref in ins[1:]:
            total = total + ref[...].astype(F32)
        size = kept.shape[0]
        kept[...] = total[:size].astype(BF16)
        sent[:size] = total[size:].astype(BF16)
        sent[size:] = jnp.zeros_like(sent[size:])
        sums_out[...] = to_pair(a[...] + b[...])
        sent[size:, : sums_out.shape[1]] = sums_out[...]

    size = left[0].shape[0] // 2
    left, left_got, sums = call(
        left_body,
        [((size, 2 * width), BF16), ((size + low_rows, 2 * width), BF16), ((low_rows, width), BF16)],
        "left_2",
        after=[right[0]],
        weight=0.0,
    )(left[0], *left_got, sums, sums_got)
    left_got = swap("x_left", left_got, "dp", dsize, 1)

    cut = 2 * part * 2 // 3
    mine = in_order("mlp_2", mine[0], mine_got[0], lax.axis_index("dp") // GROUP, cut, [left])
    mine_got = [swap("zx_long", mine[0], "dp", dsize, 2), swap("xz_short", mine[1], "dp", dsize, 1)]

    highs = dsize // GROUP

    def join_body(*refs):
        (left, left_got, *rights), sums, outs = refs[: -2 * highs - 1], refs[-2 * highs - 1], refs[-2 * highs :]
        size = left.shape[0]
        middle = left.shape[1]
        pair = fold_pair(from_pair(sums[...]) + from_pair(left_got[size:, : sums.shape[1]]))
        totals = [left[...].astype(F32) + left_got[:size].astype(F32), rights[0][...].astype(F32)]
        for ref in rights[1:]:
            totals[1] = totals[1] + ref[...].astype(F32)
        for p, out in enumerate(outs):
            for k, total in enumerate(totals):
                out[:share, k * middle : (k + 1) * middle] = total[p * share : (p + 1) * share].astype(BF16)
            out[: pair.shape[0], 2 * middle :] = pair

    att = call(
        join_body,
        [((max(share, 4 * SUMS), 4 * width + width // 2), BF16)] * (2 * highs),
        "att_3",
        after=[mine[0]],
        weight=20.0,
    )(left, left_got, right[0], *right_got, sums)
    long_rest, short_rest = call(
        spread_body,
        [((2 * a.shape[0], width), BF16) for a in mine],
        "pairs",
        after=att[:1],
        weight=0.0,
    )(*mine, *mine_got)
    att = [att[0]] + tie("tie_att", att[1:], [long_rest])
    att_got = [
        swap("z_att", att[p], "dp", dsize, p // highs * 2 + p % highs * GROUP)
        for p in range(1, 2 * highs)
    ]
    long_rest = swap("zx_long", long_rest, "dp", dsize, 1)
    short_rest = swap("xz_short", short_rest, "dp", dsize, 2)

    g_down, g_up, mark = call(
        lambda a0, a2, a13, b0, b1, b23, *refs: assemble_body(
            (a0, a13.at[pl.ds(0, cut)], a2, a13.at[pl.ds(cut, cut)]),
            (b0, b1, b23.at[pl.ds(0, 2 * part - cut)], b23.at[pl.ds(2 * part - cut, 2 * part - cut)]),
            *refs,
        ),
        [((units, width), F32), ((width, units), F32), ((8, 128), F32)],
        "assemble",
        scratch=[
            pltpu.VMEM((units, width), F32), pltpu.VMEM((width, units), F32), pltpu.SemaphoreType.DMA((2,)),
        ],
        weight=W_LAST,
        loose_outs=True,
        after=att[1:2],
    )(mine[0], mine_got[0], long_rest, mine[1], mine_got[1], short_rest)

    count = rows * width * dsize * tsize

    def att_body(*refs):
        ins, outs = refs[: 2 * highs], refs[2 * highs :]
        out_qkv, out_proj, out_gain1, out_router, out_gain2, norms = outs
        total = ins[0][:share, : 4 * width].astype(F32)
        for ref in ins[1:]:
            total = total + ref[:share, : 4 * width].astype(F32)
        out_qkv[...] = total[:, : 3 * width]
        out_proj[...] = total[:, 3 * width :]
        sums = [unfold_pair(ref[: 4 * SUMS, 4 * width :]) for ref in ins]
        while len(sums) > 1:
            sums = [a + b for a, b in zip(sums[::2], sums[1::2])]
        for k, out in enumerate((out_gain1, out_router, out_gain2)):
            out[...] = sums[0][k : k + 1, :].reshape(width)
        norms[...] = jnp.sqrt(jnp.sum(sums[0][3:6, :], axis=-1) / count)

    g_qkv, g_proj, g_gain1, g_router, g_gain2, norms = call(
        att_body,
        [((share, 3 * width), F32), ((share, width), F32)] + [((width,), F32)] * 3 + [((3,), F32)],
        "att_4",
        weight=W_ATT4,
        after=[mark],
    )(att[0], *att_got)

    return (
        mixed, grad_input, g_gain1, g_router, g_qkv, g_proj, g_gain2, g_up, g_down, norms,
    )


def solution(mesh):
    return jax.shard_map(
        shards,
        mesh=mesh,
        in_specs=(
            P(("dp", "tensor"), None),
            P(("dp", "tensor"), None),
            P(("dp", "tensor")),
            P(),
            P(),
            P(),
            P(),
            P(),
            P(None, "tensor"),
            P("tensor", None),
            P(("dp", "tensor"), None),
        ),
        out_specs=(
            P(("dp", "tensor"), None),
            P(("dp", "tensor"), None),
            P(),
            P(),
            P(("dp", "tensor"), None),
            P(("dp", "tensor"), None),
            P(),
            P(None, "tensor"),
            P("tensor", None),
            P(),
        ),
        check_vma=False,
    )
```

```python
import math

import jax
import jax.numpy as jnp
from jax import lax
from jax.experimental import pallas as pl
from jax.experimental.pallas import tpu as pltpu
from jax.sharding import PartitionSpec as P

HEADS = 12
HEAD_DIM = 64
PAIR = 2 * HEAD_DIM
EPSILON = 1e-06
NEGATIVE = -1000000000.0
GELU_C = math.sqrt(2.0 / math.pi)
GELU_A = 0.044715
F32 = jnp.float32
BF16 = jnp.bfloat16
VMEM_LIMIT = 24


def dot_nn(a, b):
    return lax.dot_general(a, b, (((1,), (0,)), ((), ())), preferred_element_type=F32)


def dot_nt(a, b):
    return lax.dot_general(a, b, (((1,), (1,)), ((), ())), preferred_element_type=F32)


def dot_tn(a, b):
    return lax.dot_general(a, b, (((0,), (0,)), ((), ())), preferred_element_type=F32)


def iota(shape, dim):
    return lax.broadcasted_iota(jnp.int32, shape, dim)


def row_of(ref):
    return ref[...].reshape(1, ref.shape[0])


def norm_rows(rows, gain):
    center = rows - jnp.mean(rows, axis=-1, keepdims=True)
    inverse = lax.rsqrt(jnp.mean(center * center, axis=-1, keepdims=True) + EPSILON)
    unit = center * inverse
    return unit * gain, unit, inverse


def norm_back(grad_out, unit, inverse, gain):
    scaled = grad_out * gain
    mean_grad = jnp.mean(scaled, axis=-1, keepdims=True)
    mean_cross = jnp.mean(scaled * unit, axis=-1, keepdims=True)
    grad_in = inverse * (scaled - mean_grad - unit * mean_cross)
    return grad_in, jnp.sum(grad_out * unit, axis=0, keepdims=True)


class Pair(list):
    pass


def call(body, outs, name, scratch=(), loose=(), after=(), weight=1.0, limit=VMEM_LIMIT, loose_outs=False):
    vmem = pl.BlockSpec(memory_space=pltpu.VMEM)
    anywhere = pl.BlockSpec(memory_space=pl.ANY)

    def run(*args):
        flat = []
        for a in args:
            flat += a if isinstance(a, Pair) else [a[0] if isinstance(a, tuple) else a]
        given = list({id(a): a for a in flat}.values())
        index = [[id(g) for g in given].index(id(a)) for a in flat]

        def inner(*refs):
            held = []
            for a in args:
                at = index[sum(len(h) if isinstance(h, tuple) else 1 for h in held)]
                if isinstance(a, Pair):
                    nxt = index[sum(len(h) if isinstance(h, tuple) else 1 for h in held) + 1]
                    held.append((refs[at], refs[nxt]))
                elif isinstance(a, tuple):
                    held.append(refs[at].at[pl.ds(a[1] * a[2], a[2])])
                else:
                    held.append(refs[at])
            body(*held, *refs[len(given) + len(after) :])

        spaces = [anywhere if any(index[j] == i for j in loose) else vmem for i in range(len(given))]
        return pl.pallas_call(
            inner,
            out_shape=tuple(jax.ShapeDtypeStruct(s, d) for s, d in outs),
            in_specs=spaces + [anywhere] * len(after),
            out_specs=tuple(anywhere if loose_outs else vmem for _ in outs),
            scratch_shapes=list(scratch),
            compiler_params=pltpu.CompilerParams(vmem_limit_bytes=limit * 2**20),
            cost_estimate=pl.CostEstimate(
                flops=1 + int(weight * 1e9), bytes_accessed=1, transcendentals=0
            ),
            name=name,
        )(*given, *after)

    return run


def places(cap, rows, half, blk):
    k, j = iota((rows, rows), 0), iota((rows, rows), 1)
    cap_col = jnp.sum(jnp.where(k == j, cap, 0.0), axis=1, keepdims=True)
    rank_row = jnp.sum(jnp.where(k < j, cap_col, 0.0), axis=0, keepdims=True)
    rank_col = jnp.sum(jnp.where(j < k, cap, 0.0), axis=1, keepdims=True)
    at_row = iota((1, rows), 1).astype(F32)
    at_col = iota((rows, 1), 0).astype(F32)
    dest_row = jnp.where(cap > 0.5, rank_row, blk + at_row - rank_row)
    dest_col = jnp.where(cap_col > 0.5, rank_col, blk + at_col - rank_col)
    return dest_row.astype(jnp.int32), dest_col.astype(jnp.int32)


def sorted_rows(cot, cap, blk):
    rows = cot.shape[0]
    dest_row, _ = places(row_of(cap).astype(F32), rows, rows // 2, blk)
    pick = (iota((2 * blk, rows), 0) == dest_row).astype(BF16)
    c = dot_nn(pick, cot[...]).astype(BF16)
    return c[blk:], c[:blk]


def pre_body(
    tok_far, cot_far, cap_far, lens_far, gain2_far, cot_core, cap_core,
    xc, xn, n2n, cotn, cotc, cotn_core, cotc_core, bias,
    tok, cot, cap, lens, gain2, sems,
):
    pairs = ((cap_far, cap), (tok_far, tok), (lens_far, lens), (gain2_far, gain2), (cot_far, cot))
    copies = [pltpu.make_async_copy(a, b, sems.at[i]) for i, (a, b) in enumerate(pairs)]
    for c in copies:
        c.start()
    cotn_core[...], cotc_core[...] = sorted_rows(cot_core, cap_core, xc.shape[0])
    for c in copies:
        c.wait()
    rows = tok.shape[0]
    blk = xc.shape[0]
    dest_row, _ = places(row_of(cap).astype(F32), rows, rows // 2, blk)
    pick = (iota((2 * blk, rows), 0) == dest_row).astype(BF16)
    x = dot_nn(pick, tok[...])
    xc[...] = x[:blk].astype(BF16)
    xn[...] = x[blk:].astype(BF16)
    n2n[...] = norm_rows(x[blk:], row_of(gain2))[0].astype(BF16)
    c = dot_nn(pick, cot[...]).astype(BF16)
    cotn[...] = c[blk:]
    cotc[...] = c[:blk]
    position = iota((1, rows), 1)
    crop = jnp.ones((1, rows), F32)
    end = 0
    for s in range(lens.shape[1]):
        end = end + lens[0, s]
        crop = crop + (position >= end).astype(F32)
    crop_col = jnp.sum(jnp.where(iota((blk, rows), 0) == dest_row, crop, 0.0), axis=1, keepdims=True)
    crop_row = jnp.sum(
        jnp.where(iota((blk, blk), 0) == iota((blk, blk), 1), crop_col, 0.0), axis=0, keepdims=True
    )
    bias[...] = jnp.where(crop_col == crop_row, 0.0, NEGATIVE)


def sort_body(count, *refs):
    for cot, cap, left, right, out_c in zip(*(refs[k * count : (k + 1) * count] for k in range(5))):
        rows, out_c[...] = sorted_rows(cot, cap, out_c.shape[0])
        middle = left.shape[1]
        left[...], right[...] = rows[:, :middle], rows[:, middle:]


def halve_body(count, *refs):
    for array, left, right in zip(*(refs[k * count : (k + 1) * count] for k in range(3))):
        middle = left.shape[1]
        left[...], right[...] = array[:, :middle], array[:, middle:]


def half_mask(shape, e):
    return (iota(shape, 1) < HEAD_DIM) == (e == 0)


def fore_body(
    half,
    xc, bias, gain1, router, w_qkv, w_out, gain2,
    n1, qkv, probs, heads, attended, gate, n2c, stats,
):
    blk, width = xc.shape
    x = xc[...].astype(F32)
    low = norm_rows(x, row_of(gain1))[0].astype(BF16)
    n1[...] = low
    logit = jnp.sum(low.astype(F32) * row_of(router), axis=-1, keepdims=True)
    gated = jnp.where(iota((blk, 1), 0) < half, jax.nn.sigmoid(logit), 0.0)
    gate[...] = gated
    qkv[...] = dot_nn(low, w_qkv[...]).astype(BF16)
    scale = 1.0 / math.sqrt(HEAD_DIM)
    for pair in range(HEADS // 2):
        at = pair * PAIR
        q = qkv[:, at : at + PAIR]
        k = qkv[:, width + at : width + at + PAIR]
        v = qkv[:, 2 * width + at : 2 * width + at + PAIR]
        total = None
        for e in range(2):
            mask = half_mask((blk, PAIR), e)
            zero = jnp.zeros_like(q)
            scores = dot_nt(jnp.where(mask, q, zero), k) * scale + bias[...]
            exponent = jnp.exp(scores - jnp.max(scores, axis=-1, keepdims=True))
            prob = (exponent / jnp.sum(exponent, axis=-1, keepdims=True)).astype(BF16)
            probs[2 * pair + e] = prob
            part = dot_nn(prob, jnp.where(mask, v, zero))
            total = part if total is None else total + part
        heads[:, at : at + PAIR] = total.astype(BF16)
    att = dot_nn(heads[...], w_out[...])
    attended[...] = att
    branch = gated * att
    resid = x + branch
    n2c[...] = norm_rows(resid, row_of(gain2))[0].astype(BF16)
    stats[0:1, :] = jnp.sum(resid * resid, axis=0, keepdims=True)
    stats[1:2, :] = jnp.sum(branch * branch, axis=0, keepdims=True)


def mlp_body(blk, outs_at, n2s, cots, w_up, w_down, act, dpre, *outs):
    for s, (n2, cot) in enumerate(zip(n2s, cots)):
        rows = pl.ds(s * blk, blk)
        pre = dot_nn(whole(n2), w_up[...])
        d_act = dot_nt(whole(cot), w_down[...])
        square = pre * pre
        t = jnp.tanh(pre * (GELU_C + GELU_C * GELU_A * square))
        half_up = 0.5 + 0.5 * t
        slope = half_up + pre * (0.5 - 0.5 * t * t) * (GELU_C + 3.0 * GELU_C * GELU_A * square)
        a = (pre * half_up).astype(BF16)
        d = (d_act * slope).astype(BF16)
        act[rows, :] = a
        dpre[rows, :] = d
        (d_out, d_at), (h_out, h_at) = outs_at[s]
        outs[d_out][pl.ds(d_at, blk), :] = dot_nt(d, w_up[...]).astype(BF16)
        outs[h_out][pl.ds(h_at, blk), :] = dot_nn(a, w_down[...]).astype(BF16)


def copy_rows(sources, target):
    at = 0
    for ref in sources:
        rows = whole(ref)
        target[at : at + rows.shape[0]] = rows
        at += rows.shape[0]


def whole(ref):
    if isinstance(ref, tuple):
        return jnp.concatenate([r[...] for r in ref], axis=1)
    return ref[...]


def near_weights_body(act, dpre, n2s, cots, down, up, n2, cot):
    copy_rows(cots, cot)
    copy_rows(n2s, n2)
    down[...] = dot_tn(act[...], cot[...])
    up[...] = dot_tn(n2[...], dpre[...])


def weights_body(quarters, acts, dpres, n2s, cots, down, up, outs, act, dpre, n2, cot, total, grad_up):
    units = down.shape[0]
    part = units // quarters
    copy_rows(acts, act)
    copy_rows(cots, cot)
    total[...] = (down[...] + dot_tn(act[...], cot[...])).astype(BF16)
    copy_rows(dpres, dpre)
    copy_rows(n2s, n2)
    grad_up[...] = (up[...] + dot_tn(n2[...], dpre[...])).astype(BF16)
    lo = lax.rem(lax.axis_index("dp"), quarters)
    down_keep, down_send, up_keep, up_send = outs
    blocks = grad_up.shape[0] // units
    for p in range(quarters):
        first = lax.bitwise_xor(lo, p) * part
        target, at = (down_keep, down_send)[p % 2], p // 2 * part
        target[at : at + part] = total[pl.ds(pl.multiple_of(first, 16), part), :]
        target, at = (up_keep, up_send)[p // 2], p % 2 * part
        for k in range(blocks):
            row = pl.multiple_of(first * blocks + k * part, 16)
            target[at : at + part, k * units : (k + 1) * units] = grad_up[pl.ds(row, part), :]


def halves_body(down, down_got, up, up_got, kept, down_send, up_send):
    size = down_send.shape[0]
    a = down[...].astype(F32) + down_got[...].astype(F32)
    b = up[...].astype(F32) + up_got[...].astype(F32)
    kept[:size] = a[:size]
    kept[size:] = b[:size]
    down_send[...] = a[size:].astype(BF16)
    up_send[...] = b[size:].astype(BF16)


def own_body(kept, down_got, up_got, mine):
    size = down_got.shape[0]
    mine[:size] = (kept[:size] + down_got[...].astype(F32)).astype(BF16)
    mine[size:] = (kept[size:] + up_got[...].astype(F32)).astype(BF16)


def far_sum_body(d_c0, d_c1, n0, n1, h0, h1, joint, rest):
    def both(a, b):
        return (a[...].astype(F32) + b[...].astype(F32)).astype(BF16)

    joint[...] = both(d_c0, d_c1)
    size = n0.shape[0]
    rest[:size] = both(n0, n1)
    rest[size:] = both(h0, h1)


def add_body(count, *refs):
    total = refs[0][...].astype(F32)
    for ref in refs[1:count]:
        total = total + ref[...].astype(F32)
    refs[count][...] = total.astype(refs[count].dtype)


def spread_body(a, b, a_got, b_got, *outs):
    for own, other, both in ((a, a_got, outs[0]), (b, b_got, outs[1])):
        size = own.shape[0]
        both[:size] = own[...]
        both[size:] = other[...]


def assemble_body(long, short, down_far, up_far, mark, down, up, sems):
    units = up.shape[1]
    part = units // len(long)
    blocks = up.shape[0] // units
    lo = lax.rem(lax.axis_index("dp"), len(long))
    firsts = [lax.bitwise_xor(lo, p) * part for p in range(len(long))]
    for first, rows in zip(firsts, long):
        down[pl.ds(pl.multiple_of(first, 8), part), :] = rows[:part].astype(F32)
    down_copy = pltpu.make_async_copy(down, down_far, sems.at[0])
    down_copy.start()
    for first, *pieces in zip(firsts, long, short):
        offset = 0
        for rows in (pieces[0][part:].astype(F32), pieces[1][...].astype(F32)):
            for k in range(blocks):
                at = pl.multiple_of(first * blocks + k * part + offset, 8)
                up[pl.ds(at, rows.shape[0]), :] = rows[:, k * units : (k + 1) * units]
            offset += rows.shape[0]
    up_copy = pltpu.make_async_copy(up, up_far, sems.at[1])
    up_copy.start()
    down_copy.wait()
    up_copy.wait()


def back_body(
    half,
    d_n2_0, d_n2_1, d_n2_2, cc, xc, attended, gate, heads, qkv, probs, w_out, gain2,
    d_resid_out, d_qkv, d_att_out, d_logit_out, g_gain2,
):
    blk, width = xc.shape
    scale = 1.0 / math.sqrt(HEAD_DIM)
    gated = gate[...]
    att = attended[...]
    resid = xc[...].astype(F32) + gated * att
    _, unit2, inverse2 = norm_rows(resid, row_of(gain2))
    d_n2 = d_n2_0[...].astype(F32) + d_n2_1[...].astype(F32)
    for at in range(0, d_n2_2.shape[0], blk):
        d_n2 = d_n2 + d_n2_2[at : at + blk].astype(F32)
    back2, g_gain2[...] = norm_back(d_n2, unit2, inverse2, row_of(gain2))
    d_resid = cc[...].astype(F32) + back2
    d_resid_out[...] = d_resid
    d_att = (d_resid * gated).astype(BF16)
    keep = (iota((blk, 1), 0) < half).astype(F32)
    d_gate = keep * jnp.sum(d_resid * att, axis=-1, keepdims=True)
    d_logit_out[...] = d_gate * gated * (1.0 - gated)
    d_att_out[...] = d_att
    d_heads = dot_nt(d_att, w_out[...]).astype(BF16)
    for pair in range(HEADS // 2):
        at = pair * PAIR
        q = qkv[:, at : at + PAIR]
        k = qkv[:, width + at : width + at + PAIR]
        v = qkv[:, 2 * width + at : 2 * width + at + PAIR]
        d_o = d_heads[:, at : at + PAIR]
        zero = jnp.zeros_like(q)
        d_q = d_k = d_v = 0.0
        for e in range(2):
            mask = half_mask((blk, PAIR), e)
            d_oe = jnp.where(mask, d_o, zero)
            prob = probs[2 * pair + e]
            prob_f = prob.astype(F32)
            d_prob = dot_nt(d_oe, v)
            d_score = (
                prob_f * (d_prob - jnp.sum(prob_f * d_prob, axis=-1, keepdims=True))
            ).astype(BF16)
            d_v = d_v + dot_tn(prob, d_oe)
            d_q = d_q + dot_nn(d_score, jnp.where(mask, k, zero))
            d_k = d_k + dot_tn(d_score, jnp.where(mask, q, zero))
        d_qkv[:, at : at + PAIR] = (d_q * scale).astype(BF16)
        d_qkv[:, width + at : width + at + PAIR] = (d_k * scale).astype(BF16)
        d_qkv[:, 2 * width + at : 2 * width + at + PAIR] = d_v.astype(BF16)


def products_body(tsize, heads, n1, d_qkv, d_att, table, *outs):
    width = n1.shape[1]
    me = lax.axis_index("dp") * tsize + lax.axis_index("tensor")
    share = width // (tsize * lax.axis_size("dp"))
    mid = outs[0].shape[0]
    for side in range(2):
        source = lax.bitwise_xor(table[side : side + 1, :], me) * share + table[2:3, :]
        order = (iota((width, width), 0) == source).astype(BF16)
        low = dot_nn(n1[...], order).astype(BF16)
        keep, send = outs[2 * side : 2 * side + 2]
        for k in range(2):
            at = k * width
            if side and k:
                product = dot_tn(dot_nn(heads[...], order).astype(BF16), d_att[...])
            else:
                column = (2 * side + k) * width
                product = dot_tn(low, d_qkv[:, column : column + width])
            product = product.astype(BF16)
            keep[:, at : at + width] = product[:mid]
            send[:, at : at + width] = product[mid:]


def to_pair(sums):
    top = sums.astype(BF16)
    return jnp.concatenate([top, (sums - top.astype(F32)).astype(BF16)], axis=0)


def fold_pair(sums):
    used = sums[:SUMS]
    top = used.astype(BF16).astype(F32)
    middle = sums.shape[1] // 2
    blocks = [a[:, k : k + middle] for a in (top, used - top) for k in (0, middle)]
    return jnp.concatenate(blocks, axis=0).astype(BF16)


def unfold_pair(folded):
    wide = folded.astype(F32)
    a, b, c, d = (wide[k * SUMS : (k + 1) * SUMS] for k in range(4))
    return jnp.concatenate([a + c, b + d], axis=1)


def from_pair(pair):
    size = pair.shape[0] // 2
    return pair[:size].astype(F32) + pair[size:].astype(F32)


def add_split_body(count, pieces, *refs):
    total = refs[0][...].astype(F32)
    for ref in refs[1:count]:
        total = total + ref[...].astype(F32)
    size = total.shape[0] // pieces
    for p in range(pieces):
        refs[count + p][...] = total[p * size : (p + 1) * size].astype(refs[count + p].dtype)


def put_back(pick, rows):
    top = rows.astype(BF16)
    rest = (rows - top.astype(F32)).astype(BF16)
    return dot_nn(pick, top) + dot_nn(pick, rest)


def post_body(
    cap, d_n0, hid_c0, hid_n0, d_nx, hid_c1, hid_n1, rest,
    xc, xn, cn, attended, gate, d_resid_c, d_qkv, d_logit, n1, w_qkv, gain1, gain2, router, g_gain2c, stats1,
    mixed, grad_in, sums,
):
    rows = mixed.shape[0]
    blk = xc.shape[0]
    _, dest_col = places(row_of(cap).astype(F32), rows, rows // 2, blk)
    pick_c = (iota((rows, blk), 1) == dest_col).astype(BF16)
    pick_n = (iota((rows, blk), 1) + blk == dest_col).astype(BF16)
    x_c, x_n = xc[...].astype(F32), xn[...].astype(F32)

    d_n1 = dot_nt(d_qkv[...], w_qkv[...]) + d_logit[...] * row_of(router)
    _, unit1, inverse1 = norm_rows(x_c, row_of(gain1))
    back1, g_gain1 = norm_back(d_n1, unit1, inverse1, row_of(gain1))
    grad_c = d_resid_c[...] + back1

    def summed(first, second, others, start, stop):
        total = first[...].astype(F32) + second[...].astype(F32)
        for o in range(start, stop, blk):
            total = total + others[o : o + blk].astype(F32)
        return total

    third = rest.shape[0] // 3
    d_n2n = summed(d_n0, d_nx, rest, 0, third)
    h_n = summed(hid_n0, hid_n1, rest, third, 2 * third)
    h_c = summed(hid_c0, hid_c1, rest, 2 * third, 3 * third)
    mix_c = (x_c + gate[...] * attended[...] + h_c).astype(BF16)
    mix_n = (x_n + h_n).astype(BF16)
    mixed[...] = (dot_nn(pick_c, mix_c) + dot_nn(pick_n, mix_n)).astype(BF16)
    _, unit, inverse = norm_rows(x_n, row_of(gain2))
    back, g_gain2n = norm_back(d_n2n, unit, inverse, row_of(gain2))
    d_resid_n = cn[...].astype(F32) + back
    grad_in[...] = put_back(pick_c, grad_c) + put_back(pick_n, d_resid_n)

    def over_rows(a):
        return jnp.sum(a, axis=0, keepdims=True)

    sums[...] = jnp.zeros_like(sums)
    sums[0:1, :] = g_gain1
    sums[1:2, :] = over_rows(d_logit[...] * n1[...].astype(F32))
    sums[2:3, :] = g_gain2c[...] + g_gain2n
    sums[3:4, :] = stats1[0:1, :] + over_rows(x_n * x_n)
    sums[4:5, :] = stats1[1:2, :]
    sums[5:6, :] = over_rows(h_c * h_c) + over_rows(h_n * h_n)


CORES = 2
GROUP = 4
SUMS = 6
PARTS = 1
W_MLP1 = 10.0
W_MLP2 = 0.0
W_LAST = 5.0
W_ATT4 = 20.0


def swap(name, array, axis, size, bits):
    with jax.named_scope(name):
        return lax.ppermute(array, axis, [(t, t ^ bits) for t in range(size)])


def add(name, arrays, after=(), weight=1.0):
    return call(
        lambda *refs: add_body(len(arrays), *refs),
        [(arrays[0].shape, BF16)],
        name,
        after=after,
        weight=weight,
    )(*arrays)[0]


def in_order(name, own, others, place, cut, after):
    if len(others) > 1:
        held = jnp.stack([own, *others])
        own, *others = [
            lax.dynamic_index_in_dim(held, place ^ at, 0, keepdims=False) for at in range(len(held))
        ]

    def body(*refs):
        total = refs[0][...].astype(F32)
        for ref in refs[1:-2]:
            total = total + ref[...].astype(F32)
        refs[-2][...] = total[:cut].astype(BF16)
        refs[-1][...] = total[cut:].astype(BF16)

    rows, columns = own.shape
    return call(
        body, [((cut, columns), BF16), ((rows - cut, columns), BF16)], name, after=after, weight=W_MLP2
    )(own, *others)


def shards(
    tokens, lengths, capacity, norm1_gain, router, w_qkv, w_out, norm2_gain, w_up, w_down, cotangent
):
    rows, width = tokens.shape
    half = rows // 2
    blk = -(-half // 16) * 16
    units = w_up.shape[1]
    tsize, dsize = lax.axis_size("tensor"), lax.axis_size("dp")
    ysize = tsize // CORES
    others = range(1, ysize)
    cap, gain1, gain2, route = capacity, norm1_gain, norm2_gain, router
    small = (blk, width)

    def far(name, array):
        return [swap("y_" + name, array, "tensor", tsize, dy * CORES) for dy in others]

    def across(name, array):
        return swap("core_" + name, array, "tensor", tsize, 1)

    cap_far, cot_far = far("cap", cap), far("cot", cotangent)
    xc, xn, n2n, cotn, cotc, cotn_core, cotc_core, bias = call(
        pre_body,
        [(small, BF16)] * 7 + [((blk, blk), F32)],
        "pre",
        scratch=[
            pltpu.VMEM(tokens.shape, BF16), pltpu.VMEM(cotangent.shape, BF16), pltpu.VMEM(cap.shape, jnp.int32),
            pltpu.SMEM(lengths.shape, jnp.int32), pltpu.VMEM(gain2.shape, F32), pltpu.SemaphoreType.DMA((5,)),
        ],
        loose=range(5),
        after=cap_far,
        weight=20.0,
    )(tokens, cotangent, cap, lengths, gain2, across("cot", cotangent), across("cap", cap))

    def group(name, pieces):
        return [swap("xz_" + name, pieces[p], "dp", dsize, p) for p in range(1, GROUP)]

    def high(name, pieces):
        return [
            swap("zz_" + name, pieces[p % len(pieces)], "dp", dsize, p * GROUP)
            for p in range(1, dsize // GROUP)
        ]

    n2n_far, n2n_core = far("n2n", n2n), across("n2n", n2n)

    n1, qkv, probs, heads, attended, gate, n2c, stats1 = call(
        lambda *refs: fore_body(half, *refs),
        [
            (small, BF16), ((blk, 3 * width), BF16), ((HEADS, blk, blk), BF16), (small, BF16),
            (small, F32), ((blk, 1), F32), (small, BF16), ((2, width), F32),
        ],
        "fore",
    )(xc, bias, gain1, route, w_qkv, w_out, gain2)

    n2c_far, n2c_core = far("n2c", n2c), across("n2c", n2c)

    def mlp(name, n2s, cots, outs, outs_at, after=(), weight=1.0):
        tall = blk * len(outs_at)
        count = len(n2s)
        return call(
            lambda *refs: mlp_body(
                blk, outs_at, refs[:count], refs[count : 2 * count], *refs[2 * count :]
            ),
            [((tall, units), BF16)] * 2 + [((n * blk, width), BF16) for n in outs],
            name,
            after=after,
            weight=weight,
        )(*n2s, *cots, w_up, w_down)

    n2_near = [n2c, n2n, n2c_core, n2n_core]
    cot_near = [cotc, cotn, cotc_core, cotn_core]
    at_near = [((c, k * blk), (c, (2 + k) * blk)) for c in range(CORES) for k in range(2)]
    act_a, dpre_a, near_0, near_1 = mlp("mlp_near", n2_near, cot_near, [4, 4], at_near)
    near_1 = across("near", near_1)

    def tie(name, arrays, after):
        return list(
            pl.pallas_call(
                lambda *refs: None,
                out_shape=tuple(jax.ShapeDtypeStruct(a.shape, a.dtype) for a in arrays),
                in_specs=[pl.BlockSpec(memory_space=pl.ANY)] * (len(arrays) + len(after)),
                out_specs=tuple(pl.BlockSpec(memory_space=pl.ANY) for _ in arrays),
                input_output_aliases={i: i for i in range(len(arrays))},
                compiler_params=pltpu.CompilerParams(vmem_limit_bytes=2**20),
                name=name,
            )(*arrays, *after)
        )

    count = len(cot_far)
    slim = (blk, width // 2)
    sorted_far = call(
        lambda *refs: sort_body(count, *refs),
        [(slim, BF16)] * (2 * count) + [(small, BF16)] * count,
        "sort_far",
        after=[act_a],
        weight=0.0,
    )(*cot_far, *cap_far)
    cotn_far = [Pair(sorted_far[i : 2 * count : count]) for i in range(count)]
    cotc_far = list(sorted_far[2 * count :])
    cotn_all = cotn_far + [Pair([across("far_cotn", a) for a in p]) for p in cotn_far]
    halves = call(
        lambda *refs: halve_body(count, *refs),
        [(slim, BF16)] * (2 * count),
        "halve_n2n",
        after=[a for p in cotn_all[count:] for a in p],
        weight=0.0,
    )(*n2n_far)
    n2n_far = [Pair(halves[i::count]) for i in range(count)]
    n2n_all = n2n_far + [Pair([across("far_n2n", a) for a in p]) for p in n2n_far]
    cotc_all = cotc_far + [across("far_cotc", a) for a in cotc_far]

    tall = 4 * blk
    down_near, up_near = call(
        lambda act, dpre, *refs: near_weights_body(act, dpre, refs[:4], refs[4:8], *refs[8:]),
        [((units, width), F32), ((width, units), F32)],
        "weights_near",
        scratch=[pltpu.VMEM((tall, width), BF16)] * 2,
        after=n2n_far[0][:1],
        weight=0.0,
    )(act_a, dpre_a, *n2_near, *cot_near)


    far_at = range(CORES * (ysize - 1))
    place = lambda s: (s // (ysize - 1), s % (ysize - 1) * blk)
    act_n, dpre_n, far_n0, far_n1 = mlp(
        "mlp_far_n", n2n_all, cotn_all, [2 * (ysize - 1)] * 2,
        [(place(s), (place(s)[0], place(s)[1] + (ysize - 1) * blk)) for s in far_at],
        [down_near], 0.0,
    )
    far_n1 = across("far_n", far_n1)
    n2c_far = tie("tie_c", n2c_far, [act_n, *cotc_all[count:]])
    n2c_all = n2c_far + [across("far_n2c", a) for a in n2c_far]
    def far_c(name, n2s, cots, after=()):
        outs_at = [((0, i * blk), (1, i * blk)) for i in range(len(n2s))]
        return mlp(name, n2s, cots, [len(n2s)] * 2, outs_at, after)

    count = ysize - 1
    act_c0, dpre_c0, d_c0, hid_c0 = far_c("mlp_far_c0", n2c_all[:count], cotc_all[:count])
    act_c1, dpre_c1, d_c1, hid_c1 = far_c("mlp_far_c1", n2c_all[count:], cotc_all[count:], [act_c0])
    d_c1, hid_c1 = across("d_c", d_c1), across("hid_c", hid_c1)

    def send_back(name, joint, groups):
        if ysize == 2:
            return swap("y_" + name, joint, "tensor", tsize, CORES)
        cut = joint.reshape(groups, ysize - 1, blk, width)
        got = [swap("y_" + name, cut[:, dy - 1], "tensor", tsize, dy * CORES) for dy in others]
        return jnp.stack(got, axis=1).reshape(joint.shape)

    cots, n2s = cotn_all + cotc_all, n2n_all + n2c_all
    count, tall = len(cots), len(cots) * blk
    part = units // GROUP

    def weights(*refs):
        acts, dpres, refs = refs[:3], refs[3:6], refs[6:]
        n2s, cots, refs = refs[:count], refs[count : 2 * count], refs[2 * count :]
        weights_body(
            GROUP, acts, dpres, n2s, cots, *refs[:2], refs[2:6], *refs[6:]
        )

    down_keep, down_got, up_keep, up_got = call(
        weights,
        [((2 * part, width), BF16)] * 4,
        "weights",
        scratch=[
            pltpu.VMEM((tall, units), BF16), pltpu.VMEM((tall, units), BF16),
            pltpu.VMEM((tall, width), BF16), pltpu.VMEM((tall, width), BF16),
            pltpu.VMEM((units, width), BF16), pltpu.VMEM((width, units), BF16),
        ],
        after=[],
    )(act_n, act_c0, act_c1, dpre_n, dpre_c0, dpre_c1, *n2s, *cots, down_near, up_near)
    mark = down_keep
    down_got = swap("xz_down", down_got, "dp", dsize, 1)
    up_got = swap("zx_up", up_got, "dp", dsize, 2)
    joint, rest = call(
        far_sum_body,
        [(((ysize - 1) * blk, width), BF16), ((3 * (ysize - 1) * blk, width), BF16)],
        "far_sum",
        after=[mark],
    )(d_c0, d_c1, far_n0, far_n1, hid_c0, hid_c1)
    d_c2 = send_back("d_c", joint, 1)
    rest = send_back("rest", rest, 3)

    mark = joint

    shares = tsize * dsize
    share = width // shares
    def owners(y_first):
        table = []
        for core in range(CORES):
            for first in range(ysize if y_first else 2):
                for then in range(2 if y_first else ysize):
                    y, x = (first, then) if y_first else (then, first)
                    for z in range(2):
                        for hi in range(dsize // GROUP):
                            place = (hi * GROUP + z * 2 + x) * tsize + y * CORES + core
                            table += [place] * share
        return table

    table = jnp.array([owners(True), owners(False), list(range(share)) * shares], jnp.int32)
    d_resid_c, d_qkv, d_att, d_logit, g_gain2c = call(
        lambda *refs: back_body(half, *refs),
        [
            (small, F32), ((blk, 3 * width), BF16), (small, BF16), ((blk, 1), F32), ((1, width), F32),
        ],
        "back",
        after=[mark],
        weight=20.0,
    )(
        (near_0, 0, blk), (near_1, 0, blk), d_c2, cotc, xc, attended, gate, heads, qkv, probs,
        w_out, gain2,
    )
    kept, down_got, up_got = call(
        halves_body,
        [((2 * part, width), F32), ((part, width), BF16), ((part, width), BF16)],
        "mlp_0",
        after=[d_resid_c],
        weight=0.0,
    )(down_keep, down_got, up_keep, up_got)
    mark = kept
    down_got = swap("xz_down", down_got, "dp", dsize, 2)
    up_got = swap("zx_up", up_got, "dp", dsize, 1)

    left, left_got, right, right_got = call(
        lambda *refs: products_body(tsize, *refs),
        [((width // 2, 2 * width), BF16)] * 4,
        "products",
        after=[mark],
    )(heads, n1, d_qkv, d_att, table)
    left_got, right_got = across("left", left_got), across("right", right_got)

    def sums_of(name, *sets, after=(), along=(), weight=1.0):
        given = [a for arrays, _ in sets for a in arrays]

        def body(*refs):
            ins, outs = list(refs[: len(given)]), list(refs[len(given) + len(along) :])
            if along:
                outs[-1][...] = refs[len(given)][...] + refs[len(given) + 1][...]
            for arrays, count in sets:
                add_split_body(len(arrays), count, *ins[: len(arrays)], *outs[:count])
                del ins[: len(arrays)], outs[:count]

        shapes = []
        for arrays, count in sets:
            rows, columns = arrays[0].shape
            shapes += [((rows // count, columns), BF16)] * count
        shapes += [(a.shape, a.dtype) for a in along[:1]]
        return call(body, shapes, name, after=after, weight=weight)(*given, *along)

    mine = call(
        own_body, [((2 * part, width), BF16)], "mlp_1", after=[left], weight=W_MLP1
    )(kept, down_got, up_got)
    mine_got = [high("mlp", mine)]

    *left, right, right_got = sums_of(
        "att_1", ([left, left_got], ysize), ([right, right_got], 2), after=[mine[0], rest]
    )
    left_got = [swap("y_left", left[p], "tensor", tsize, p * CORES) for p in others]
    right_got = swap("x_right", right_got, "dp", dsize, 1)

    mixed, grad_input, sums = call(
        post_body,
        [((rows, width), BF16), ((rows, width), F32), ((8, width), F32)],
        "post",
        after=[right],
        weight=20.0,
    )(
        cap, (near_0, 1, blk), (near_0, 2, blk), (near_0, 3, blk), (near_1, 1, blk), (near_1, 2, blk),
        (near_1, 3, blk), rest,
        xc, xn, cotn, attended, gate, d_resid_c, d_qkv, d_logit, n1, w_qkv, gain1, gain2, route, g_gain2c,
        stats1,
    )

    step = 1
    while step < tsize // 2:
        sums = sums + swap("sums", sums, "tensor", tsize, step)
        step *= 2
    sums_got = swap("sums", sums, "tensor", tsize, step)

    right = sums_of("right_2", ([right, right_got], ysize), after=[sums], weight=0.0)
    right_got = [swap("y_right", right[p], "tensor", tsize, p * CORES) for p in others]
    low_rows = 2 * sums.shape[0]

    def left_body(*refs):
        *ins, a, b, kept, sent, sums_out = refs
        total = ins[0][...].astype(F32)
        for ref in ins[1:]:
            total = total + ref[...].astype(F32)
        size = kept.shape[0]
        kept[...] = total[:size].astype(BF16)
        sent[:size] = total[size:].astype(BF16)
        sent[size:] = jnp.zeros_like(sent[size:])
        sums_out[...] = to_pair(a[...] + b[...])
        sent[size:, : sums_out.shape[1]] = sums_out[...]

    size = left[0].shape[0] // 2
    left, left_got, sums = call(
        left_body,
        [((size, 2 * width), BF16), ((size + low_rows, 2 * width), BF16), ((low_rows, width), BF16)],
        "left_2",
        after=[right[0]],
        weight=0.0,
    )(left[0], *left_got, sums, sums_got)
    left_got = swap("x_left", left_got, "dp", dsize, 1)

    cut = 2 * part * 17 // 24 // 16 * 16
    mine = in_order("mlp_2", mine[0], mine_got[0], lax.axis_index("dp") // GROUP, cut, [left])
    mine_got = [swap("zx_long", mine[0], "dp", dsize, 2), swap("xz_short", mine[1], "dp", dsize, 1)]

    highs = dsize // GROUP

    def join_body(*refs):
        (left, left_got, *rights), sums, outs = refs[: -2 * highs - 1], refs[-2 * highs - 1], refs[-2 * highs :]
        size = left.shape[0]
        middle = left.shape[1]
        pair = fold_pair(from_pair(sums[...]) + from_pair(left_got[size:, : sums.shape[1]]))
        totals = [left[...].astype(F32) + left_got[:size].astype(F32), rights[0][...].astype(F32)]
        for ref in rights[1:]:
            totals[1] = totals[1] + ref[...].astype(F32)
        for p, out in enumerate(outs):
            for k, total in enumerate(totals):
                out[:share, k * middle : (k + 1) * middle] = total[p * share : (p + 1) * share].astype(BF16)
            out[: pair.shape[0], 2 * middle :] = pair

    att = call(
        join_body,
        [((max(share, 4 * SUMS), 4 * width + width // 2), BF16)] * (2 * highs),
        "att_3",
        after=[mine[0]],
        weight=20.0,
    )(left, left_got, right[0], *right_got, sums)
    long_rest, short_rest = call(
        spread_body,
        [((2 * a.shape[0], width), BF16) for a in mine],
        "pairs",
        after=att[:1],
        weight=0.0,
    )(*mine, *mine_got)
    att = [att[0]] + tie("tie_att", att[1:], [long_rest])
    att_got = [
        swap("z_att", att[p], "dp", dsize, p // highs * 2 + p % highs * GROUP)
        for p in range(1, 2 * highs)
    ]
    long_rest = swap("zx_long", long_rest, "dp", dsize, 1)
    short_rest = swap("xz_short", short_rest, "dp", dsize, 2)

    g_down, g_up, mark = call(
        lambda a0, a2, a13, b0, b1, b23, *refs: assemble_body(
            (a0, a13.at[pl.ds(0, cut)], a2, a13.at[pl.ds(cut, cut)]),
            (b0, b1, b23.at[pl.ds(0, 2 * part - cut)], b23.at[pl.ds(2 * part - cut, 2 * part - cut)]),
            *refs,
        ),
        [((units, width), F32), ((width, units), F32), ((8, 128), F32)],
        "assemble",
        scratch=[
            pltpu.VMEM((units, width), F32), pltpu.VMEM((width, units), F32), pltpu.SemaphoreType.DMA((2,)),
        ],
        weight=W_LAST,
        loose_outs=True,
        after=att[1:2],
    )(mine[0], mine_got[0], long_rest, mine[1], mine_got[1], short_rest)

    count = rows * width * dsize * tsize

    def att_body(*refs):
        ins, outs = refs[: 2 * highs], refs[2 * highs :]
        out_qkv, out_proj, out_gain1, out_router, out_gain2, norms = outs
        total = ins[0][:share, : 4 * width].astype(F32)
        for ref in ins[1:]:
            total = total + ref[:share, : 4 * width].astype(F32)
        out_qkv[...] = total[:, : 3 * width]
        out_proj[...] = total[:, 3 * width :]
        sums = [unfold_pair(ref[: 4 * SUMS, 4 * width :]) for ref in ins]
        while len(sums) > 1:
            sums = [a + b for a, b in zip(sums[::2], sums[1::2])]
        for k, out in enumerate((out_gain1, out_router, out_gain2)):
            out[...] = sums[0][k : k + 1, :].reshape(width)
        norms[...] = jnp.sqrt(jnp.sum(sums[0][3:6, :], axis=-1) / count)

    g_qkv, g_proj, g_gain1, g_router, g_gain2, norms = call(
        att_body,
        [((share, 3 * width), F32), ((share, width), F32)] + [((width,), F32)] * 3 + [((3,), F32)],
        "att_4",
        weight=W_ATT4,
        after=[mark],
    )(att[0], *att_got)

    return (
        mixed, grad_input, g_gain1, g_router, g_qkv, g_proj, g_gain2, g_up, g_down, norms,
    )


def solution(mesh):
    return jax.shard_map(
        shards,
        mesh=mesh,
        in_specs=(
            P(("dp", "tensor"), None),
            P(("dp", "tensor"), None),
            P(("dp", "tensor")),
            P(),
            P(),
            P(),
            P(),
            P(),
            P(None, "tensor"),
            P("tensor", None),
            P(("dp", "tensor"), None),
        ),
        out_specs=(
            P(("dp", "tensor"), None),
            P(("dp", "tensor"), None),
            P(),
            P(),
            P(("dp", "tensor"), None),
            P(("dp", "tensor"), None),
            P(),
            P(None, "tensor"),
            P("tensor", None),
            P(),
        ),
        check_vma=False,
    )
```
